32 devices in a mesh: dp: 8 (over z, y), fsdp: 4 (over x, core).
Axes of the slice: x: 2, y: 2, z: 4, core: 2. Of those that a mesh axis runs over, the one named last changes fastest.
Arguments:
- latents: bfloat16 [24576, 768], P(('dp', 'fsdp')), may hold values from -6 to 6
- noise_draw: bfloat16 [24576, 768], P(('dp', 'fsdp')), may hold values from -6 to 6
- text_states: bfloat16 [96, 128, 768], P(('dp', 'fsdp')), may hold values from -6 to 6
- time_steps: int32 [96], P(('dp', 'fsdp')), may hold values from 0 to 999
- item_lengths: int32 [32, 3], P(('dp', 'fsdp')), may hold values from 1 to 512, 768 in all within a row
- text_lengths: int32 [96], P(('dp', 'fsdp')), may hold values from 1 to 128
- cotangent: bfloat16 [24576, 768], P(('dp', 'fsdp')), may hold values from -6 to 6
- time_in: bfloat16 [256, 768], P('fsdp', 'dp'), may hold values from -0.375 to 0.375
- time_out: bfloat16 [768, 768], P('fsdp', 'dp'), may hold values from -0.21875 to 0.21875
- modulation: bfloat16 [768, 6912], P('fsdp', 'dp'), may hold values from -0.21875 to 0.21875
- self_project: bfloat16 [768, 2304], P('fsdp', 'dp'), may hold values from -0.21875 to 0.21875
- self_output: bfloat16 [768, 768], P('fsdp', 'dp'), may hold values from -0.875 to 0.875
- cross_query: bfloat16 [768, 768], P('fsdp', 'dp'), may hold values from -0.21875 to 0.21875
- cross_memory: bfloat16 [768, 1536], P('fsdp', 'dp'), may hold values from -0.21875 to 0.21875
- cross_output: bfloat16 [768, 768], P('fsdp', 'dp'), may hold values from -0.625 to 0.625
- up_project: bfloat16 [768, 3072], P('fsdp', 'dp'), may hold values from -0.21875 to 0.21875
- down_project: bfloat16 [3072, 768], P('fsdp', 'dp'), may hold values from -0.109375 to 0.109375
Outputs:
- block_out: bfloat16 [24576, 768], P(('dp', 'fsdp'))
- latents_grad: float32 [24576, 768], P(('dp', 'fsdp'))
- time_in_grad: float32 [256, 768], P('fsdp', 'dp')
- time_out_grad: float32 [768, 768], P('fsdp', 'dp')
- modulation_grad: float32 [768, 6912], P('fsdp', 'dp')
- self_project_grad: float32 [768, 2304], P('fsdp', 'dp')
- self_output_grad: float32 [768, 768], P('fsdp', 'dp')
- cross_query_grad: float32 [768, 768], P('fsdp', 'dp')
- cross_memory_grad: float32 [768, 1536], P('fsdp', 'dp')
- cross_output_grad: float32 [768, 768], P('fsdp', 'dp')
- up_project_grad: float32 [768, 3072], P('fsdp', 'dp')
- down_project_grad: float32 [3072, 768], P('fsdp', 'dp')
The draws below stay inside these ranges and needn't reach their ends.
Inputs may be any that keep to these rules, and one draw needn't show every extreme that they name: `item_lengths`: each device's 3 lengths sum to 768; one of them is 512.
All inputs are finite; a program needn't handle non-finite values.
Results may differ from the reference program's by a relative error of at most 0.022.
Values may be sent and summed in bfloat16 or wider, within the bound.
A program may use at most 256 MiB of HBM per device.

```python
import math
import jax
import jax.numpy as jnp
import numpy as np
from jax import lax

D = 768
HEADS = 12
FF = 3072
FREQ = 256
TEXT = 128
IT_DEV = 3
TOK_DEV = 768
HD = 64
LONGEST = 512
SHARDS = 32
ITEMS = 96
TOKENS = 24576


def plant(values, rng, least, largest):
    place = [jax.random.randint(jax.random.fold_in(rng, axis), (), 0, length) for axis, length in enumerate(values.shape)]
    longest = values.shape.index(max(values.shape))
    beside = place[:longest] + [(place[longest] + 1) % values.shape[longest]] + place[longest + 1:]
    return values.at[tuple(place)].set(least).at[tuple(beside)].set(largest)


def shard_levels(own_key, dims, cuts, least, high):
    loudness, own = 1.0, jax.random.fold_in(own_key, 6)
    for axis_at, shards_of in cuts:
        draws = jnp.exp(jax.random.uniform(jax.random.fold_in(own, axis_at), (shards_of,), jnp.float32, least / len(cuts), high / len(cuts)))
        loudness = loudness * jnp.repeat(draws, dims[axis_at] // shards_of).reshape([-1 if axis == axis_at else 1 for axis in range(len(dims))])
    return loudness


def profile(count, total, limit, skew):
    portions = [(1 << 20) // math.isqrt(grade ** skew) + 1 for grade in range(2, count + 1)]
    spare, holding = total - limit - (count - 1), [1] * (count - 1)
    while spare > 0:
        movable = [i for i in range(count - 1) if holding[i] < limit]
        pool, left = sum([portions[i] for i in movable]), spare
        for i in movable:
            extra = min(limit - holding[i], max(1, left * portions[i] // pool), spare)
            holding[i] = holding[i] + extra
            spare = spare - extra
    return np.array([limit] + holding)


def uneven_parts(rng, amount, total, most, skew):
    if amount == 2:
        one = jax.random.randint(rng, (), max(1, total - most), min(most, total - 1) + 1)
        return jnp.stack([one, total - one])
    lengths = jnp.asarray(profile(amount, total, most, skew), jnp.int32)
    twos = (amount - 1) // 2
    giver, sink = lengths[1:1 + 2 * twos:2], lengths[2:2 + 2 * twos:2]
    slack = jnp.minimum(giver - 1, most - sink)
    shifted = jax.random.randint(jax.random.fold_in(rng, 1), (twos,), 0, 1 << 20) % (slack + 1)
    lengths = lengths.at[1:1 + 2 * twos:2].set(giver - shifted).at[2:2 + 2 * twos:2].set(sink + shifted)
    return lengths[jax.random.permutation(jax.random.fold_in(rng, 2), amount)]


def gaussian(rng, dims, scale, bound, cuts=(), kind=jnp.bfloat16):
    loudness = shard_levels(rng, dims, cuts, -0.22, 0.18) if cuts else 1.0
    values = jax.random.normal(rng, dims, jnp.float32) * scale * loudness
    return jnp.minimum(jnp.maximum(values, -bound), bound).astype(kind)


def setup_inputs(seed: int = 0) -> dict:
    streams_of = jax.random.split(jax.random.key(seed), 18)
    latents = gaussian(streams_of[0], (TOKENS, D), 1.0, 6.0, ((0, 32),))
    noise_draw = gaussian(streams_of[1], (TOKENS, D), 1.0, 6.0, ((0, 32),))
    text_states = gaussian(streams_of[2], (ITEMS, TEXT, D), 1.0, 6.0, ((0, 32),))
    time_steps = plant(jax.random.randint(streams_of[3], (ITEMS,), 0, 1000), jax.random.fold_in(streams_of[3], 1), 0, 999).astype(jnp.int32)
    item_lengths = jax.vmap(lambda own: uneven_parts(own, IT_DEV, TOK_DEV, LONGEST, 0))(jax.random.split(streams_of[4], SHARDS)).reshape((SHARDS, IT_DEV)).astype(jnp.int32)
    text_lengths = plant(jax.random.randint(streams_of[5], (ITEMS,), 1, TEXT + 1), jax.random.fold_in(streams_of[5], 1), 1, TEXT).astype(jnp.int32)
    cotangent = gaussian(streams_of[6], (TOKENS, D), 1.0, 6.0, ((0, 32),))
    time_in = gaussian(streams_of[7], (FREQ, D), FREQ ** -0.5, 0.375, ((0, 4), (1, 8)))
    time_out = gaussian(streams_of[8], (D, D), D ** -0.5, 0.21875, ((0, 4), (1, 8)))
    modulation = gaussian(streams_of[9], (D, 9 * D), D ** -0.5, 0.21875, ((0, 4), (1, 8)))
    self_project = gaussian(streams_of[10], (D, 3 * D), D ** -0.5, 0.21875, ((0, 4), (1, 8)))
    self_output = gaussian(streams_of[11], (D, D), (D // 16) ** -0.5, 0.875, ((0, 4), (1, 8)))
    cross_query = gaussian(streams_of[12], (D, D), D ** -0.5, 0.21875, ((0, 4), (1, 8)))
    cross_memory = gaussian(streams_of[13], (D, 2 * D), D ** -0.5, 0.21875, ((0, 4), (1, 8)))
    cross_output = gaussian(streams_of[14], (D, D), (D // 8) ** -0.5, 0.625, ((0, 4), (1, 8)))
    up_project = gaussian(streams_of[15], (D, FF), D ** -0.5, 0.21875, ((0, 4), (1, 8)))
    down_project = gaussian(streams_of[16], (FF, D), FF ** -0.5, 0.109375, ((0, 4), (1, 8)))
    return {"latents": latents, "noise_draw": noise_draw, "text_states": text_states, "time_steps": time_steps, "item_lengths": item_lengths, "text_lengths": text_lengths, "cotangent": cotangent, "time_in": time_in, "time_out": time_out, "modulation": modulation, "self_project": self_project, "self_output": self_output, "cross_query": cross_query, "cross_memory": cross_memory, "cross_output": cross_output, "up_project": up_project, "down_project": down_project}


HIGHEST = lax.Precision.HIGHEST

@jax.custom_vjp
def low(v):
    return lax.optimization_barrier(v.astype(jnp.bfloat16)).astype(jnp.float32)

@jax.custom_vjp
def low_back(v):
    return v

def low_keep(v):
    return (low(v), None)

def low_pass(kept, grad):
    return (grad,)

def back_keep(v):
    return (v, None)

def back_low(kept, grad):
    return (low(grad),)
low.defvjp(low_keep, low_pass)
low_back.defvjp(back_keep, back_low)

def high_dot(left, right):
    return jnp.dot(left, right, precision=HIGHEST, preferred_element_type=jnp.float32)

def modulate(stream, offset, stretch):
    center = stream - lax.optimization_barrier(jnp.mean(stream, axis=1, keepdims=True))
    spread = lax.optimization_barrier(jnp.mean(center * center, axis=1, keepdims=True))
    return center * lax.rsqrt(spread + 1e-06) * (1.0 + stretch) + offset

def layout(frame_count, lengths_row, text_row, text_width):
    item_ends = jnp.cumsum(lengths_row).astype(jnp.int32)
    places = jnp.arange(frame_count, dtype=jnp.int32)
    owners = lax.optimization_barrier(jnp.sum((places[:, None] >= item_ends[None, :]).astype(jnp.int32), axis=1))
    member = (owners[:, None] == jnp.arange(lengths_row.shape[0], dtype=jnp.int32)[None, :]).astype(jnp.float32)
    same_item = owners[:, None] == owners[None, :]
    slot_index = jnp.arange(lengths_row.shape[0] * text_width, dtype=jnp.int32)
    slot_item = slot_index // text_width
    slot_live = slot_index % text_width < jnp.repeat(text_row, text_width)
    text_mask = (slot_item[None, :] == owners[:, None]) & slot_live[None, :]
    return (member, same_item, text_mask)

def plan(step_row):
    levels = step_row.astype(jnp.float32)
    cumulative = jnp.cos(0.5 * math.pi * (levels / 1000.0 + 0.008) / 1.008) ** 2
    half_width = FREQ // 2
    frequency = jnp.exp(-math.log(10000.0) * jnp.arange(half_width, dtype=jnp.float32) / half_width)
    angles = levels[:, None] * frequency[None, :]
    embedding = jnp.concatenate([jnp.cos(angles), jnp.sin(angles)], axis=1)
    return (jnp.sqrt(cumulative), jnp.sqrt(1.0 - cumulative), embedding)

def split_heads(rows):
    return rows.reshape(rows.shape[0], HEADS, -1).transpose(1, 0, 2)

def join_heads(stacked):
    return stacked.transpose(1, 0, 2).reshape(stacked.shape[1], -1)

def attend(queries, key_rows, value_rows, allowed, factor):

    def single(parts):
        head_query, head_key, head_value = parts
        scores = low_back(jnp.where(allowed, high_dot(head_query, head_key.T) * factor, -1e+30))
        probs = jax.nn.softmax(scores, axis=1)
        return low(low_back(high_dot(low(probs), head_value)))
    joined = lax.map(jax.checkpoint(single), (split_heads(queries), split_heads(key_rows), split_heads(value_rows)))
    return join_heads(joined)

def group(weights, pieces):
    time_in, time_out, modulation, self_project, self_output, cross_query, cross_memory, cross_output, up_project, down_project = weights
    latent_rows, noise_rows, text_rows, step_row, lengths_row, text_row = pieces
    member, same_item, text_mask = layout(latent_rows.shape[0], lengths_row, text_row, TEXT)
    keep_part, noise_part, embedding = plan(step_row)
    stream = high_dot(member, keep_part[:, None]) * latent_rows + high_dot(member, noise_part[:, None]) * noise_rows
    hidden_time = jax.nn.silu(high_dot(embedding, time_in))
    condition = jax.nn.silu(high_dot(hidden_time, time_out))
    mod_rows = low_back(high_dot(low(condition), modulation))
    mod_terms = jnp.split(high_dot(member, mod_rows), 9, axis=1)
    factor = float(HD) ** (-0.5)
    normed_one = low(modulate(stream, mod_terms[0], mod_terms[1]))
    packed = low(low_back(high_dot(normed_one, self_project)))
    query_a, key_a, value_a = jnp.split(packed, 3, axis=1)
    attended = attend(query_a, key_a, value_a, same_item, factor)
    branch_one = low_back(high_dot(attended, self_output))
    stream_one = stream + mod_terms[2] * branch_one
    normed_two = low(modulate(stream_one, mod_terms[3], mod_terms[4]))
    query_b = low(low_back(high_dot(normed_two, cross_query)))
    memory = low(low_back(high_dot(text_rows.reshape(-1, D), cross_memory)))
    key_b, value_b = jnp.split(memory, 2, axis=1)
    crossed = attend(query_b, key_b, value_b, text_mask, factor)
    branch_two = low_back(high_dot(crossed, cross_output))
    stream_two = stream_one + mod_terms[5] * branch_two
    normed_three = low(modulate(stream_two, mod_terms[6], mod_terms[7]))
    inner_rows = low_back(high_dot(normed_three, up_project))
    active = low(jax.nn.gelu(inner_rows, approximate=True))
    branch_three = low_back(high_dot(active, down_project))
    return stream_two + mod_terms[8] * branch_three

def reference(latents, noise_draw, text_states, time_steps, item_lengths, text_lengths, cotangent, time_in, time_out, modulation, self_project, self_output, cross_query, cross_memory, cross_output, up_project, down_project):
    weights = (time_in.astype(jnp.float32), time_out.astype(jnp.float32), modulation.astype(jnp.float32), self_project.astype(jnp.float32), self_output.astype(jnp.float32), cross_query.astype(jnp.float32), cross_memory.astype(jnp.float32), cross_output.astype(jnp.float32), up_project.astype(jnp.float32), down_project.astype(jnp.float32))
    latent_set = latents.astype(jnp.float32).reshape(SHARDS, TOK_DEV, D)
    others = (noise_draw.astype(jnp.float32).reshape(SHARDS, TOK_DEV, D), text_states.astype(jnp.float32).reshape(SHARDS, IT_DEV, TEXT, D), time_steps.reshape(SHARDS, IT_DEV), item_lengths, text_lengths.reshape(SHARDS, IT_DEV))

    def forward(weight_set, latent_rows):

        def one_group(pieces):
            return group(weight_set, pieces)
        return lax.map(jax.checkpoint(one_group), (latent_rows,) + others)
    outputs, pullback = jax.vjp(forward, weights, latent_set)
    weight_grads, latent_grad = pullback(cotangent.astype(jnp.float32).reshape(SHARDS, TOK_DEV, D))
    return (outputs.reshape(TOKENS, D).astype(jnp.bfloat16), latent_grad.reshape(TOKENS, D), weight_grads[0], weight_grads[1], weight_grads[2], weight_grads[3], weight_grads[4], weight_grads[5], weight_grads[6], weight_grads[7], weight_grads[8], weight_grads[9])
```

```python
from functools import partial
import math

import jax
import jax.numpy as jnp
from jax import lax
from jax.experimental import pallas as pl
from jax.experimental.pallas import tpu as pltpu
from jax.sharding import PartitionSpec as P

F32, BF16 = jnp.float32, jnp.bfloat16
HEADS = 12
FREQ = 256
HD = 64
FACTOR = float(HD) ** -0.5
PAIR = 2 * HD
PAIRS = HEADS // 2
BIG = 1e30
TILE = 256
MIB = 2**20


def dot(left, right, lc, rc):
    return lax.dot_general(left, right, (((lc,), (rc,)), ((), ())), preferred_element_type=F32)


def nt(left, right):
    return dot(left, right, 1, 1)


def nn(left, right):
    return dot(left, right, 1, 0)


def tn(left, right):
    return dot(left, right, 0, 0)


def owners_column(lens, first, rows):
    place = lax.broadcasted_iota(jnp.int32, (rows, 1), 0) + first
    end = lens[0, 0]
    return (place >= end).astype(jnp.int32) + (place >= end + lens[0, 1]).astype(jnp.int32)


def owners_row(lens, cols):
    place = lax.broadcasted_iota(jnp.int32, (1, cols), 1)
    end = lens[0, 0]
    return (place >= end).astype(jnp.int32) + (place >= end + lens[0, 1]).astype(jnp.int32)


def pick(own, a, b, c):
    return jnp.where(own == 0, a, jnp.where(own == 1, b, c))


def expand(own, mod, block, width):
    lo = block * width
    return pick(own, mod[0:1, lo : lo + width], mod[1:2, lo : lo + width], mod[2:3, lo : lo + width])


def item_sums(lens, first, rows, values):
    items = lax.broadcasted_iota(jnp.int32, (16, rows), 0)
    place = lax.broadcasted_iota(jnp.int32, (16, rows), 1) + first
    end = lens[0, 0]
    own = (place >= end).astype(jnp.int32) + (place >= end + lens[0, 1]).astype(jnp.int32)
    member = jnp.where(items == own, 1.0, 0.0).astype(BF16)
    return nn(member, values.astype(BF16))


def fill_masks(lens, tlens, aq, aks, akc):
    rows = aq.shape[0]
    lane = lax.broadcasted_iota(jnp.int32, (rows, PAIR), 1) % HD
    own = owners_column(lens, 0, rows)
    aq[...] = jnp.where(own == lane, 1.0, 0.0).astype(BF16)
    minus = jnp.where((lane >= 3) & (lane < 6), -1.0, 0.0)
    aks[...] = jnp.where((lane < 3) & (own != lane), -BIG, minus).astype(BF16)
    slots = akc.shape[0]
    text = slots // 3
    lane = lax.broadcasted_iota(jnp.int32, (slots, PAIR), 1) % HD
    minus = jnp.where((lane >= 3) & (lane < 6), -1.0, 0.0)
    slot = lax.broadcasted_iota(jnp.int32, (slots, 1), 0)
    item = (slot >= text).astype(jnp.int32) + (slot >= 2 * text).astype(jnp.int32)
    live = slot - item * text < pick(item, tlens[0], tlens[1], tlens[2])
    akc[...] = jnp.where((lane < 3) & ((item != lane) | ~live), -BIG, minus).astype(BF16)


def pieces(column):
    one = column.astype(BF16).astype(F32)
    two = (column - one).astype(BF16).astype(F32)
    return one, two, column - one - two


def attention_forward(q, k, k_at, v_at, ak, aq, out, qaug):
    frames = q.shape[0]

    def pair(p, carry):
        lanes = pl.ds(pl.multiple_of(p * PAIR, PAIR), PAIR)
        kp = k[:, pl.ds(pl.multiple_of(k_at + p * PAIR, PAIR), PAIR)]
        vp = k[:, pl.ds(pl.multiple_of(v_at + p * PAIR, PAIR), PAIR)]
        klow = lax.broadcasted_iota(jnp.int32, kp.shape, 1) < HD
        keys = (jnp.where(klow, kp, ak[...]), jnp.where(klow, ak[...], kp))
        one = jnp.ones_like(vp)
        values = (jnp.where(klow, vp, one), jnp.where(klow, one, vp))
        lane = lax.broadcasted_iota(jnp.int32, (TILE, PAIR), 1)
        low, inner = lane < HD, lane % HD
        for t in range(frames // TILE):
            rows = pl.ds(t * TILE, TILE)
            qp = q[rows, lanes] * jnp.asarray(FACTOR, BF16)
            mark = aq[rows, :]
            done = []
            for h in range(2):
                own = low if h == 0 else ~low
                qh = jnp.where(own, qp, mark)
                s = nt(qh, keys[h])
                top = jnp.max(s, axis=1, keepdims=True)
                e = jnp.exp(s - top).astype(BF16)
                o = nn(e, values[h])
                total = o[:, HD : HD + 1] if h == 0 else o[:, 0:1]
                done.append(o * (1.0 / total))
                a, b, c = pieces(top + jnp.log(total))
                extra = jnp.where(inner == 3, a, jnp.where(inner == 4, b, c))
                extra = jnp.where((inner >= 3) & (inner < 6), extra, mark.astype(F32)).astype(BF16)
                at = pl.ds(pl.multiple_of((2 * p + h) * PAIR, PAIR), PAIR)
                qaug[rows, at] = jnp.where(own, qp, extra)
            out[rows, lanes] = jnp.where(low, done[0], done[1]).astype(BF16)
        return carry

    lax.fori_loop(0, PAIRS, pair, 0)


def attention_backward(qaug, k, k_at, v_at, ak, att, datt, dq, dk, dk_at, dv_at, acc):
    frames = att.shape[0]
    tall = k.shape[0]
    step = TILE if tall % TILE == 0 else PAIR

    def pair(p, carry):
        lanes = pl.ds(pl.multiple_of(p * PAIR, PAIR), PAIR)
        lane = lax.broadcasted_iota(jnp.int32, (frames, PAIR), 1)
        low, inner = lane < HD, lane % HD
        do = datt[:, lanes]
        both = do.astype(F32) * att[:, lanes].astype(F32)
        outs, queries = [], []
        for h in range(2):
            own = low if h == 0 else ~low
            a, b, c = pieces(jnp.sum(jnp.where(own, both, 0.0), axis=1, keepdims=True))
            extra = jnp.where(inner == 3, a, jnp.where(inner == 4, b, c))
            extra = jnp.where((inner >= 3) & (inner < 6), extra, 0.0).astype(BF16)
            outs.append(jnp.where(own, do, extra))
            queries.append(qaug[:, pl.ds(pl.multiple_of((2 * p + h) * PAIR, PAIR), PAIR)])
        for t in range(tall // step):
            rows = pl.ds(t * step, step)
            kp = k[rows, pl.ds(pl.multiple_of(k_at + p * PAIR, PAIR), PAIR)]
            vp = k[rows, pl.ds(pl.multiple_of(v_at + p * PAIR, PAIR), PAIR)]
            mark = ak[rows, :]
            klow = lax.broadcasted_iota(jnp.int32, kp.shape, 1) < HD
            kt = kp.T
            dks, dvs = [], []
            for h in range(2):
                own = klow if h == 0 else ~klow
                pt = jnp.exp(nt(jnp.where(own, kp, mark), queries[h]))
                dpt = nt(jnp.where(own, vp, mark), outs[h])
                dst = (pt * dpt).astype(BF16)
                dvs.append(nn(pt.astype(BF16), do))
                dks.append(nn(dst, queries[h]))
                part = nn(kt[h * HD : (h + 1) * HD, :], dst)
                at = pl.ds(h * HD, HD)
                if t == 0:
                    acc[at, :] = part
                else:
                    acc[at, :] += part
            dk[rows, pl.ds(pl.multiple_of(dk_at + p * PAIR, PAIR), PAIR)] = jnp.where(klow, dks[0], dks[1]).astype(BF16)
            dk[rows, pl.ds(pl.multiple_of(dv_at + p * PAIR, PAIR), PAIR)] = jnp.where(klow, dvs[0], dvs[1]).astype(BF16)
        dq[:, lanes] = (acc[...].T * FACTOR).astype(BF16)
        return carry

    lax.fori_loop(0, PAIRS, pair, 0)


def norm_tile(s):
    width = s.shape[1]
    center = s - jnp.sum(s, axis=1, keepdims=True) * (1.0 / width)
    spread = jnp.sum(center * center, axis=1, keepdims=True) * (1.0 / width)
    rs = lax.rsqrt(spread + 1e-06)
    return center * rs, rs


def tiles(count, fn):
    def step(i, carry):
        fn(pl.multiple_of(i * TILE, TILE))
        return carry

    lax.fori_loop(0, count // TILE, step, 0)


def big_nt(left, right, out, width):
    def step(n, carry):
        cols = pl.ds(pl.multiple_of(n * width, width), width)
        out[:, cols] = nt(left[...], right[cols, :]).astype(BF16)
        return carry

    lax.fori_loop(0, right.shape[0] // width, step, 0)


def big_tn(left, right, out, width):
    def step(n, carry):
        cols = pl.ds(pl.multiple_of(n * width, width), width)
        out[cols, :] = tn(left[:, cols], right[...]).astype(BF16)
        return carry

    lax.fori_loop(0, left.shape[1] // width, step, 0)


def norm_into(s, rows, own, lens, mod, sub, xh, m, rs, width):
    hat, r = norm_tile(s)
    xh[rows, :] = hat.astype(BF16)
    base = 3 * sub
    m[rows, :] = (hat * (1.0 + expand(own, mod, base + 1, width)) + expand(own, mod, base, width)).astype(BF16)
    lane = lax.broadcasted_iota(jnp.int32, (TILE, 128), 1)
    rs[rows, :] = jnp.where(lane == sub, r, rs[rows, :])


def forward_attention(lens, tlens, keep, loud, mod, lat, noi, text, wsp, wso, wcq, wcm, wco,
                      stream, xh1, m1, packed, qa1, att1, br1, xh2, m2, mem, qa2, att2, br2, rs,
                      aq, aks, akc, qb, tmp):
    frames, width = lat.shape
    fill_masks(lens, tlens, aq, aks, akc)
    rs[...] = jnp.zeros_like(rs)

    def start(at):
        rows = pl.ds(at, TILE)
        own = owners_column(lens, at, TILE)
        s = pick(own, keep[0], keep[1], keep[2]) * lat[rows, :].astype(F32)
        s = s + pick(own, loud[0], loud[1], loud[2]) * noi[rows, :].astype(F32)
        stream[rows, :] = s
        norm_into(s, rows, own, lens, mod, 0, xh1, m1, rs, width)

    tiles(frames, start)
    big_nt(m1, wsp, packed, width)
    attention_forward(packed, packed, width, 2 * width, aks, aq, att1, qa1)
    tmp[...] = nt(att1[...], wso[...])

    def middle(at):
        rows = pl.ds(at, TILE)
        own = owners_column(lens, at, TILE)
        br = tmp[rows, :]
        br1[rows, :] = br.astype(BF16)
        s = stream[rows, :] + expand(own, mod, 2, width) * br
        stream[rows, :] = s
        norm_into(s, rows, own, lens, mod, 1, xh2, m2, rs, width)

    tiles(frames, middle)
    big_nt(m2, wcq, qb, width)
    big_nt(text, wcm, mem, width)
    attention_forward(qb, mem, 0, width, akc, aq, att2, qa2)
    tmp[...] = nt(att2[...], wco[...])

    def last(at):
        rows = pl.ds(at, TILE)
        own = owners_column(lens, at, TILE)
        br = tmp[rows, :]
        br2[rows, :] = br.astype(BF16)
        stream[rows, :] = stream[rows, :] + expand(own, mod, 5, width) * br

    tiles(frames, last)


GELU_A, GELU_B = math.sqrt(2.0 / math.pi), 0.044715


def forward_ff(lens, mod, stream, wup, wdn, xh3, m3, act, slope, br3, out, rs, tmp):
    frames, width = stream.shape
    rs[...] = jnp.zeros_like(rs)

    def start(at):
        rows = pl.ds(at, TILE)
        own = owners_column(lens, at, TILE)
        norm_into(stream[rows, :], rows, own, lens, mod, 2, xh3, m3, rs, width)

    tiles(frames, start)

    def chunk(n, carry):
        cols = pl.ds(pl.multiple_of(n * width, width), width)
        tmp[...] = nt(m3[...], wup[cols, :])

        def gelu(at):
            rows = pl.ds(at, TILE)
            x = tmp[rows, :]
            sq = x * x
            t = jnp.tanh(x * (GELU_A + GELU_A * GELU_B * sq))
            half = 0.5 + 0.5 * t
            act[rows, cols] = (x * half).astype(BF16)
            slope[rows, cols] = (half + half * (1.0 - t) * x * (GELU_A + 3.0 * GELU_A * GELU_B * sq)).astype(BF16)

        tiles(frames, gelu)
        return carry

    lax.fori_loop(0, wup.shape[0] // width, chunk, 0)
    tmp[...] = nt(act[...], wdn[...])

    def last(at):
        rows = pl.ds(at, TILE)
        own = owners_column(lens, at, TILE)
        br = tmp[rows, :]
        br3[rows, :] = br.astype(BF16)
        out[rows, :] = (stream[rows, :] + expand(own, mod, 8, width) * br).astype(BF16)

    tiles(frames, last)


def norm_back(dm, hat, r, stretch):
    width = dm.shape[1]
    dh = dm * (1.0 + stretch)
    a = jnp.sum(dh, axis=1, keepdims=True) * (1.0 / width)
    b = jnp.sum(dh * hat, axis=1, keepdims=True) * (1.0 / width)
    return r * (dh - a - hat * b)


def add_sums(lens, at, sums, cols, values):
    sums[:, cols] += item_sums(lens, at, TILE, values)


def gate_tile(lens, at, own, mod, g, br, sub, sums, b, width):
    rows = pl.ds(at, TILE)
    add_sums(lens, at, sums, pl.ds((3 * sub + 2) * width, width), g * br[rows, :].astype(F32))
    b[rows, :] = (expand(own, mod, 3 * sub + 2, width) * g).astype(BF16)


def norm_back_tile(lens, at, own, mod, dm, xh, rs, sub, sums, width):
    rows = pl.ds(at, TILE)
    hat = xh[rows, :].astype(F32)
    add_sums(lens, at, sums, pl.ds(3 * sub * width, width), dm)
    add_sums(lens, at, sums, pl.ds((3 * sub + 1) * width, width), dm * hat)
    return norm_back(dm, hat, rs[rows, sub : sub + 1], expand(own, mod, 3 * sub + 1, width))


def backward_ff(lens, mod, cot, br3, act, slope, xh3, m3, rs, wup, wdn, g, b2, br2, dwd, dwu, sums, b3, ig, tmp):
    frames, width = cot.shape
    sums[...] = jnp.zeros_like(sums)

    def start(at):
        rows = pl.ds(at, TILE)
        own = owners_column(lens, at, TILE)
        gate_tile(lens, at, own, mod, cot[rows, :].astype(F32), br3, 2, sums, b3, width)

    tiles(frames, start)

    def chunk(n, carry):
        cols = pl.ds(pl.multiple_of(n * width, width), width)
        dwd[:, cols] = tn(b3[...], act[:, cols]).astype(BF16)
        ig[:, cols] = (nn(b3[...], wdn[:, cols]) * slope[:, cols].astype(F32)).astype(BF16)
        dwu[cols, :] = tn(ig[:, cols], m3[...]).astype(BF16)
        return carry

    lax.fori_loop(0, wup.shape[0] // width, chunk, 0)
    tmp[...] = nn(ig[...], wup[...])

    def last(at):
        rows = pl.ds(at, TILE)
        own = owners_column(lens, at, TILE)
        s = cot[rows, :].astype(F32) + norm_back_tile(lens, at, own, mod, tmp[rows, :], xh3, rs, 2, sums, width)
        g[rows, :] = s
        gate_tile(lens, at, own, mod, s, br2, 1, sums, b2, width)

    tiles(frames, last)


def backward_attention(lens, tlens, keep, mod, text, g, b2, xh1, m1, packed, qa1, att1, br1, xh2, m2, mem, qa2, att2, rs,
                       wsp, wso, wcq, wcm, wco, sums_in,
                       lat_grad, dsp, dso, dcq, dcm, dco, sums,
                       aq, aks, akc, datt, dq, dmem, dpack, acc, tmp, stage):
    frames, width = g.shape
    fill_masks(lens, tlens, aq, aks, akc)
    sums[...] = sums_in[...]
    big_tn(b2, att2, dco, width)
    datt[...] = nn(b2[...], wco[...]).astype(BF16)
    attention_backward(qa2, mem, 0, width, akc, att2, datt, dq, dmem, 0, width, acc)
    big_tn(dq, m2, dcq, width)
    big_tn(dmem, text, dcm, width)
    tmp[...] = nn(dq[...], wcq[...])

    def middle(at):
        rows = pl.ds(at, TILE)
        own = owners_column(lens, at, TILE)
        s = g[rows, :] + norm_back_tile(lens, at, own, mod, tmp[rows, :], xh2, rs, 1, sums, width)
        stage[rows, :] = s
        gate_tile(lens, at, own, mod, s, br1, 0, sums, dq, width)

    tiles(frames, middle)
    big_tn(dq, att1, dso, width)
    datt[...] = nn(dq[...], wso[...]).astype(BF16)
    attention_backward(qa1, packed, width, 2 * width, aks, att1, datt, dpack, dpack, width, 2 * width, acc)
    big_tn(dpack, m1, dsp, width)
    tmp[...] = nn(dpack[...], wsp[...])

    def last(at):
        rows = pl.ds(at, TILE)
        own = owners_column(lens, at, TILE)
        s = stage[rows, :] + norm_back_tile(lens, at, own, mod, tmp[rows, :], xh1, rs, 0, sums, width)
        lat_grad[rows, :] = pick(own, keep[0], keep[1], keep[2]) * s

    tiles(frames, last)


def sds(shape, kind=BF16):
    return jax.ShapeDtypeStruct(shape, kind)


VM = pl.BlockSpec(memory_space=pltpu.VMEM)
SM = pl.BlockSpec(memory_space=pltpu.SMEM)


def call(body, scalars, ins, outs, scratch, flops):
    cost = pl.CostEstimate(flops=int(flops), bytes_accessed=int(3e7), transcendentals=0)
    return pl.pallas_call(
        body,
        out_shape=outs,
        in_specs=[SM] * len(scalars) + [VM] * len(ins),
        out_specs=[VM] * len(outs),
        scratch_shapes=scratch,
        cost_estimate=cost,
        compiler_params=pltpu.CompilerParams(vmem_limit_bytes=62 * MIB),
    )(*scalars, *ins)


def run_forward(lens, tlens, keep, loud, mod, lat, noi, text, wsp, wso, wcq, wcm, wco, wup, wdn):
    t, d = lat.shape
    x = text.shape[0]
    wide = HEADS * PAIR
    a = call(forward_attention, (lens, tlens, keep, loud), (mod, lat, noi, text, wsp, wso, wcq, wcm, wco),
             [sds((t, d), F32), sds((t, d)), sds((t, d)), sds((t, 3 * d)), sds((t, wide)), sds((t, d)), sds((t, d)),
              sds((t, d)), sds((t, d)), sds((x, 2 * d)), sds((t, wide)), sds((t, d)), sds((t, d)), sds((t, 128), F32)],
             [pltpu.VMEM((t, PAIR), BF16), pltpu.VMEM((t, PAIR), BF16), pltpu.VMEM((x, PAIR), BF16),
              pltpu.VMEM((t, d), BF16), pltpu.VMEM((t, d), F32)], 3e10)
    ff = wup.shape[0]
    b = call(forward_ff, (lens,), (mod, a[0], wup, wdn),
             [sds((t, d)), sds((t, d)), sds((t, ff)), sds((t, ff)), sds((t, d)), sds((t, d)), sds((t, 128), F32)],
             [pltpu.VMEM((t, d), F32)], 1e10)
    return a, b


def run_backward(lens, tlens, keep, mod, text, cot, a, b, wsp, wso, wcq, wcm, wco, wup, wdn):
    t, d = cot.shape
    x = text.shape[0]
    stream, xh1, m1, packed, qa1, att1, br1, xh2, m2, mem, qa2, att2, br2, rs = a
    xh3, m3, act, slope, br3, out, rs3 = b
    ff = wup.shape[0]
    g, b2, dwd, dwu, sums = call(
        partial(lambda lens, mod, cot, br3, act, slope, xh3, m3, rs, wup, wdn, br2, g, b2, dwd, dwu, sums, b3, ig, tmp:
                backward_ff(lens, mod, cot, br3, act, slope, xh3, m3, rs, wup, wdn, g, b2, br2, dwd, dwu, sums, b3, ig, tmp)),
        (lens,), (mod, cot, br3, act, slope, xh3, m3, rs3, wup, wdn, br2),
        [sds((t, d), F32), sds((t, d)), sds((d, ff)), sds((ff, d)), sds((16, 9 * d), F32)],
        [pltpu.VMEM((t, d), BF16), pltpu.VMEM((t, ff), BF16), pltpu.VMEM((t, d), F32)], 3e10)
    lat_grad, dsp, dso, dcq, dcm, dco, sums = call(
        backward_attention, (lens, tlens, keep),
        (mod, text, g, b2, xh1, m1, packed, qa1, att1, br1, xh2, m2, mem, qa2, att2, rs, wsp, wso, wcq, wcm, wco, sums),
        [sds((t, d), F32), sds((3 * d, d)), sds((d, d)), sds((d, d)), sds((2 * d, d)), sds((d, d)), sds((16, 9 * d), F32)],
        [pltpu.VMEM((t, PAIR), BF16), pltpu.VMEM((t, PAIR), BF16), pltpu.VMEM((x, PAIR), BF16),
         pltpu.VMEM((t, d), BF16), pltpu.VMEM((t, d), BF16), pltpu.VMEM((x, 2 * d), BF16), pltpu.VMEM((t, 3 * d), BF16),
         pltpu.VMEM((PAIR, t), F32), pltpu.VMEM((t, d), F32), pltpu.VMEM((t, d), F32)], 6e10)
    return out, lat_grad, dsp, dso, dcq, dcm, dco, dwu, dwd, sums

MESH = pl.DeviceIdType.MESH
ANY = pl.BlockSpec(memory_space=pl.ANY)
UNITS = (
    (0, 0, 1, 0, 2, 0), (1, 0, 1, 0, 2, 1),
    (2, 0, 2 / 3, 0, 2, 0), (2, 2 / 3, 1 / 3, 0, 2, 1),
    (3, 0, 1, 0, 2, 1), (4, 0, 1, 0, 2, 0),
    (5, 0, 1 / 2, 0, 2, 0), (5, 1 / 2, 1 / 2, 0, 2, 1),
    (6, 0, 1, 0, 2, 1),
    (7, 0, 1 / 2, 0, 2, 0), (7, 1 / 2, 1 / 2, 0, 2, 1),
    (8, 0, 1, 0, 1, 0), (8, 0, 1, 1, 1, 1),
)


class Place:
    def __init__(self, depth):
        dp, fsdp = lax.axis_index("dp"), lax.axis_index("fsdp")
        self.depth = depth
        self.z, self.y = dp // 2, dp % 2
        self.x, self.c = fsdp // 2, fsdp % 2

    def at(self, z=None, y=None, x=None, c=None):
        z = self.z if z is None else z
        y = self.y if y is None else y
        x = self.x if x is None else x
        c = self.c if c is None else c
        return (z * 2 + y, x * 2 + c)

    def other_z(self, k):
        return lax.rem(self.z + k, self.depth)

    def barrier(self):
        bar = pltpu.get_barrier_semaphore()
        ids = [self.at(z=self.other_z(k)) for k in range(1, self.depth)]
        ids += [self.at(y=1 - self.y), self.at(x=1 - self.x), self.at(c=1 - self.c)]
        for d in ids:
            pl.semaphore_signal(bar, inc=1, device_id=d, device_id_type=MESH)
        pl.semaphore_wait(bar, len(ids))


class Counter:
    def __init__(self, send, recv):
        self.send, self.recv, self.n = send, recv, 0

    def remote(self, src, dst, device):
        n, self.n = self.n, self.n + 1
        return pltpu.make_async_remote_copy(src_ref=src, dst_ref=dst, send_sem=self.send.at[n], recv_sem=self.recv.at[n],
                                            device_id=device, device_id_type=MESH)

    def local(self, src, dst):
        n, self.n = self.n, self.n + 1
        return pltpu.make_async_copy(src, dst, self.send.at[n])


def unit_shape(unit, shapes):
    w, r0, nr, l0, nl, route = unit
    c8, share = shapes[w]
    half = c8 // 2
    return w, int(round(half * r0)), int(round(half * nr)), l0 * share, nl * share, route, half


class GatherUnit:
    def __init__(self, unit, shapes, place, count, block, out):
        w, r0, n, l0, nl, route, half = unit_shape(unit, shapes)
        self.p, p = place, place
        self.route = route
        share = shapes[w][1]
        row = pl.ds(pl.multiple_of(p.c * half + r0, 16), n)
        other = pl.ds(pl.multiple_of((1 - p.c) * half + r0, 16), n)
        lane = lambda x: pl.ds(pl.multiple_of(x * (2 * share) + l0, 128), nl)
        own = block[w].at[pl.ds(r0, n), pl.ds(l0, nl)]
        o = out[w]
        mine, theirs = lane(p.x), lane(1 - p.x)
        D = p.depth
        dst = o.at[p.z, p.y, row, mine]
        self.local = count.local(own, dst)
        self.zs = [count.remote(own, dst, p.at(z=p.other_z(k))) for k in range(1, D)]
        self.second, self.third = [], []
        for k in range(D):
            zz = p.z if k == 0 else p.other_z(D - k)
            if route == 0:
                a = o.at[zz, p.y, row, mine]
                self.second.append(count.remote(own if k == 0 else a, a, p.at(y=1 - p.y)))
            else:
                a = o.at[zz, p.y, row, mine]
                self.second.append(count.remote(own if k == 0 else a, a, p.at(x=1 - p.x)))
        for k in range(D):
            zz = p.z if k == 0 else p.other_z(D - k)
            if route == 0:
                a = o.at[zz, :, row, mine]
                self.third.append(count.remote(a, a, p.at(x=1 - p.x)))
            else:
                lanes = pl.ds(l0, nl)
                a = [o.at[zz, p.y, row, lane(i)] for i in range(2)]
                self.third.append([count.remote(v, v, p.at(y=1 - p.y)) for v in a])
        sib = [o.at[:, :, row, lane(i)] for i in range(2)]
        self.sib = [count.remote(v, v, p.at(c=1 - p.c)) for v in sib]

    def flat(self, v):
        return v if isinstance(v, list) else [v]

    def begin(self):
        self.local.start()
        for cp in self.zs:
            cp.start()
        self.second[0].start()

    def step_z(self):
        for k, cp in enumerate(self.zs, 1):
            cp.wait_recv()
            self.second[k].start()
        self.local.wait()

    def step_second(self):
        for k, cp in enumerate(self.second):
            cp.wait_recv()
            for c in self.flat(self.third[k]):
                c.start()

    def step_third(self):
        for v in self.third:
            for c in self.flat(v):
                c.wait_recv()
        for c in self.sib:
            c.start()

    def finish(self):
        for c in self.sib:
            c.wait()
        for c in self.zs + self.second + [c for v in self.third for c in self.flat(v)]:
            c.wait_send()


def gather_body(depth, shapes, *refs):
    nw = len(shapes)
    ins, outs = refs[:nw], refs[nw : 2 * nw]
    rest = refs[2 * nw :]
    turned, landed, block = rest[:nw], rest[nw : 2 * nw], rest[2 * nw : 3 * nw]
    send, recv = rest[3 * nw :]
    p = Place(depth)
    count = Counter(send, recv)
    swaps = []
    for w, (c8, share) in enumerate(shapes):
        turned[w][...] = ins[w][...].T
    p.barrier()
    for w, (c8, share) in enumerate(shapes):
        half = c8 // 2
        theirs = turned[w].at[pl.ds(pl.multiple_of((1 - p.c) * half, 16), half), :]
        swaps.append(count.remote(theirs, landed[w], p.at(c=1 - p.c)))
        swaps[-1].start()
    for w, (c8, share) in enumerate(shapes):
        half = c8 // 2
        swaps[w].wait_recv()
        own = turned[w][pl.ds(pl.multiple_of(p.c * half, 16), half), :]
        got = landed[w][...]
        first = p.c == 0
        block[w][...] = jnp.concatenate([jnp.where(first, own, got), jnp.where(first, got, own)], axis=1)
    units = [GatherUnit(u, shapes, p, count, block, outs) for u in UNITS]
    n = len(units)
    ahead = 2
    begun = 0
    for t in range(n + 2):
        while begun < min(n, t + ahead):
            units[begun].begin()
            begun += 1
        if t < n:
            units[t].step_z()
        if 0 <= t - 1 < n:
            units[t - 1].step_second()
        if 0 <= t - 2 < n:
            units[t - 2].step_third()
    for u in units:
        u.finish()
    for s in swaps:
        s.wait_send()


def copies_of_gather(depth, nw):
    return nw + sum(1 + (depth - 1) + depth + depth * (1 if u[5] == 0 else 2) + 2 for u in UNITS)


def gather(mesh, weights):
    depth = mesh.shape["dp"] // 2
    nx = mesh.shape["fsdp"] // 2
    shapes = [(w.shape[1], w.shape[0]) for w in weights]
    ns = copies_of_gather(depth, len(weights))
    outs = [sds((depth, 2, c8, share * 2 * nx)) for c8, share in shapes]
    full = pl.pallas_call(
        partial(gather_body, depth, shapes),
        out_shape=outs,
        in_specs=[VM] * len(weights),
        out_specs=[ANY] * len(weights),
        scratch_shapes=[pltpu.VMEM((c8, share), BF16) for c8, share in shapes]
        + [pltpu.VMEM((c8 // 2, share), BF16) for c8, share in shapes]
        + [pltpu.VMEM((c8 // 2, 2 * share), BF16) for c8, share in shapes]
        + [pltpu.SemaphoreType.DMA((ns,)), pltpu.SemaphoreType.DMA((ns,))],
        compiler_params=pltpu.CompilerParams(collective_id=0, has_side_effects=True, vmem_limit_bytes=40 * MIB),
    )(*weights)
    return [f.reshape(-1, f.shape[-1]) for f in full]


SUM_UNITS = (
    (6, 0, 1, 0, 1, 0), (6, 0, 1, 1, 1, 1), (5, 0, 1 / 2, 0, 2, 0), (5, 1 / 2, 1 / 2, 0, 2, 1),
    (4, 0, 1, 0, 2, 0), (2, 0, 1, 0, 2, 1), (3, 0, 1 / 2, 0, 2, 0), (3, 1 / 2, 1 / 2, 0, 2, 1),
    (1, 0, 1, 0, 2, 1), (0, 0, 2 / 3, 0, 2, 0), (0, 2 / 3, 1 / 3, 0, 2, 1),
)


def each(count, fn):
    def step(i, carry):
        fn(i)
        return carry

    lax.fori_loop(0, count, step, 0)


def plus(a, b):
    return (a.astype(F32) + b.astype(F32)).astype(BF16)


class SumUnit:
    def __init__(self, unit, shapes, place, count, grads, held, cores, first, second, lasts, final):
        w, r0, n, l0, nl, route, half = unit_shape(unit, shapes)
        self.p, self.route, self.D = place, route, place.depth
        p, D = place, place.depth
        share = shapes[w][1]
        row = pl.ds(pl.multiple_of(p.c * half + r0, 16), n)
        other = pl.ds(pl.multiple_of((1 - p.c) * half + r0, 16), n)
        self.held, self.cores, self.first, self.second, self.lasts = held, cores, first, second, lasts
        self.final, self.at = final[w], (pl.ds(r0, n), pl.ds(l0, nl))
        self.loads, self.swaps = [], []
        for i in range(2):
            lane = pl.ds(i * 2 * share + l0, nl)
            self.loads.append(count.local(grads[w].at[:, :, row, lane], held.at[i]))
            self.swaps.append(count.remote(grads[w].at[:, :, other, lane], cores.at[i], p.at(c=1 - p.c)))
        x, y, z = p.x, p.y, p.z
        if route == 0:
            self.one = count.remote(held.at[1 - x], first, p.at(x=1 - x))
            self.two = count.remote(held.at[x, :, 1 - y], second, p.at(y=1 - y))
        else:
            self.one = count.remote(held.at[:, :, 1 - y], first, p.at(y=1 - y))
            self.two = count.remote(held.at[1 - x, :, y], second, p.at(x=1 - x))
        self.three = []
        for k in range(1, D):
            zz = p.other_z(k)
            self.three.append(count.remote(held.at[x, zz, y], lasts.at[k - 1], p.at(z=zz)))

    def begin(self):
        for c in self.loads + self.swaps:
            c.start()

    def step_core(self):
        for c in self.loads:
            c.wait()
        for c in self.swaps:
            c.wait_recv()
        x, y, D = self.p.x, self.p.y, self.D
        held, cores = self.held, self.cores
        if self.route == 0:
            def add(xx):
                def fn(i):
                    held[xx, i // 2, i % 2] = plus(held[xx, i // 2, i % 2], cores[xx, i // 2, i % 2])
                each(2 * D, fn)
            add(1 - x)
            self.one.start()
            add(x)
        else:
            def add(yy):
                def fn(i):
                    held[i // D, i % D, yy] = plus(held[i // D, i % D, yy], cores[i // D, i % D, yy])
                each(2 * D, fn)
            add(1 - y)
            self.one.start()
            add(y)

    def step_one(self):
        self.one.wait_recv()
        x, y, D = self.p.x, self.p.y, self.D
        held, got = self.held, self.first
        if self.route == 0:
            def add(yy):
                def fn(i):
                    held[x, i, yy] = plus(held[x, i, yy], got[i, yy])
                each(D, fn)
            add(1 - y)
            self.two.start()
            add(y)
        else:
            def add(xx):
                def fn(i):
                    held[xx, i, y] = plus(held[xx, i, y], got[xx, i])
                each(D, fn)
            add(1 - x)
            self.two.start()
            add(x)

    def step_two(self):
        self.two.wait_recv()
        x, y = self.p.x, self.p.y
        held, got = self.held, self.second
        for k in range(1, self.D):
            zz = self.p.other_z(k)
            held[x, zz, y] = plus(held[x, zz, y], got[zz])
            self.three[k - 1].start()

    def step_three(self):
        for c in self.three:
            c.wait_recv()
        x, y, z = self.p.x, self.p.y, self.p.z
        total = self.held[x, z, y].astype(F32) + self.second[z].astype(F32)
        for k in range(self.D - 1):
            total += self.lasts[k].astype(F32)
        self.final[self.at] = total

    def finish(self):
        for c in self.swaps + [self.one, self.two] + self.three:
            c.wait_send()


def sum_scratch(shapes, depth, units):
    scratch = []
    for u in units:
        w, r0, n, l0, nl, route, half = unit_shape(u, shapes)
        scratch.append(pltpu.VMEM((2, depth, 2, n, nl), BF16))
        scratch.append(pltpu.VMEM((2, depth, 2, n, nl), BF16))
        scratch.append(pltpu.VMEM((depth, 2, n, nl) if route == 0 else (2, depth, n, nl), BF16))
        scratch.append(pltpu.VMEM((depth, n, nl), BF16))
        scratch.append(pltpu.VMEM((depth - 1, n, nl), BF16))
    return scratch


class LastSwap:
    def __init__(self, w, shapes, place, count, final, part, out):
        self.c8, self.share = shapes[w]
        self.p, self.final, self.part, self.out = place, final[w], part[w], out[w]
        half = self.c8 // 2
        self.rows = pl.ds(pl.multiple_of(place.c * half, 16), half)
        self.copy = count.remote(self.part, self.out.at[self.rows, :], place.at(c=1 - place.c))

    def begin(self):
        total = self.final[...]
        low, high = total[:, : self.share], total[:, self.share :]
        first = self.p.c == 0
        self.part[...] = jnp.where(first, high, low)
        self.copy.start()
        self.out[self.rows, :] = jnp.where(first, low, high)

    def finish(self):
        self.copy.wait()


def reduce_body(depth, shapes, *refs):
    nw = len(shapes)
    grads, outs, rest = refs[:nw], refs[nw : 2 * nw], refs[2 * nw :]
    final, part, rest = rest[:nw], rest[nw : 2 * nw], rest[2 * nw :]
    send, recv = rest[-2:]
    p = Place(depth)
    count = Counter(send, recv)
    p.barrier()
    units = [SumUnit(u, shapes, p, count, grads, *rest[5 * i : 5 * i + 5], final) for i, u in enumerate(SUM_UNITS)]
    swaps = [LastSwap(w, shapes, p, count, final, part, outs) for w in range(nw)]
    n = len(units)
    last = {u[0]: i for i, u in enumerate(SUM_UNITS)}
    for u in units:
        u.begin()
    for t in range(n + 3):
        if t < n:
            units[t].step_core()
        if 0 <= t - 1 < n:
            units[t - 1].step_one()
        if 0 <= t - 2 < n:
            units[t - 2].step_two()
        if 0 <= t - 3 < n:
            units[t - 3].step_three()
            for w, i in last.items():
                if i == t - 3:
                    swaps[w].begin()
    for u in units:
        u.finish()
    for s in swaps:
        s.finish()


def turn_body(nw, *refs):
    for w in range(nw):
        refs[nw + w][...] = refs[w][...].T


def reduce(mesh, grads):
    depth, ncore = mesh.shape["dp"] // 2, mesh.shape["fsdp"]
    shapes = [(g.shape[0] // (2 * depth), g.shape[1] // ncore) for g in grads]
    ns = sum(4 + 2 + depth - 1 for _ in SUM_UNITS) + len(shapes)
    shares = pl.pallas_call(
        partial(reduce_body, depth, shapes),
        out_shape=[sds(s, F32) for s in shapes],
        in_specs=[ANY] * len(grads),
        out_specs=[VM] * len(grads),
        scratch_shapes=[pltpu.VMEM((c8 // 2, 2 * share), F32) for c8, share in shapes]
        + [pltpu.VMEM((c8 // 2, share), F32) for c8, share in shapes]
        + sum_scratch(shapes, depth, SUM_UNITS)
        + [pltpu.SemaphoreType.DMA((ns,)), pltpu.SemaphoreType.DMA((ns,))],
        compiler_params=pltpu.CompilerParams(collective_id=1, has_side_effects=True, vmem_limit_bytes=50 * MIB),
    )(*[g.reshape(depth, 2, c8, g.shape[1]) for g, (c8, _) in zip(grads, shapes)])
    return pl.pallas_call(
        partial(turn_body, len(shapes)),
        out_shape=[sds(s[::-1], F32) for s in shapes],
        in_specs=[VM] * len(grads),
        out_specs=[VM] * len(grads),
    )(*shares)


HIGHEST = lax.Precision.HIGHEST
BOTH = ("dp", "fsdp")


def high_dot(left, right, lc=1, rc=0):
    return lax.dot_general(left, right, (((lc,), (rc,)), ((), ())), precision=HIGHEST, preferred_element_type=F32)


def plan(step_row):
    levels = step_row.astype(F32)
    cumulative = jnp.cos(0.5 * math.pi * (levels / 1000.0 + 0.008) / 1.008) ** 2
    half_width = FREQ // 2
    frequency = jnp.exp(-math.log(10000.0) * jnp.arange(half_width, dtype=F32) / half_width)
    angles = levels[:, None] * frequency[None, :]
    embedding = jnp.concatenate([jnp.cos(angles), jnp.sin(angles)], axis=1)
    return jnp.sqrt(cumulative), jnp.sqrt(1.0 - cumulative), embedding


def silu_slope(v):
    s = jax.nn.sigmoid(v)
    return s * (1.0 + v * (1.0 - s))


def plain_gather(w):
    part = lax.all_gather(w, "fsdp", axis=0, tiled=True)
    return lax.all_gather(part, "dp", axis=1, tiled=True).T


def plain_reduce(g):
    part = lax.psum_scatter(g.T, "dp", scatter_dimension=1, tiled=True).astype(BF16)
    return lax.psum_scatter(part, "fsdp", scatter_dimension=0, tiled=True).astype(F32)


def fits(mesh, weights):
    if mesh.shape["fsdp"] != 4 or mesh.shape["dp"] % 2:
        return False
    return all(w.shape[0] * 2 % 128 == 0 and w.shape[1] % 32 == 0 for w in weights)


def columns(values, index, width):
    return lax.dynamic_slice_in_dim(values, index * width, width, axis=1)


def body(mesh, latents, noise_draw, text_states, time_steps, item_lengths, text_lengths, cotangent, time_in, time_out,
         modulation, *others):
    ndp, nfs = mesh.shape["dp"], mesh.shape["fsdp"]
    i, j = lax.axis_index("dp"), lax.axis_index("fsdp")
    width = latents.shape[1]
    items = time_steps.shape[0]
    sent = (time_in, time_out) + others
    direct = fits(mesh, sent)
    full = gather(mesh, sent) if direct else [plain_gather(w) for w in sent]
    t_in, t_out = full[0].astype(F32), full[1].astype(F32)
    weights = full[2:]

    all_steps = lax.all_gather(time_steps, BOTH, axis=0, tiled=True)
    keep, loud, _ = plan(time_steps)
    _, _, embedding = plan(all_steps)
    pre_one = high_dot(embedding, t_in, 1, 1)
    hidden = jax.nn.silu(pre_one)
    pre_two = high_dot(hidden, t_out, 1, 1)
    cond_low = jax.nn.silu(pre_two).astype(BF16)
    deep, wide = modulation.shape
    mine = columns(cond_low, j, deep)
    part = jnp.dot(mine, modulation, preferred_element_type=F32).reshape(ndp, nfs * items, wide)
    part = lax.psum_scatter(part, "fsdp", scatter_dimension=1, tiled=True)
    rows = lax.all_to_all(part, "dp", 0, 0, tiled=True)
    mod = jnp.pad(rows.transpose(1, 0, 2).reshape(items, -1), ((0, 8 - items), (0, 0)))

    text = text_states.reshape(-1, width)
    a, b = run_forward(item_lengths, text_lengths, keep, loud, mod, latents, noise_draw, text, *weights)
    out, lat_grad, *grads, sums = run_backward(item_lengths, text_lengths, keep, mod, text, cotangent, a, b, *weights)
    shares = reduce(mesh, grads) if direct else [plain_reduce(g) for g in grads]

    sent_sums = sums[:items].astype(BF16).reshape(items, ndp, wide).transpose(1, 0, 2)
    got = lax.all_to_all(sent_sums, "dp", 0, 0, tiled=True)
    got = lax.all_gather(got, "fsdp", axis=1, tiled=True).reshape(-1, wide)
    modulation_grad = lax.dot_general(mine, got, (((0,), (0,)), ((), ())), preferred_element_type=F32)
    back = lax.dot_general(got, modulation, (((1,), (1,)), ((), ())), preferred_element_type=F32)
    back = lax.all_gather(lax.psum(back, "dp"), "fsdp", axis=1, tiled=True)
    back_two = back * silu_slope(pre_two)
    back_one = high_dot(back_two, t_out) * silu_slope(pre_one)
    time_in_grad = high_dot(columns(embedding, j, time_in.shape[0]), columns(back_one, i, time_in.shape[1]), 0, 0)
    time_out_grad = high_dot(columns(hidden, j, time_out.shape[0]), columns(back_two, i, time_out.shape[1]), 0, 0)
    return (out, lat_grad, time_in_grad, time_out_grad, modulation_grad, *shares)


def solution(mesh):
    rows, weight = P(BOTH, None), P("fsdp", "dp")
    return jax.shard_map(
        partial(body, mesh),
        mesh=mesh,
        in_specs=(rows, rows, P(BOTH, None, None), P(BOTH), rows, P(BOTH), rows) + (weight,) * 10,
        out_specs=(rows, rows) + (weight,) * 10,
        check_vma=False,
    )
```

```python
from functools import partial
import math

import jax
import jax.numpy as jnp
from jax import lax
from jax.experimental import pallas as pl
from jax.experimental.pallas import tpu as pltpu
from jax.sharding import PartitionSpec as P

F32, BF16 = jnp.float32, jnp.bfloat16
HEADS = 12
FREQ = 256
HD = 64
FACTOR = float(HD) ** -0.5
PAIR = 2 * HD
PAIRS = HEADS // 2
BIG = 1e30
TILE = 256
MIB = 2**20


def dot(left, right, lc, rc):
    return lax.dot_general(left, right, (((lc,), (rc,)), ((), ())), preferred_element_type=F32)


def nt(left, right):
    return dot(left, right, 1, 1)


def nn(left, right):
    return dot(left, right, 1, 0)


def tn(left, right):
    return dot(left, right, 0, 0)


def owners_column(lens, first, rows):
    place = lax.broadcasted_iota(jnp.int32, (rows, 1), 0) + first
    end = lens[0, 0]
    return (place >= end).astype(jnp.int32) + (place >= end + lens[0, 1]).astype(jnp.int32)


def owners_row(lens, cols):
    place = lax.broadcasted_iota(jnp.int32, (1, cols), 1)
    end = lens[0, 0]
    return (place >= end).astype(jnp.int32) + (place >= end + lens[0, 1]).astype(jnp.int32)


def pick(own, a, b, c):
    return jnp.where(own == 0, a, jnp.where(own == 1, b, c))


def expand(own, mod, block, width):
    lo = block * width
    return pick(own, mod[0:1, lo : lo + width], mod[1:2, lo : lo + width], mod[2:3, lo : lo + width])


def item_sums(lens, first, rows, values):
    items = lax.broadcasted_iota(jnp.int32, (16, rows), 0)
    place = lax.broadcasted_iota(jnp.int32, (16, rows), 1) + first
    end = lens[0, 0]
    own = (place >= end).astype(jnp.int32) + (place >= end + lens[0, 1]).astype(jnp.int32)
    member = jnp.where(items == own, 1.0, 0.0).astype(BF16)
    return nn(member, values.astype(BF16))


def fill_masks(lens, tlens, aq, aks, akc):
    rows = aq.shape[0]
    lane = lax.broadcasted_iota(jnp.int32, (rows, PAIR), 1) % HD
    own = owners_column(lens, 0, rows)
    aq[...] = jnp.where(own == lane, 1.0, 0.0).astype(BF16)
    minus = jnp.where((lane >= 3) & (lane < 6), -1.0, 0.0)
    aks[...] = jnp.where((lane < 3) & (own != lane), -BIG, minus).astype(BF16)
    slots = akc.shape[0]
    text = slots // 3
    lane = lax.broadcasted_iota(jnp.int32, (slots, PAIR), 1) % HD
    minus = jnp.where((lane >= 3) & (lane < 6), -1.0, 0.0)
    slot = lax.broadcasted_iota(jnp.int32, (slots, 1), 0)
    item = (slot >= text).astype(jnp.int32) + (slot >= 2 * text).astype(jnp.int32)
    live = slot - item * text < pick(item, tlens[0], tlens[1], tlens[2])
    akc[...] = jnp.where((lane < 3) & ((item != lane) | ~live), -BIG, minus).astype(BF16)


def pieces(column):
    one = column.astype(BF16).astype(F32)
    two = (column - one).astype(BF16).astype(F32)
    return one, two, column - one - two


def in_parts(pair, pump, step=2):
    if pump is None:
        lax.fori_loop(0, PAIRS, pair, 0)
        return
    for first in range(0, PAIRS, step):
        lax.fori_loop(first, first + step, pair, 0)
        pump()


def attention_forward(q, k, k_at, v_at, ak, aq, out, qaug, pump=None):
    frames = q.shape[0]

    def pair(p, carry):
        lanes = pl.ds(pl.multiple_of(p * PAIR, PAIR), PAIR)
        kp = k[:, pl.ds(pl.multiple_of(k_at + p * PAIR, PAIR), PAIR)]
        vp = k[:, pl.ds(pl.multiple_of(v_at + p * PAIR, PAIR), PAIR)]
        klow = lax.broadcasted_iota(jnp.int32, kp.shape, 1) < HD
        keys = (jnp.where(klow, kp, ak[...]), jnp.where(klow, ak[...], kp))
        one = jnp.ones_like(vp)
        values = (jnp.where(klow, vp, one), jnp.where(klow, one, vp))
        lane = lax.broadcasted_iota(jnp.int32, (TILE, PAIR), 1)
        low, inner = lane < HD, lane % HD
        for t in range(frames // TILE):
            rows = pl.ds(t * TILE, TILE)
            qp = q[rows, lanes] * jnp.asarray(FACTOR, BF16)
            mark = aq[rows, :]
            done = []
            for h in range(2):
                own = low if h == 0 else ~low
                qh = jnp.where(own, qp, mark)
                s = nt(qh, keys[h])
                top = jnp.max(s, axis=1, keepdims=True)
                e = jnp.exp(s - top).astype(BF16)
                o = nn(e, values[h])
                total = o[:, HD : HD + 1] if h == 0 else o[:, 0:1]
                done.append(o * (1.0 / total))
                a, b, c = pieces(top + jnp.log(total))
                extra = jnp.where(inner == 3, a, jnp.where(inner == 4, b, c))
                extra = jnp.where((inner >= 3) & (inner < 6), extra, mark.astype(F32)).astype(BF16)
                at = pl.ds(pl.multiple_of((2 * p + h) * PAIR, PAIR), PAIR)
                qaug[rows, at] = jnp.where(own, qp, extra)
            out[rows, lanes] = jnp.where(low, done[0], done[1]).astype(BF16)
        return carry

    in_parts(pair, pump)


def attention_backward(qaug, k, k_at, v_at, ak, att, datt, dq, dk, dk_at, dv_at, acc, pump=None):
    frames = att.shape[0]
    tall = k.shape[0]
    step = TILE if tall % TILE == 0 else PAIR

    def pair(p, carry):
        lanes = pl.ds(pl.multiple_of(p * PAIR, PAIR), PAIR)
        lane = lax.broadcasted_iota(jnp.int32, (frames, PAIR), 1)
        low, inner = lane < HD, lane % HD
        do = datt[:, lanes]
        both = do.astype(F32) * att[:, lanes].astype(F32)
        outs, queries = [], []
        for h in range(2):
            own = low if h == 0 else ~low
            a, b, c = pieces(jnp.sum(jnp.where(own, both, 0.0), axis=1, keepdims=True))
            extra = jnp.where(inner == 3, a, jnp.where(inner == 4, b, c))
            extra = jnp.where((inner >= 3) & (inner < 6), extra, 0.0).astype(BF16)
            outs.append(jnp.where(own, do, extra))
            queries.append(qaug[:, pl.ds(pl.multiple_of((2 * p + h) * PAIR, PAIR), PAIR)])
        for t in range(tall // step):
            rows = pl.ds(t * step, step)
            kp = k[rows, pl.ds(pl.multiple_of(k_at + p * PAIR, PAIR), PAIR)]
            vp = k[rows, pl.ds(pl.multiple_of(v_at + p * PAIR, PAIR), PAIR)]
            mark = ak[rows, :]
            klow = lax.broadcasted_iota(jnp.int32, kp.shape, 1) < HD
            kt = kp.T
            dks, dvs = [], []
            for h in range(2):
                own = klow if h == 0 else ~klow
                pt = jnp.exp(nt(jnp.where(own, kp, mark), queries[h]))
                dpt = nt(jnp.where(own, vp, mark), outs[h])
                dst = (pt * dpt).astype(BF16)
                dvs.append(nn(pt.astype(BF16), do))
                dks.append(nn(dst, queries[h]))
                part = nn(kt[h * HD : (h + 1) * HD, :], dst)
                at = pl.ds(h * HD, HD)
                if t == 0:
                    acc[at, :] = part
                else:
                    acc[at, :] += part
            dk[rows, pl.ds(pl.multiple_of(dk_at + p * PAIR, PAIR), PAIR)] = jnp.where(klow, dks[0], dks[1]).astype(BF16)
            dk[rows, pl.ds(pl.multiple_of(dv_at + p * PAIR, PAIR), PAIR)] = jnp.where(klow, dvs[0], dvs[1]).astype(BF16)
        dq[:, lanes] = (acc[...].T * FACTOR).astype(BF16)
        return carry

    in_parts(pair, pump)


def norm_tile(s):
    width = s.shape[1]
    center = s - jnp.sum(s, axis=1, keepdims=True) * (1.0 / width)
    spread = jnp.sum(center * center, axis=1, keepdims=True) * (1.0 / width)
    rs = lax.rsqrt(spread + 1e-06)
    return center * rs, rs


def tiles(count, fn):
    def step(i, carry):
        fn(pl.multiple_of(i * TILE, TILE))
        return carry

    lax.fori_loop(0, count // TILE, step, 0)


def big_nt(left, right, out, width):
    def step(n, carry):
        cols = pl.ds(pl.multiple_of(n * width, width), width)
        out[:, cols] = nt(left[...], right[cols, :]).astype(BF16)
        return carry

    lax.fori_loop(0, right.shape[0] // width, step, 0)


def big_tn(left, right, out, width):
    def step(n, carry):
        cols = pl.ds(pl.multiple_of(n * width, width), width)
        out[cols, :] = tn(left[:, cols], right[...]).astype(BF16)
        return carry

    lax.fori_loop(0, left.shape[1] // width, step, 0)


def norm_into(s, rows, own, lens, mod, sub, xh, m, rs, width):
    hat, r = norm_tile(s)
    xh[rows, :] = hat.astype(BF16)
    base = 3 * sub
    m[rows, :] = (hat * (1.0 + expand(own, mod, base + 1, width)) + expand(own, mod, base, width)).astype(BF16)
    lane = lax.broadcasted_iota(jnp.int32, (TILE, 128), 1)
    rs[rows, :] = jnp.where(lane == sub, r, rs[rows, :])


class NoLinks:
    pump = None

    def use(self, *names):
        pass

    def fetch(self, *names):
        pass

    def tick(self, n=1):
        pass

    def modulation(self):
        pass

    def done(self, *names):
        pass


def forward_attention(links, lens, tlens, keep, loud, mod, lat, noi, text, wsp, wso, wcq, wcm, wco,
                      stream, xh1, m1, packed, qa1, att1, br1, xh2, m2, mem, qa2, att2, br2, rs,
                      aq, aks, akc, qb, tmp):
    frames, width = lat.shape
    fill_masks(lens, tlens, aq, aks, akc)
    rs[...] = jnp.zeros_like(rs)
    links.modulation()

    def start(at):
        rows = pl.ds(at, TILE)
        own = owners_column(lens, at, TILE)
        s = pick(own, keep[0], keep[1], keep[2]) * lat[rows, :].astype(F32)
        s = s + pick(own, loud[0], loud[1], loud[2]) * noi[rows, :].astype(F32)
        stream[rows, :] = s
        norm_into(s, rows, own, lens, mod, 0, xh1, m1, rs, width)

    tiles(frames, start)
    links.done("xh1", "m1")
    links.use("wsp")
    big_nt(m1, wsp, packed, width)
    links.done("packed")
    links.tick()
    attention_forward(packed, packed, width, 2 * width, aks, aq, att1, qa1, links.pump)
    links.done("att1", "qa1")
    links.use("wso")
    tmp[...] = nt(att1[...], wso[...])

    def middle(at):
        rows = pl.ds(at, TILE)
        own = owners_column(lens, at, TILE)
        br = tmp[rows, :]
        br1[rows, :] = br.astype(BF16)
        s = stream[rows, :] + expand(own, mod, 2, width) * br
        stream[rows, :] = s
        norm_into(s, rows, own, lens, mod, 1, xh2, m2, rs, width)

    tiles(frames, middle)
    links.done("br1", "xh2", "m2", "rs")
    links.tick()
    links.use("wcq", "wcm")
    big_nt(m2, wcq, qb, width)
    big_nt(text, wcm, mem, width)
    links.done("mem")
    attention_forward(qb, mem, 0, width, akc, aq, att2, qa2, links.pump)
    links.done("att2", "qa2")
    links.use("wco")
    tmp[...] = nt(att2[...], wco[...])

    def last(at):
        rows = pl.ds(at, TILE)
        own = owners_column(lens, at, TILE)
        br = tmp[rows, :]
        br2[rows, :] = br.astype(BF16)
        stream[rows, :] = stream[rows, :] + expand(own, mod, 5, width) * br

    tiles(frames, last)
    links.done("br2", "stream")


GELU_A, GELU_B = math.sqrt(2.0 / math.pi), 0.044715


def forward_ff(lens, mod, stream, wup, wdn, xh3, m3, act, slope, br3, out, rs, tmp):
    frames, width = stream.shape
    rs[...] = jnp.zeros_like(rs)

    def start(at):
        rows = pl.ds(at, TILE)
        own = owners_column(lens, at, TILE)
        norm_into(stream[rows, :], rows, own, lens, mod, 2, xh3, m3, rs, width)

    tiles(frames, start)

    def chunk(n, carry):
        cols = pl.ds(pl.multiple_of(n * width, width), width)
        tmp[...] = nt(m3[...], wup[cols, :])

        def gelu(at):
            rows = pl.ds(at, TILE)
            x = tmp[rows, :]
            sq = x * x
            t = jnp.tanh(x * (GELU_A + GELU_A * GELU_B * sq))
            half = 0.5 + 0.5 * t
            act[rows, cols] = (x * half).astype(BF16)
            slope[rows, cols] = (half + half * (1.0 - t) * x * (GELU_A + 3.0 * GELU_A * GELU_B * sq)).astype(BF16)

        tiles(frames, gelu)
        return carry

    lax.fori_loop(0, wup.shape[0] // width, chunk, 0)
    tmp[...] = nt(act[...], wdn[...])

    def last(at):
        rows = pl.ds(at, TILE)
        own = owners_column(lens, at, TILE)
        br = tmp[rows, :]
        br3[rows, :] = br.astype(BF16)
        out[rows, :] = (stream[rows, :] + expand(own, mod, 8, width) * br).astype(BF16)

    tiles(frames, last)


def norm_back(dm, hat, r, stretch):
    width = dm.shape[1]
    dh = dm * (1.0 + stretch)
    a = jnp.sum(dh, axis=1, keepdims=True) * (1.0 / width)
    b = jnp.sum(dh * hat, axis=1, keepdims=True) * (1.0 / width)
    return r * (dh - a - hat * b)


def add_sums(lens, at, sums, cols, values):
    sums[:, cols] += item_sums(lens, at, TILE, values)


def gate_tile(lens, at, own, mod, g, br, sub, sums, b, width):
    rows = pl.ds(at, TILE)
    add_sums(lens, at, sums, pl.ds((3 * sub + 2) * width, width), g * br[rows, :].astype(F32))
    b[rows, :] = (expand(own, mod, 3 * sub + 2, width) * g).astype(BF16)


def norm_back_tile(lens, at, own, mod, dm, xh, rs, sub, sums, width):
    rows = pl.ds(at, TILE)
    hat = xh[rows, :].astype(F32)
    add_sums(lens, at, sums, pl.ds(3 * sub * width, width), dm)
    add_sums(lens, at, sums, pl.ds((3 * sub + 1) * width, width), dm * hat)
    return norm_back(dm, hat, rs[rows, sub : sub + 1], expand(own, mod, 3 * sub + 1, width))


def backward_ff(lens, mod, cot, br3, act, slope, xh3, m3, rs, wup, wdn, g, b2, br2, dwd, dwu, sums, b3, ig, tmp):
    frames, width = cot.shape
    sums[...] = jnp.zeros_like(sums)

    def start(at):
        rows = pl.ds(at, TILE)
        own = owners_column(lens, at, TILE)
        gate_tile(lens, at, own, mod, cot[rows, :].astype(F32), br3, 2, sums, b3, width)

    tiles(frames, start)

    def chunk(n, carry):
        cols = pl.ds(pl.multiple_of(n * width, width), width)
        dwd[:, cols] = tn(b3[...], act[:, cols]).astype(BF16)
        ig[:, cols] = (nn(b3[...], wdn[:, cols]) * slope[:, cols].astype(F32)).astype(BF16)
        dwu[cols, :] = tn(ig[:, cols], m3[...]).astype(BF16)
        return carry

    lax.fori_loop(0, wup.shape[0] // width, chunk, 0)
    tmp[...] = nn(ig[...], wup[...])

    def last(at):
        rows = pl.ds(at, TILE)
        own = owners_column(lens, at, TILE)
        s = cot[rows, :].astype(F32) + norm_back_tile(lens, at, own, mod, tmp[rows, :], xh3, rs, 2, sums, width)
        g[rows, :] = s
        gate_tile(lens, at, own, mod, s, br2, 1, sums, b2, width)

    tiles(frames, last)


def backward_attention(lens, tlens, keep, mod, text, g, b2, xh1, m1, packed, qa1, att1, br1, xh2, m2, mem, qa2, att2, rs,
                       wsp, wso, wcq, wcm, wco, sums_in,
                       lat_grad, dsp, dso, dcq, dcm, dco, sums,
                       aq, aks, akc, datt, dq, dmem, dpack, acc, tmp, stage):
    frames, width = g.shape
    fill_masks(lens, tlens, aq, aks, akc)
    sums[...] = sums_in[...]
    big_tn(b2, att2, dco, width)
    datt[...] = nn(b2[...], wco[...]).astype(BF16)
    attention_backward(qa2, mem, 0, width, akc, att2, datt, dq, dmem, 0, width, acc)
    big_tn(dq, m2, dcq, width)
    big_tn(dmem, text, dcm, width)
    tmp[...] = nn(dq[...], wcq[...])

    def middle(at):
        rows = pl.ds(at, TILE)
        own = owners_column(lens, at, TILE)
        s = g[rows, :] + norm_back_tile(lens, at, own, mod, tmp[rows, :], xh2, rs, 1, sums, width)
        stage[rows, :] = s
        gate_tile(lens, at, own, mod, s, br1, 0, sums, dq, width)

    tiles(frames, middle)
    big_tn(dq, att1, dso, width)
    datt[...] = nn(dq[...], wso[...]).astype(BF16)
    attention_backward(qa1, packed, width, 2 * width, aks, att1, datt, dpack, dpack, width, 2 * width, acc)
    big_tn(dpack, m1, dsp, width)
    tmp[...] = nn(dpack[...], wsp[...])

    def last(at):
        rows = pl.ds(at, TILE)
        own = owners_column(lens, at, TILE)
        s = stage[rows, :] + norm_back_tile(lens, at, own, mod, tmp[rows, :], xh1, rs, 0, sums, width)
        lat_grad[rows, :] = pick(own, keep[0], keep[1], keep[2]) * s

    tiles(frames, last)


def sds(shape, kind=BF16):
    return jax.ShapeDtypeStruct(shape, kind)


VM = pl.BlockSpec(memory_space=pltpu.VMEM)
SM = pl.BlockSpec(memory_space=pltpu.SMEM)


def call(body, scalars, ins, outs, scratch, flops):
    cost = pl.CostEstimate(flops=int(flops), bytes_accessed=int(3e7), transcendentals=0)
    return pl.pallas_call(
        body,
        out_shape=outs,
        in_specs=[SM] * len(scalars) + [VM] * len(ins),
        out_specs=[VM] * len(outs),
        scratch_shapes=scratch,
        cost_estimate=cost,
        compiler_params=pltpu.CompilerParams(vmem_limit_bytes=62 * MIB),
    )(*scalars, *ins)


def run_attention(lens, tlens, keep, loud, mod, lat, noi, text, wsp, wso, wcq, wcm, wco):
    t, d = lat.shape
    x = text.shape[0]
    wide = HEADS * PAIR
    return call(partial(forward_attention, NoLinks()), (lens, tlens, keep, loud),
                (mod, lat, noi, text, wsp, wso, wcq, wcm, wco),
                [sds((t, d), F32), sds((t, d)), sds((t, d)), sds((t, 3 * d)), sds((t, wide)), sds((t, d)), sds((t, d)),
                 sds((t, d)), sds((t, d)), sds((x, 2 * d)), sds((t, wide)), sds((t, d)), sds((t, d)), sds((t, 128), F32)],
                [pltpu.VMEM((t, PAIR), BF16), pltpu.VMEM((t, PAIR), BF16), pltpu.VMEM((x, PAIR), BF16),
                 pltpu.VMEM((t, d), BF16), pltpu.VMEM((t, d), F32)], 3e10)


def run_ff(lens, mod, stream, wup, wdn):
    t, d = stream.shape
    ff = wup.shape[0]
    return call(forward_ff, (lens,), (mod, stream, wup, wdn),
                [sds((t, d)), sds((t, d)), sds((t, ff)), sds((t, ff)), sds((t, d)), sds((t, d)), sds((t, 128), F32)],
                [pltpu.VMEM((t, d), F32)], 1e10)


def run_backward(lens, tlens, keep, mod, text, cot, a, b, wsp, wso, wcq, wcm, wco, wup, wdn):
    t, d = cot.shape
    x = text.shape[0]
    stream, xh1, m1, packed, qa1, att1, br1, xh2, m2, mem, qa2, att2, br2, rs = a
    xh3, m3, act, slope, br3, out, rs3 = b
    ff = wup.shape[0]
    g, b2, dwd, dwu, sums = call(
        partial(lambda lens, mod, cot, br3, act, slope, xh3, m3, rs, wup, wdn, br2, g, b2, dwd, dwu, sums, b3, ig, tmp:
                backward_ff(lens, mod, cot, br3, act, slope, xh3, m3, rs, wup, wdn, g, b2, br2, dwd, dwu, sums, b3, ig, tmp)),
        (lens,), (mod, cot, br3, act, slope, xh3, m3, rs3, wup, wdn, br2),
        [sds((t, d), F32), sds((t, d)), sds((d, ff)), sds((ff, d)), sds((16, 9 * d), F32)],
        [pltpu.VMEM((t, d), BF16), pltpu.VMEM((t, ff), BF16), pltpu.VMEM((t, d), F32)], 3e10)
    lat_grad, dsp, dso, dcq, dcm, dco, sums = call(
        backward_attention, (lens, tlens, keep),
        (mod, text, g, b2, xh1, m1, packed, qa1, att1, br1, xh2, m2, mem, qa2, att2, rs, wsp, wso, wcq, wcm, wco, sums),
        [sds((t, d), F32), sds((3 * d, d)), sds((d, d)), sds((d, d)), sds((2 * d, d)), sds((d, d)), sds((16, 9 * d), F32)],
        [pltpu.VMEM((t, PAIR), BF16), pltpu.VMEM((t, PAIR), BF16), pltpu.VMEM((x, PAIR), BF16),
         pltpu.VMEM((t, d), BF16), pltpu.VMEM((t, d), BF16), pltpu.VMEM((x, 2 * d), BF16), pltpu.VMEM((t, 3 * d), BF16),
         pltpu.VMEM((PAIR, t), F32), pltpu.VMEM((t, d), F32), pltpu.VMEM((t, d), F32)], 6e10)
    return out, lat_grad, dsp, dso, dcq, dcm, dco, dwu, dwd, sums

MESH = pl.DeviceIdType.MESH
ANY = pl.BlockSpec(memory_space=pl.ANY)
UNITS = (
    (0, 0, 1, 0, 2, 0), (1, 0, 1, 0, 2, 1),
    (2, 0, 2 / 3, 0, 2, 0), (2, 2 / 3, 1 / 3, 0, 2, 1),
    (3, 0, 1, 0, 2, 1), (4, 0, 1, 0, 2, 0),
    (5, 0, 1 / 2, 0, 2, 0), (5, 1 / 2, 1 / 2, 0, 2, 1),
    (6, 0, 1, 0, 2, 1),
    (7, 0, 1 / 2, 0, 2, 0), (7, 1 / 2, 1 / 2, 0, 2, 1),
    (8, 0, 1, 0, 1, 0), (8, 0, 1, 1, 1, 1),
)


class Place:
    def __init__(self, depth):
        dp, fsdp = lax.axis_index("dp"), lax.axis_index("fsdp")
        self.depth = depth
        self.z, self.y = dp // 2, dp % 2
        self.x, self.c = fsdp // 2, fsdp % 2

    def at(self, z=None, y=None, x=None, c=None):
        z = self.z if z is None else z
        y = self.y if y is None else y
        x = self.x if x is None else x
        c = self.c if c is None else c
        return (z * 2 + y, x * 2 + c)

    def flat(self, ncore):
        return (self.z * 2 + self.y) * ncore + self.x * 2 + self.c

    def other_z(self, k):
        return lax.rem(self.z + k, self.depth)

    def barrier(self, every=None):
        bar = pltpu.get_barrier_semaphore()
        if every is not None:
            for d in every:
                pl.semaphore_signal(bar, inc=1, device_id=d, device_id_type=MESH)
            pl.semaphore_wait(bar, len(every))
            return
        ids = [self.at(z=self.other_z(k)) for k in range(1, self.depth)]
        ids += [self.at(y=1 - self.y), self.at(x=1 - self.x), self.at(c=1 - self.c)]
        for d in ids:
            pl.semaphore_signal(bar, inc=1, device_id=d, device_id_type=MESH)
        pl.semaphore_wait(bar, len(ids))


class Counter:
    def __init__(self, send, recv):
        self.send, self.recv, self.n = send, recv, 0

    def remote(self, src, dst, device):
        n, self.n = self.n, self.n + 1
        return pltpu.make_async_remote_copy(src_ref=src, dst_ref=dst, send_sem=self.send.at[n], recv_sem=self.recv.at[n],
                                            device_id=device, device_id_type=MESH)

    def local(self, src, dst):
        n, self.n = self.n, self.n + 1
        return pltpu.make_async_copy(src, dst, self.send.at[n])


def unit_shape(unit, shapes):
    w, r0, nr, l0, nl, route = unit
    c8, share = shapes[w]
    half = c8 // 2
    return w, int(round(half * r0)), int(round(half * nr)), l0 * share, nl * share, route, half


class GatherUnit:
    def __init__(self, unit, shapes, place, count, block, out):
        w, r0, n, l0, nl, route, half = unit_shape(unit, shapes)
        self.p, p = place, place
        self.route = route
        share = shapes[w][1]
        row = pl.ds(pl.multiple_of(p.c * half + r0, 16), n)
        other = pl.ds(pl.multiple_of((1 - p.c) * half + r0, 16), n)
        lane = lambda x: pl.ds(pl.multiple_of(x * (2 * share) + l0, 128), nl)
        own = block[w].at[pl.ds(r0, n), pl.ds(l0, nl)]
        o = out[w]
        mine, theirs = lane(p.x), lane(1 - p.x)
        D = p.depth
        dst = o.at[p.z, p.y, row, mine]
        self.local = count.local(own, dst)
        self.zs = [count.remote(own, dst, p.at(z=p.other_z(k))) for k in range(1, D)]
        self.second, self.third = [], []
        for k in range(D):
            zz = p.z if k == 0 else p.other_z(D - k)
            if route == 0:
                a = o.at[zz, p.y, row, mine]
                self.second.append(count.remote(own if k == 0 else a, a, p.at(y=1 - p.y)))
            else:
                a = o.at[zz, p.y, row, mine]
                self.second.append(count.remote(own if k == 0 else a, a, p.at(x=1 - p.x)))
        for k in range(D):
            zz = p.z if k == 0 else p.other_z(D - k)
            if route == 0:
                a = o.at[zz, :, row, mine]
                self.third.append(count.remote(a, a, p.at(x=1 - p.x)))
            else:
                lanes = pl.ds(l0, nl)
                a = [o.at[zz, p.y, row, lane(i)] for i in range(2)]
                self.third.append([count.remote(v, v, p.at(y=1 - p.y)) for v in a])
        sib = [o.at[:, :, row, lane(i)] for i in range(2)]
        self.sib = [count.remote(v, v, p.at(c=1 - p.c)) for v in sib]

    def flat(self, v):
        return v if isinstance(v, list) else [v]

    def begin(self):
        self.local.start()
        for cp in self.zs:
            cp.start()
        self.second[0].start()

    def step_z(self):
        for k, cp in enumerate(self.zs, 1):
            cp.wait_recv()
            self.second[k].start()
        self.local.wait()

    def step_second(self):
        for k, cp in enumerate(self.second):
            cp.wait_recv()
            for c in self.flat(self.third[k]):
                c.start()

    def step_third(self):
        for v in self.third:
            for c in self.flat(v):
                c.wait_recv()
        for c in self.sib:
            c.start()

    def settled(self):
        for c in self.sib:
            c.wait_recv()

    def finish(self):
        for c in self.sib + self.zs + self.second + [c for v in self.third for c in self.flat(v)]:
            c.wait_send()


def others(place, ndp, ncore):
    total = ndp * ncore
    me = place.flat(ncore)
    found = []
    for k in range(1, total):
        t = lax.rem(me + k, total)
        found.append((k, t, (t // ncore, t % ncore)))
    return found


def split_columns(values, index, parts, width):
    picked = values[:, :width]
    for i in range(1, parts):
        picked = jnp.where(index == i, values[:, i * width : (i + 1) * width], picked)
    return picked


def three(value):
    one = value.astype(BF16)
    rest = value - one.astype(F32)
    two = rest.astype(BF16)
    return one, two, (rest - two.astype(F32)).astype(BF16)


def fine_nt(left, right):
    a, b, c = three(left)
    return nt(a, right) + (nt(b, right) + nt(c, right))


def fine_nn(left, right):
    a, b, c = three(left)
    return nn(a, right) + (nn(b, right) + nn(c, right))


def silu(v):
    return v / (1.0 + jnp.exp(-v))


class ForwardLinks:
    NAMES = ("tin", "tout", "wsp", "wso", "wcq", "wcm", "wco", "wup", "wdn")

    def __init__(self, mesh, shapes, r):
        self.ndp, self.ncore = mesh.shape["dp"], mesh.shape["fsdp"]
        self.shapes, self.r = shapes, r
        depth = self.ndp // 2
        self.p = p = Place(depth)
        self.count = count = Counter(r["send"], r["recv"])
        self.every = others(p, self.ndp, self.ncore)
        nw = len(shapes)
        turned, landed, block = r["turned"], r["landed"], r["block"]
        for w in range(nw):
            turned[w][...] = r["shards"][w][...].T
        me = p.flat(self.ncore)
        r["eall"][me] = r["emb"][...]
        p.barrier([d for _, _, d in self.every])
        self.spread = []
        swaps = []
        for w, (c8, share) in enumerate(shapes):
            half = c8 // 2
            theirs = turned[w].at[pl.ds(pl.multiple_of((1 - p.c) * half, 16), half), :]
            swaps.append(count.remote(theirs, landed[w], p.at(c=1 - p.c)))
            swaps[-1].start()
        for k, t, d in self.every:
            c = count.remote(r["eall"].at[me], r["eall"].at[me], d)
            c.start()
            self.spread.append(c)
        self.units = []
        for w, (c8, share) in enumerate(shapes):
            half = c8 // 2
            swaps[w].wait_recv()
            own = turned[w][pl.ds(pl.multiple_of(p.c * half, 16), half), :]
            got = landed[w][...]
            first = p.c == 0
            block[w][...] = jnp.concatenate([jnp.where(first, own, got), jnp.where(first, got, own)], axis=1)
            for u in UNITS:
                if u[0] == w:
                    self.units.append(GatherUnit(u, shapes, p, count, block, r["full"]))
                    self.units[-1].begin()
        self.swaps = swaps
        self.now, self.fetched, self.waiting, self.saves = 0, {}, {}, []
        self.pump = self.tick

    def tick(self, n=1):
        for _ in range(n):
            t, self.now = self.now, self.now + 1
            if t < len(self.units):
                self.units[t].step_z()
            if 0 <= t - 1 < len(self.units):
                self.units[t - 1].step_second()
            if 0 <= t - 2 < len(self.units):
                self.units[t - 2].step_third()

    def fetch(self, *names):
        for name in names:
            if name in self.fetched:
                continue
            w = self.NAMES.index(name)
            mine = [i for i, u in enumerate(UNITS) if u[0] == w]
            while self.now - 3 < mine[-1]:
                self.tick()
            for i in mine:
                self.units[i].settled()
            c8 = self.shapes[w][0]
            self.fetched[name] = []
            for z in range(self.p.depth):
                for y in range(2):
                    c = self.count.local(self.r["full"][w].at[z, y], self.r[name].at[pl.ds((2 * z + y) * c8, c8), :])
                    c.start()
                    self.fetched[name].append(c)

    def use(self, *names):
        self.fetch(*names)
        for name in names:
            for c in self.fetched[name]:
                c.wait()

    def modulation(self):
        r, p = self.r, self.p
        self.fetch("tin", "tout")
        self.tick(2)
        for c in self.spread:
            c.wait_recv()
        self.use("tin", "tout")
        total = self.ndp * self.ncore
        rows = total * 8
        one = fine_nt(r["eall"][...].reshape(rows, FREQ), r["tin"][...])
        hidden = silu(one)
        two = fine_nt(hidden, r["tout"][...])
        r["pre1"][...] = one
        r["pre2"][...] = two
        cond = silu(two)
        deep, wide = r["modw"].shape
        part = wide // 2
        mine = split_columns(cond, p.x * 2 + p.c, self.ncore, deep)
        low = mine.astype(BF16)
        high = pltpu.roll(mine, 4, 0).astype(BF16)
        ready = nn(low, r["modw"][:, :part]) + nn(high, r["modw"][:, part:])
        pad = r["psend"].shape[2] - part
        r["psend"][...] = jnp.concatenate([ready, jnp.zeros((rows, pad), F32)], axis=1).reshape(total, 8, part + pad)
        me = p.flat(self.ncore)
        self.parts = []
        for k, t, d in self.every:
            c = self.count.remote(r["psend"].at[t], r["pgot"].at[me], d)
            c.start()
            self.parts.append(c)
        r["pgot"][me] = r["psend"][me]
        self.done("pre1", "pre2", "eall")
        self.tick(1)
        for c in self.parts:
            c.wait_recv()
        found = []
        for i in range(self.ndp):
            s = r["pgot"][i * self.ncore]
            for j in range(1, self.ncore):
                s = s + r["pgot"][i * self.ncore + j]
            found += [s[:4, :part], s[4:, :part]]
        rows = jnp.concatenate(found, axis=1)
        r["mod"][...] = jnp.concatenate([rows, jnp.zeros_like(rows)], axis=0)
        self.done("mod")

    def done(self, *names):
        for name in names:
            c = self.count.local(self.r[name], self.r["out_" + name])
            c.start()
            self.saves.append(c)

    def finish(self):
        while self.now < len(self.units) + 2:
            self.tick()
        for i, u in enumerate(self.units):
            if self.NAMES[UNITS[i][0]] not in self.fetched:
                u.settled()
            u.finish()
        for c in self.swaps + self.spread + self.parts:
            c.wait_send()
        for c in self.saves:
            c.wait()


SAVED = ("mod", "pre1", "pre2", "eall", "stream", "xh1", "m1", "packed", "qa1", "att1", "br1", "xh2", "m2", "mem", "qa2",
         "att2", "br2", "rs")


def gather_forward(mesh, lens, tlens, keep, loud, emb, lat, noi, text, modw, shards):
    ndp, ncore = mesh.shape["dp"], mesh.shape["fsdp"]
    depth, total = ndp // 2, ndp * ncore
    shapes = [(w.shape[1], w.shape[0]) for w in shards]
    nw = len(shapes)
    t, d = lat.shape
    x, wide = text.shape[0], HEADS * PAIR
    vm = lambda shape, kind=BF16: pltpu.VMEM(shape, kind)
    part = modw.shape[1] // 2
    padded = -(-part // 128) * 128
    kept = {
        "mod": ((8, 9 * d), F32), "pre1": ((total * 8, d), F32), "pre2": ((total * 8, d), F32),
        "eall": ((total, 8, FREQ), F32), "stream": ((t, d), F32), "xh1": ((t, d), BF16), "m1": ((t, d), BF16),
        "packed": ((t, 3 * d), BF16), "qa1": ((t, wide), BF16), "att1": ((t, d), BF16), "br1": ((t, d), BF16),
        "xh2": ((t, d), BF16), "m2": ((t, d), BF16), "mem": ((x, 2 * d), BF16), "qa2": ((t, wide), BF16),
        "att2": ((t, d), BF16), "br2": ((t, d), BF16), "rs": ((t, 128), F32),
    }
    full = [(c8 * ndp, share * ncore) for c8, share in shapes]
    scratch = {name: vm(*kept[name]) for name in SAVED}
    for w, name in enumerate(ForwardLinks.NAMES[:7]):
        scratch[name] = vm(full[w])
    scratch.update(aq=vm((t, PAIR)), aks=vm((t, PAIR)), akc=vm((x, PAIR)), qb=vm((t, d)), tmp=vm((t, d), F32))
    scratch.update(psend=vm((total, 8, padded), F32), pgot=vm((total, 8, padded), F32))
    for w, (c8, share) in enumerate(shapes):
        scratch[f"turned{w}"] = vm((c8, share))
        scratch[f"landed{w}"] = vm((c8 // 2, share))
        scratch[f"block{w}"] = vm((c8 // 2, 2 * share))
    ns = 9 + 2 * (total - 1) + len(SAVED) + 7 * ndp
    ns += sum(1 + (depth - 1) + depth + depth * (1 if u[5] == 0 else 2) + 2 for u in UNITS)
    scratch.update(send=pltpu.SemaphoreType.DMA((ns,)), recv=pltpu.SemaphoreType.DMA((ns,)))
    names = list(scratch)

    def kernel(*refs):
        lens, tlens, keep, loud, emb, lat, noi, text, modw = refs[:9]
        r = dict(emb=emb, modw=modw, shards=refs[9 : 9 + nw])
        at = 9 + nw
        r["full"] = refs[at : at + nw]
        at += nw
        for name in SAVED:
            r["out_" + name] = refs[at]
            at += 1
        r.update(zip(names, refs[at:]))
        for kind in ("turned", "landed", "block"):
            r[kind] = [r[f"{kind}{w}"] for w in range(nw)]
        links = ForwardLinks(mesh, shapes, r)
        forward_attention(links, lens, tlens, keep, loud, r["mod"], lat, noi, text,
                          *[r[n] for n in ("wsp", "wso", "wcq", "wcm", "wco", "stream", "xh1", "m1", "packed", "qa1",
                                           "att1", "br1", "xh2", "m2", "mem", "qa2", "att2", "br2", "rs", "aq", "aks",
                                           "akc", "qb", "tmp")])
        links.finish()

    got = pl.pallas_call(
        kernel,
        out_shape=[sds((depth, 2, c8, share * ncore)) for c8, share in shapes] + [sds(*kept[n]) for n in SAVED],
        in_specs=[SM] * 4 + [VM] * (5 + nw),
        out_specs=[ANY] * (nw + len(SAVED)),
        scratch_shapes=list(scratch.values()),
        cost_estimate=pl.CostEstimate(flops=int(3e10), bytes_accessed=int(6e7), transcendentals=0),
        compiler_params=pltpu.CompilerParams(collective_id=0, has_side_effects=True, vmem_limit_bytes=60 * MIB),
    )(lens, tlens, keep, loud, emb, lat, noi, text, modw, *shards)
    weights = [f.reshape(-1, f.shape[-1]) for f in got[:nw]]
    return weights, dict(zip(SAVED, got[nw:]))


SUM_UNITS = (
    (6, 0, 1, 0, 1, 0), (6, 0, 1, 1, 1, 1), (5, 0, 1 / 2, 0, 2, 0), (5, 1 / 2, 1 / 2, 0, 2, 1),
    (4, 0, 1, 0, 2, 0), (2, 0, 1, 0, 2, 1), (3, 0, 1 / 2, 0, 2, 0), (3, 1 / 2, 1 / 2, 0, 2, 1),
    (1, 0, 1, 0, 2, 1), (0, 0, 2 / 3, 0, 2, 0), (0, 2 / 3, 1 / 3, 0, 2, 1),
)


def each(count, fn):
    def step(i, carry):
        fn(i)
        return carry

    lax.fori_loop(0, count, step, 0)


def plus(a, b):
    return (a.astype(F32) + b.astype(F32)).astype(BF16)


class SumUnit:
    def __init__(self, unit, shapes, place, count, grads, held, cores, first, second, lasts, final):
        w, r0, n, l0, nl, route, half = unit_shape(unit, shapes)
        self.p, self.route, self.D = place, route, place.depth
        p, D = place, place.depth
        share = shapes[w][1]
        row = pl.ds(pl.multiple_of(p.c * half + r0, 16), n)
        other = pl.ds(pl.multiple_of((1 - p.c) * half + r0, 16), n)
        self.held, self.cores, self.first, self.second, self.lasts = held, cores, first, second, lasts
        self.final, self.at = final[w], (pl.ds(r0, n), pl.ds(l0, nl))
        self.loads, self.swaps = [], []
        for i in range(2):
            lane = pl.ds(i * 2 * share + l0, nl)
            self.loads.append(count.local(grads[w].at[:, :, row, lane], held.at[i]))
            self.swaps.append(count.remote(grads[w].at[:, :, other, lane], cores.at[i], p.at(c=1 - p.c)))
        x, y, z = p.x, p.y, p.z
        if route == 0:
            self.one = count.remote(held.at[1 - x], first, p.at(x=1 - x))
            self.two = count.remote(held.at[x, :, 1 - y], second, p.at(y=1 - y))
        else:
            self.one = count.remote(held.at[:, :, 1 - y], first, p.at(y=1 - y))
            self.two = count.remote(held.at[1 - x, :, y], second, p.at(x=1 - x))
        self.three = []
        for k in range(1, D):
            zz = p.other_z(k)
            self.three.append(count.remote(held.at[x, zz, y], lasts.at[k - 1], p.at(z=zz)))

    def begin(self):
        for c in self.loads + self.swaps:
            c.start()

    def step_core(self):
        for c in self.loads:
            c.wait()
        for c in self.swaps:
            c.wait_recv()
        x, y, D = self.p.x, self.p.y, self.D
        held, cores = self.held, self.cores
        if self.route == 0:
            def add(xx):
                def fn(i):
                    held[xx, i // 2, i % 2] = plus(held[xx, i // 2, i % 2], cores[xx, i // 2, i % 2])
                each(2 * D, fn)
            add(1 - x)
            self.one.start()
            add(x)
        else:
            def add(yy):
                def fn(i):
                    held[i // D, i % D, yy] = plus(held[i // D, i % D, yy], cores[i // D, i % D, yy])
                each(2 * D, fn)
            add(1 - y)
            self.one.start()
            add(y)

    def step_one(self):
        self.one.wait_recv()
        x, y, D = self.p.x, self.p.y, self.D
        held, got = self.held, self.first
        if self.route == 0:
            def add(yy):
                def fn(i):
                    held[x, i, yy] = plus(held[x, i, yy], got[i, yy])
                each(D, fn)
            add(1 - y)
            self.two.start()
            add(y)
        else:
            def add(xx):
                def fn(i):
                    held[xx, i, y] = plus(held[xx, i, y], got[xx, i])
                each(D, fn)
            add(1 - x)
            self.two.start()
            add(x)

    def step_two(self):
        self.two.wait_recv()
        x, y = self.p.x, self.p.y
        held, got = self.held, self.second
        for k in range(1, self.D):
            zz = self.p.other_z(k)
            held[x, zz, y] = plus(held[x, zz, y], got[zz])
            self.three[k - 1].start()

    def step_three(self):
        for c in self.three:
            c.wait_recv()
        x, y, z = self.p.x, self.p.y, self.p.z
        total = self.held[x, z, y].astype(F32) + self.second[z].astype(F32)
        for k in range(self.D - 1):
            total += self.lasts[k].astype(F32)
        self.final[self.at] = total

    def finish(self):
        for c in self.swaps + [self.one, self.two] + self.three:
            c.wait_send()


def sum_scratch(shapes, depth, units):
    scratch = []
    for u in units:
        w, r0, n, l0, nl, route, half = unit_shape(u, shapes)
        scratch.append(pltpu.VMEM((2, depth, 2, n, nl), BF16))
        scratch.append(pltpu.VMEM((2, depth, 2, n, nl), BF16))
        scratch.append(pltpu.VMEM((depth, 2, n, nl) if route == 0 else (2, depth, n, nl), BF16))
        scratch.append(pltpu.VMEM((depth, n, nl), BF16))
        scratch.append(pltpu.VMEM((depth - 1, n, nl), BF16))
    return scratch


class LastSwap:
    def __init__(self, w, shapes, place, count, final, part, out):
        self.c8, self.share = shapes[w]
        self.p, self.final, self.part, self.out = place, final[w], part[w], out[w]
        half = self.c8 // 2
        self.rows = pl.ds(pl.multiple_of(place.c * half, 16), half)
        self.copy = count.remote(self.part, self.out.at[self.rows, :], place.at(c=1 - place.c))

    def begin(self):
        total = self.final[...]
        low, high = total[:, : self.share], total[:, self.share :]
        first = self.p.c == 0
        self.part[...] = jnp.where(first, high, low)
        self.copy.start()
        self.out[self.rows, :] = jnp.where(first, low, high)

    def finish(self):
        self.copy.wait()


def reduce_body(depth, shapes, *refs):
    nw = len(shapes)
    grads, outs, rest = refs[:nw], refs[nw : 2 * nw], refs[2 * nw :]
    final, part, rest = rest[:nw], rest[nw : 2 * nw], rest[2 * nw :]
    send, recv = rest[-2:]
    p = Place(depth)
    count = Counter(send, recv)
    p.barrier()
    units = [SumUnit(u, shapes, p, count, grads, *rest[5 * i : 5 * i + 5], final) for i, u in enumerate(SUM_UNITS)]
    swaps = [LastSwap(w, shapes, p, count, final, part, outs) for w in range(nw)]
    n = len(units)
    last = {u[0]: i for i, u in enumerate(SUM_UNITS)}
    for u in units:
        u.begin()
    for t in range(n + 3):
        if t < n:
            units[t].step_core()
        if 0 <= t - 1 < n:
            units[t - 1].step_one()
        if 0 <= t - 2 < n:
            units[t - 2].step_two()
        if 0 <= t - 3 < n:
            units[t - 3].step_three()
            for w, i in last.items():
                if i == t - 3:
                    swaps[w].begin()
    for u in units:
        u.finish()
    for s in swaps:
        s.finish()


def turn_body(nw, *refs):
    for w in range(nw):
        refs[nw + w][...] = refs[w][...].T


def reduce(mesh, grads):
    depth, ncore = mesh.shape["dp"] // 2, mesh.shape["fsdp"]
    shapes = [(g.shape[0] // (2 * depth), g.shape[1] // ncore) for g in grads]
    ns = sum(4 + 2 + depth - 1 for _ in SUM_UNITS) + len(shapes)
    shares = pl.pallas_call(
        partial(reduce_body, depth, shapes),
        out_shape=[sds(s, F32) for s in shapes],
        in_specs=[ANY] * len(grads),
        out_specs=[VM] * len(grads),
        scratch_shapes=[pltpu.VMEM((c8 // 2, 2 * share), F32) for c8, share in shapes]
        + [pltpu.VMEM((c8 // 2, share), F32) for c8, share in shapes]
        + sum_scratch(shapes, depth, SUM_UNITS)
        + [pltpu.SemaphoreType.DMA((ns,)), pltpu.SemaphoreType.DMA((ns,))],
        compiler_params=pltpu.CompilerParams(collective_id=1, has_side_effects=True, vmem_limit_bytes=50 * MIB),
    )(*[g.reshape(depth, 2, c8, g.shape[1]) for g, (c8, _) in zip(grads, shapes)])
    return pl.pallas_call(
        partial(turn_body, len(shapes)),
        out_shape=[sds(s[::-1], F32) for s in shapes],
        in_specs=[VM] * len(grads),
        out_specs=[VM] * len(grads),
    )(*shares)


HIGHEST = lax.Precision.HIGHEST
BOTH = ("dp", "fsdp")


def high_dot(left, right, lc=1, rc=0):
    return lax.dot_general(left, right, (((lc,), (rc,)), ((), ())), precision=HIGHEST, preferred_element_type=F32)


def plan(step_row):
    levels = step_row.astype(F32)
    cumulative = jnp.cos(0.5 * math.pi * (levels / 1000.0 + 0.008) / 1.008) ** 2
    half_width = FREQ // 2
    frequency = jnp.exp(-math.log(10000.0) * jnp.arange(half_width, dtype=F32) / half_width)
    angles = levels[:, None] * frequency[None, :]
    embedding = jnp.concatenate([jnp.cos(angles), jnp.sin(angles)], axis=1)
    return jnp.sqrt(cumulative), jnp.sqrt(1.0 - cumulative), embedding


def silu_slope(v):
    s = jax.nn.sigmoid(v)
    return s * (1.0 + v * (1.0 - s))


def plain_gather(w):
    part = lax.all_gather(w, "fsdp", axis=0, tiled=True)
    return lax.all_gather(part, "dp", axis=1, tiled=True).T


def plain_reduce(g):
    part = lax.psum_scatter(g.T, "dp", scatter_dimension=1, tiled=True).astype(BF16)
    return lax.psum_scatter(part, "fsdp", scatter_dimension=0, tiled=True).astype(F32)


def fits(mesh, weights):
    if mesh.shape["fsdp"] != 4 or mesh.shape["dp"] % 2:
        return False
    return all(w.shape[0] * 2 % 128 == 0 and w.shape[1] % 32 == 0 for w in weights)


def columns(values, index, width):
    return lax.dynamic_slice_in_dim(values, index * width, width, axis=1)


def body(mesh, latents, noise_draw, text_states, time_steps, item_lengths, text_lengths, cotangent, time_in, time_out,
         modulation, *others):
    ndp, nfs = mesh.shape["dp"], mesh.shape["fsdp"]
    i, j = lax.axis_index("dp"), lax.axis_index("fsdp")
    width = latents.shape[1]
    items = time_steps.shape[0]
    sent = (time_in, time_out) + others
    direct = fits(mesh, sent)
    text = text_states.reshape(-1, width)
    keep, loud, embedding = plan(time_steps)
    deep, wide = modulation.shape
    if direct:
        embedding = jnp.pad(embedding, ((0, 8 - items), (0, 0)))
        full, saved = gather_forward(mesh, item_lengths, text_lengths, keep, loud, embedding, latents, noise_draw, text,
                                     modulation, sent)
        mod = saved["mod"]
        first = [saved[n] for n in SAVED[4:]]
        embedding = saved["eall"][:, :items].reshape(-1, FREQ)
        pre_one, pre_two = [saved[n].reshape(-1, 8, width)[:, :items].reshape(-1, width) for n in ("pre1", "pre2")]
        t_out = full[1].astype(F32)
        hidden = jax.nn.silu(pre_one)
        mine = columns(jax.nn.silu(pre_two).astype(BF16), j, deep)
    else:
        full = [plain_gather(w) for w in sent]
        t_in, t_out = full[0].astype(F32), full[1].astype(F32)
        embedding = lax.all_gather(embedding, BOTH, axis=0, tiled=True)
        pre_one = high_dot(embedding, t_in, 1, 1)
        hidden = jax.nn.silu(pre_one)
        pre_two = high_dot(hidden, t_out, 1, 1)
        mine = columns(jax.nn.silu(pre_two).astype(BF16), j, deep)
        part = jnp.dot(mine, modulation, preferred_element_type=F32).reshape(ndp, nfs * items, wide)
        part = lax.psum_scatter(part, "fsdp", scatter_dimension=1, tiled=True)
        rows = lax.all_to_all(part, "dp", 0, 0, tiled=True)
        mod = jnp.pad(rows.transpose(1, 0, 2).reshape(items, -1), ((0, 8 - items), (0, 0)))
        first = run_attention(item_lengths, text_lengths, keep, loud, mod, latents, noise_draw, text, *full[2:7])
    weights = full[2:]
    second = run_ff(item_lengths, mod, first[0], *weights[5:])
    out, lat_grad, *grads, sums = run_backward(item_lengths, text_lengths, keep, mod, text, cotangent, first, second, *weights)
    shares = reduce(mesh, grads) if direct else [plain_reduce(g) for g in grads]

    sent_sums = sums[:items].astype(BF16).reshape(items, ndp, wide).transpose(1, 0, 2)
    got = lax.all_to_all(sent_sums, "dp", 0, 0, tiled=True)
    got = lax.all_gather(got, "fsdp", axis=1, tiled=True).reshape(-1, wide)
    modulation_grad = lax.dot_general(mine, got, (((0,), (0,)), ((), ())), preferred_element_type=F32)
    back = lax.dot_general(got, modulation, (((1,), (1,)), ((), ())), preferred_element_type=F32)
    back = lax.all_gather(lax.psum(back, "dp"), "fsdp", axis=1, tiled=True)
    back_two = back * silu_slope(pre_two)
    back_one = high_dot(back_two, t_out) * silu_slope(pre_one)
    time_in_grad = high_dot(columns(embedding, j, time_in.shape[0]), columns(back_one, i, time_in.shape[1]), 0, 0)
    time_out_grad = high_dot(columns(hidden, j, time_out.shape[0]), columns(back_two, i, time_out.shape[1]), 0, 0)
    return (out, lat_grad, time_in_grad, time_out_grad, modulation_grad, *shares)


def solution(mesh):
    rows, weight = P(BOTH, None), P("fsdp", "dp")
    return jax.shard_map(
        partial(body, mesh),
        mesh=mesh,
        in_specs=(rows, rows, P(BOTH, None, None), P(BOTH), rows, P(BOTH), rows) + (weight,) * 10,
        out_specs=(rows, rows) + (weight,) * 10,
        check_vma=False,
    )
```

```python
from functools import partial
import math

import jax
import jax.numpy as jnp
from jax import lax
from jax.experimental import pallas as pl
from jax.experimental.pallas import tpu as pltpu
from jax.sharding import PartitionSpec as P

F32, BF16 = jnp.float32, jnp.bfloat16
HEADS = 12
FREQ = 256
HD = 64
FACTOR = float(HD) ** -0.5
PAIR = 2 * HD
PAIRS = HEADS // 2
BIG = 1e30
TILE = 256
MIB = 2**20


def dot(left, right, lc, rc):
    return lax.dot_general(left, right, (((lc,), (rc,)), ((), ())), preferred_element_type=F32)


def nt(left, right):
    return dot(left, right, 1, 1)


def nn(left, right):
    return dot(left, right, 1, 0)


def tn(left, right):
    return dot(left, right, 0, 0)


def owners_column(lens, first, rows):
    place = lax.broadcasted_iota(jnp.int32, (rows, 1), 0) + first
    end = lens[0, 0]
    return (place >= end).astype(jnp.int32) + (place >= end + lens[0, 1]).astype(jnp.int32)


def owners_row(lens, cols):
    place = lax.broadcasted_iota(jnp.int32, (1, cols), 1)
    end = lens[0, 0]
    return (place >= end).astype(jnp.int32) + (place >= end + lens[0, 1]).astype(jnp.int32)


def pick(own, a, b, c):
    return jnp.where(own == 0, a, jnp.where(own == 1, b, c))


def expand(own, mod, block, width):
    lo = block * width
    return pick(own, mod[0:1, lo : lo + width], mod[1:2, lo : lo + width], mod[2:3, lo : lo + width])


def item_sums(lens, first, rows, values):
    items = lax.broadcasted_iota(jnp.int32, (16, rows), 0)
    place = lax.broadcasted_iota(jnp.int32, (16, rows), 1) + first
    end = lens[0, 0]
    own = (place >= end).astype(jnp.int32) + (place >= end + lens[0, 1]).astype(jnp.int32)
    member = jnp.where(items == own, 1.0, 0.0).astype(BF16)
    return nn(member, values.astype(BF16))


def fill_masks(lens, tlens, aq, aks, akc):
    rows = aq.shape[0]
    lane = lax.broadcasted_iota(jnp.int32, (rows, PAIR), 1) % HD
    own = owners_column(lens, 0, rows)
    aq[...] = jnp.where(own == lane, 1.0, 0.0).astype(BF16)
    minus = jnp.where((lane >= 3) & (lane < 6), -1.0, 0.0)
    aks[...] = jnp.where((lane < 3) & (own != lane), -BIG, minus).astype(BF16)
    slots = akc.shape[0]
    text = slots // 3
    lane = lax.broadcasted_iota(jnp.int32, (slots, PAIR), 1) % HD
    minus = jnp.where((lane >= 3) & (lane < 6), -1.0, 0.0)
    slot = lax.broadcasted_iota(jnp.int32, (slots, 1), 0)
    item = (slot >= text).astype(jnp.int32) + (slot >= 2 * text).astype(jnp.int32)
    live = slot - item * text < pick(item, tlens[0], tlens[1], tlens[2])
    akc[...] = jnp.where((lane < 3) & ((item != lane) | ~live), -BIG, minus).astype(BF16)


def pieces(column):
    one = column.astype(BF16).astype(F32)
    two = (column - one).astype(BF16).astype(F32)
    return one, two, column - one - two


def in_parts(pair, pump, step=3):
    if pump is None:
        lax.fori_loop(0, PAIRS, pair, 0)
        return
    for first in range(0, PAIRS, step):
        lax.fori_loop(first, first + step, pair, 0)
        pump()


def attention_forward(q, k, k_at, v_at, ak, aq, out, qaug, pump=None):
    frames = q.shape[0]

    def pair(p, carry):
        lanes = pl.ds(pl.multiple_of(p * PAIR, PAIR), PAIR)
        kp = k[:, pl.ds(pl.multiple_of(k_at + p * PAIR, PAIR), PAIR)]
        vp = k[:, pl.ds(pl.multiple_of(v_at + p * PAIR, PAIR), PAIR)]
        klow = lax.broadcasted_iota(jnp.int32, kp.shape, 1) < HD
        keys = (jnp.where(klow, kp, ak[...]), jnp.where(klow, ak[...], kp))
        one = jnp.ones_like(vp)
        values = (jnp.where(klow, vp, one), jnp.where(klow, one, vp))
        lane = lax.broadcasted_iota(jnp.int32, (TILE, PAIR), 1)
        low, inner = lane < HD, lane % HD
        for t in range(frames // TILE):
            rows = pl.ds(t * TILE, TILE)
            qp = q[rows, lanes] * jnp.asarray(FACTOR, BF16)
            mark = aq[rows, :]
            done = []
            for h in range(2):
                own = low if h == 0 else ~low
                qh = jnp.where(own, qp, mark)
                s = nt(qh, keys[h])
                top = jnp.max(s, axis=1, keepdims=True)
                e = jnp.exp(s - top).astype(BF16)
                o = nn(e, values[h])
                total = o[:, HD : HD + 1] if h == 0 else o[:, 0:1]
                done.append(o * (1.0 / total))
                a, b, c = pieces(top + jnp.log(total))
                extra = jnp.where(inner == 3, a, jnp.where(inner == 4, b, c))
                extra = jnp.where((inner >= 3) & (inner < 6), extra, mark.astype(F32)).astype(BF16)
                at = pl.ds(pl.multiple_of((2 * p + h) * PAIR, PAIR), PAIR)
                qaug[rows, at] = jnp.where(own, qp, extra)
            out[rows, lanes] = jnp.where(low, done[0], done[1]).astype(BF16)
        return carry

    in_parts(pair, pump)


def attention_backward(qaug, k, k_at, v_at, ak, att, datt, dq, dk, dk_at, dv_at, acc, pump=None):
    frames = att.shape[0]
    tall = k.shape[0]
    step = TILE if tall % TILE == 0 else PAIR

    def pair(p, carry):
        lanes = pl.ds(pl.multiple_of(p * PAIR, PAIR), PAIR)
        lane = lax.broadcasted_iota(jnp.int32, (frames, PAIR), 1)
        low, inner = lane < HD, lane % HD
        do = datt[:, lanes]
        both = do.astype(F32) * att[:, lanes].astype(F32)
        outs, queries = [], []
        for h in range(2):
            own = low if h == 0 else ~low
            a, b, c = pieces(jnp.sum(jnp.where(own, both, 0.0), axis=1, keepdims=True))
            extra = jnp.where(inner == 3, a, jnp.where(inner == 4, b, c))
            extra = jnp.where((inner >= 3) & (inner < 6), extra, 0.0).astype(BF16)
            outs.append(jnp.where(own, do, extra))
            queries.append(qaug[:, pl.ds(pl.multiple_of((2 * p + h) * PAIR, PAIR), PAIR)])
        for t in range(tall // step):
            rows = pl.ds(t * step, step)
            kp = k[rows, pl.ds(pl.multiple_of(k_at + p * PAIR, PAIR), PAIR)]
            vp = k[rows, pl.ds(pl.multiple_of(v_at + p * PAIR, PAIR), PAIR)]
            mark = ak[rows, :]
            klow = lax.broadcasted_iota(jnp.int32, kp.shape, 1) < HD
            kt = kp.T
            dks, dvs = [], []
            for h in range(2):
                own = klow if h == 0 else ~klow
                pt = jnp.exp(nt(jnp.where(own, kp, mark), queries[h]))
                dpt = nt(jnp.where(own, vp, mark), outs[h])
                dst = (pt * dpt).astype(BF16)
                dvs.append(nn(pt.astype(BF16), do))
                dks.append(nn(dst, queries[h]))
                part = nn(kt[h * HD : (h + 1) * HD, :], dst)
                at = pl.ds(h * HD, HD)
                if t == 0:
                    acc[at, :] = part
                else:
                    acc[at, :] += part
            dk[rows, pl.ds(pl.multiple_of(dk_at + p * PAIR, PAIR), PAIR)] = jnp.where(klow, dks[0], dks[1]).astype(BF16)
            dk[rows, pl.ds(pl.multiple_of(dv_at + p * PAIR, PAIR), PAIR)] = jnp.where(klow, dvs[0], dvs[1]).astype(BF16)
        dq[:, lanes] = (acc[...].T * FACTOR).astype(BF16)
        return carry

    in_parts(pair, pump)


def norm_tile(s):
    width = s.shape[1]
    center = s - jnp.sum(s, axis=1, keepdims=True) * (1.0 / width)
    spread = jnp.sum(center * center, axis=1, keepdims=True) * (1.0 / width)
    rs = lax.rsqrt(spread + 1e-06)
    return center * rs, rs


def tiles(count, fn):
    def step(i, carry):
        fn(pl.multiple_of(i * TILE, TILE))
        return carry

    lax.fori_loop(0, count // TILE, step, 0)


def big_nt(left, right, out, width):
    def step(n, carry):
        cols = pl.ds(pl.multiple_of(n * width, width), width)
        out[:, cols] = nt(left[...], right[cols, :]).astype(BF16)
        return carry

    lax.fori_loop(0, right.shape[0] // width, step, 0)


def big_tn(left, right, out, width):
    def step(n, carry):
        cols = pl.ds(pl.multiple_of(n * width, width), width)
        out[cols, :] = tn(left[:, cols], right[...]).astype(BF16)
        return carry

    lax.fori_loop(0, left.shape[1] // width, step, 0)


def norm_into(s, rows, own, lens, mod, sub, xh, m, rs, width):
    hat, r = norm_tile(s)
    xh[rows, :] = hat.astype(BF16)
    base = 3 * sub
    m[rows, :] = (hat * (1.0 + expand(own, mod, base + 1, width)) + expand(own, mod, base, width)).astype(BF16)
    lane = lax.broadcasted_iota(jnp.int32, (TILE, 128), 1)
    rs[rows, :] = jnp.where(lane == sub, r, rs[rows, :])


class NoLinks:
    pump = None

    def use(self, *names):
        pass

    def fetch(self, *names):
        pass

    def tick(self, n=1):
        pass

    def modulation(self):
        pass

    def done(self, *names):
        pass


def forward_attention(links, lens, tlens, keep, loud, mod, lat, noi, text, wsp, wso, wcq, wcm, wco,
                      stream, xh1, m1, packed, qa1, att1, br1, xh2, m2, mem, qa2, att2, br2, rs,
                      aq, aks, akc, qb, tmp):
    frames, width = lat.shape
    fill_masks(lens, tlens, aq, aks, akc)
    rs[...] = jnp.zeros_like(rs)
    links.modulation()

    def start(at):
        rows = pl.ds(at, TILE)
        own = owners_column(lens, at, TILE)
        s = pick(own, keep[0], keep[1], keep[2]) * lat[rows, :].astype(F32)
        s = s + pick(own, loud[0], loud[1], loud[2]) * noi[rows, :].astype(F32)
        stream[rows, :] = s
        norm_into(s, rows, own, lens, mod, 0, xh1, m1, rs, width)

    tiles(frames, start)
    links.done("xh1", "m1")
    links.use("wsp")
    big_nt(m1, wsp, packed, width)
    links.done("packed")
    links.tick()
    attention_forward(packed, packed, width, 2 * width, aks, aq, att1, qa1, links.pump)
    links.done("att1", "qa1")
    links.use("wso")
    tmp[...] = nt(att1[...], wso[...])

    def middle(at):
        rows = pl.ds(at, TILE)
        own = owners_column(lens, at, TILE)
        br = tmp[rows, :]
        br1[rows, :] = br.astype(BF16)
        s = stream[rows, :] + expand(own, mod, 2, width) * br
        stream[rows, :] = s
        norm_into(s, rows, own, lens, mod, 1, xh2, m2, rs, width)

    tiles(frames, middle)
    links.done("br1", "xh2", "m2", "rs")
    links.use("wcq", "wcm")
    big_nt(m2, wcq, qb, width)
    big_nt(text, wcm, mem, width)
    links.done("mem")
    attention_forward(qb, mem, 0, width, akc, aq, att2, qa2, links.pump)
    links.done("att2", "qa2")
    links.use("wco")
    tmp[...] = nt(att2[...], wco[...])

    def last(at):
        rows = pl.ds(at, TILE)
        own = owners_column(lens, at, TILE)
        br = tmp[rows, :]
        br2[rows, :] = br.astype(BF16)
        stream[rows, :] = stream[rows, :] + expand(own, mod, 5, width) * br

    tiles(frames, last)
    links.done("br2", "stream")


GELU_A, GELU_B = math.sqrt(2.0 / math.pi), 0.044715


def forward_ff(lens, mod, stream, wup, wdn, xh3, m3, act, slope, br3, out, rs, tmp):
    frames, width = stream.shape
    rs[...] = jnp.zeros_like(rs)

    def start(at):
        rows = pl.ds(at, TILE)
        own = owners_column(lens, at, TILE)
        norm_into(stream[rows, :], rows, own, lens, mod, 2, xh3, m3, rs, width)

    tiles(frames, start)

    def chunk(n, carry):
        cols = pl.ds(pl.multiple_of(n * width, width), width)
        tmp[...] = nt(m3[...], wup[cols, :])

        def gelu(at):
            rows = pl.ds(at, TILE)
            x = tmp[rows, :]
            sq = x * x
            t = jnp.tanh(x * (GELU_A + GELU_A * GELU_B * sq))
            half = 0.5 + 0.5 * t
            act[rows, cols] = (x * half).astype(BF16)
            slope[rows, cols] = (half + half * (1.0 - t) * x * (GELU_A + 3.0 * GELU_A * GELU_B * sq)).astype(BF16)

        tiles(frames, gelu)
        return carry

    lax.fori_loop(0, wup.shape[0] // width, chunk, 0)
    tmp[...] = nt(act[...], wdn[...])

    def last(at):
        rows = pl.ds(at, TILE)
        own = owners_column(lens, at, TILE)
        br = tmp[rows, :]
        br3[rows, :] = br.astype(BF16)
        out[rows, :] = (stream[rows, :] + expand(own, mod, 8, width) * br).astype(BF16)

    tiles(frames, last)


def norm_back(dm, hat, r, stretch):
    width = dm.shape[1]
    dh = dm * (1.0 + stretch)
    a = jnp.sum(dh, axis=1, keepdims=True) * (1.0 / width)
    b = jnp.sum(dh * hat, axis=1, keepdims=True) * (1.0 / width)
    return r * (dh - a - hat * b)


def add_sums(lens, at, sums, cols, values):
    sums[:, cols] += item_sums(lens, at, TILE, values)


def gate_tile(lens, at, own, mod, g, br, sub, sums, b, width):
    rows = pl.ds(at, TILE)
    add_sums(lens, at, sums, pl.ds((3 * sub + 2) * width, width), g * br[rows, :].astype(F32))
    b[rows, :] = (expand(own, mod, 3 * sub + 2, width) * g).astype(BF16)


def norm_back_tile(lens, at, own, mod, dm, xh, rs, sub, sums, width):
    rows = pl.ds(at, TILE)
    hat = xh[rows, :].astype(F32)
    add_sums(lens, at, sums, pl.ds(3 * sub * width, width), dm)
    add_sums(lens, at, sums, pl.ds((3 * sub + 1) * width, width), dm * hat)
    return norm_back(dm, hat, rs[rows, sub : sub + 1], expand(own, mod, 3 * sub + 1, width))


def backward_ff(lens, mod, cot, br3, act, slope, xh3, m3, rs, wup, wdn, g, b2, br2, dwd, dwu, sums, b3, ig, tmp):
    frames, width = cot.shape
    sums[...] = jnp.zeros_like(sums)

    def start(at):
        rows = pl.ds(at, TILE)
        own = owners_column(lens, at, TILE)
        gate_tile(lens, at, own, mod, cot[rows, :].astype(F32), br3, 2, sums, b3, width)

    tiles(frames, start)

    def chunk(n, carry):
        cols = pl.ds(pl.multiple_of(n * width, width), width)
        dwd[:, cols] = tn(b3[...], act[:, cols]).astype(BF16)
        ig[:, cols] = (nn(b3[...], wdn[:, cols]) * slope[:, cols].astype(F32)).astype(BF16)
        dwu[cols, :] = tn(ig[:, cols], m3[...]).astype(BF16)
        return carry

    lax.fori_loop(0, wup.shape[0] // width, chunk, 0)
    tmp[...] = nn(ig[...], wup[...])

    def last(at):
        rows = pl.ds(at, TILE)
        own = owners_column(lens, at, TILE)
        s = cot[rows, :].astype(F32) + norm_back_tile(lens, at, own, mod, tmp[rows, :], xh3, rs, 2, sums, width)
        g[rows, :] = s
        gate_tile(lens, at, own, mod, s, br2, 1, sums, b2, width)

    tiles(frames, last)


def backward_attention(lens, tlens, keep, mod, text, g, b2, xh1, m1, packed, qa1, att1, br1, xh2, m2, mem, qa2, att2, rs,
                       wsp, wso, wcq, wcm, wco, sums_in,
                       lat_grad, dsp, dso, dcq, dcm, dco, sums,
                       aq, aks, akc, datt, dq, dmem, dpack, acc, tmp, stage):
    frames, width = g.shape
    fill_masks(lens, tlens, aq, aks, akc)
    sums[...] = sums_in[...]
    big_tn(b2, att2, dco, width)
    datt[...] = nn(b2[...], wco[...]).astype(BF16)
    attention_backward(qa2, mem, 0, width, akc, att2, datt, dq, dmem, 0, width, acc)
    big_tn(dq, m2, dcq, width)
    big_tn(dmem, text, dcm, width)
    tmp[...] = nn(dq[...], wcq[...])

    def middle(at):
        rows = pl.ds(at, TILE)
        own = owners_column(lens, at, TILE)
        s = g[rows, :] + norm_back_tile(lens, at, own, mod, tmp[rows, :], xh2, rs, 1, sums, width)
        stage[rows, :] = s
        gate_tile(lens, at, own, mod, s, br1, 0, sums, dq, width)

    tiles(frames, middle)
    big_tn(dq, att1, dso, width)
    datt[...] = nn(dq[...], wso[...]).astype(BF16)
    attention_backward(qa1, packed, width, 2 * width, aks, att1, datt, dpack, dpack, width, 2 * width, acc)
    big_tn(dpack, m1, dsp, width)
    tmp[...] = nn(dpack[...], wsp[...])

    def last(at):
        rows = pl.ds(at, TILE)
        own = owners_column(lens, at, TILE)
        s = stage[rows, :] + norm_back_tile(lens, at, own, mod, tmp[rows, :], xh1, rs, 0, sums, width)
        lat_grad[rows, :] = pick(own, keep[0], keep[1], keep[2]) * s

    tiles(frames, last)


def sds(shape, kind=BF16):
    return jax.ShapeDtypeStruct(shape, kind)


VM = pl.BlockSpec(memory_space=pltpu.VMEM)
SM = pl.BlockSpec(memory_space=pltpu.SMEM)


def call(body, scalars, ins, outs, scratch, flops):
    cost = pl.CostEstimate(flops=int(flops), bytes_accessed=int(3e7), transcendentals=0)
    return pl.pallas_call(
        body,
        out_shape=outs,
        in_specs=[SM] * len(scalars) + [VM] * len(ins),
        out_specs=[VM] * len(outs),
        scratch_shapes=scratch,
        cost_estimate=cost,
        compiler_params=pltpu.CompilerParams(vmem_limit_bytes=62 * MIB),
    )(*scalars, *ins)


def run_attention(lens, tlens, keep, loud, mod, lat, noi, text, wsp, wso, wcq, wcm, wco):
    t, d = lat.shape
    x = text.shape[0]
    wide = HEADS * PAIR
    return call(partial(forward_attention, NoLinks()), (lens, tlens, keep, loud),
                (mod, lat, noi, text, wsp, wso, wcq, wcm, wco),
                [sds((t, d), F32), sds((t, d)), sds((t, d)), sds((t, 3 * d)), sds((t, wide)), sds((t, d)), sds((t, d)),
                 sds((t, d)), sds((t, d)), sds((x, 2 * d)), sds((t, wide)), sds((t, d)), sds((t, d)), sds((t, 128), F32)],
                [pltpu.VMEM((t, PAIR), BF16), pltpu.VMEM((t, PAIR), BF16), pltpu.VMEM((x, PAIR), BF16),
                 pltpu.VMEM((t, d), BF16), pltpu.VMEM((t, d), F32)], 3e10)


def run_ff(lens, mod, stream, wup, wdn):
    t, d = stream.shape
    ff = wup.shape[0]
    return call(forward_ff, (lens,), (mod, stream, wup, wdn),
                [sds((t, d)), sds((t, d)), sds((t, ff)), sds((t, ff)), sds((t, d)), sds((t, d)), sds((t, 128), F32)],
                [pltpu.VMEM((t, d), F32)], 1e10)


def run_ff_back(lens, mod, cot, br2, kept, wup, wdn):
    t, d = cot.shape
    xh3, m3, act, slope, br3, out, rs3 = kept
    ff = wup.shape[0]

    def kernel(lens, mod, cot, br3, act, slope, xh3, m3, rs, wup, wdn, br2, g, b2, dwd, dwu, sums, b3, ig, tmp):
        backward_ff(lens, mod, cot, br3, act, slope, xh3, m3, rs, wup, wdn, g, b2, br2, dwd, dwu, sums, b3, ig, tmp)

    return call(kernel, (lens,), (mod, cot, br3, act, slope, xh3, m3, rs3, wup, wdn, br2),
                [sds((t, d), F32), sds((t, d)), sds((d, ff)), sds((ff, d)), sds((16, 9 * d), F32)],
                [pltpu.VMEM((t, d), BF16), pltpu.VMEM((t, ff), BF16), pltpu.VMEM((t, d), F32)], 3e10)


def run_backward(lens, tlens, keep, mod, text, cot, a, b, wsp, wso, wcq, wcm, wco, wup, wdn):
    t, d = cot.shape
    x = text.shape[0]
    stream, xh1, m1, packed, qa1, att1, br1, xh2, m2, mem, qa2, att2, br2, rs = a
    out = b[5]
    g, b2, dwd, dwu, sums = run_ff_back(lens, mod, cot, br2, b, wup, wdn)
    lat_grad, dsp, dso, dcq, dcm, dco, sums = call(
        backward_attention, (lens, tlens, keep),
        (mod, text, g, b2, xh1, m1, packed, qa1, att1, br1, xh2, m2, mem, qa2, att2, rs, wsp, wso, wcq, wcm, wco, sums),
        [sds((t, d), F32), sds((3 * d, d)), sds((d, d)), sds((d, d)), sds((2 * d, d)), sds((d, d)), sds((16, 9 * d), F32)],
        [pltpu.VMEM((t, PAIR), BF16), pltpu.VMEM((t, PAIR), BF16), pltpu.VMEM((x, PAIR), BF16),
         pltpu.VMEM((t, d), BF16), pltpu.VMEM((t, d), BF16), pltpu.VMEM((x, 2 * d), BF16), pltpu.VMEM((t, 3 * d), BF16),
         pltpu.VMEM((PAIR, t), F32), pltpu.VMEM((t, d), F32), pltpu.VMEM((t, d), F32)], 6e10)
    return out, lat_grad, dsp, dso, dcq, dcm, dco, dwu, dwd, sums

MESH = pl.DeviceIdType.MESH
ANY = pl.BlockSpec(memory_space=pl.ANY)
GROUPS = (
    ((0, 0, 1, 0, 2, 0), (1, 0, 1 / 3, 0, 2, 0), (1, 1 / 3, 2 / 3, 0, 2, 1)),
    ((2, 0, 5 / 9, 0, 2, 0), (2, 5 / 9, 4 / 9, 0, 2, 1)),
    ((3, 0, 1, 0, 2, 1), (4, 0, 1, 0, 2, 0)),
    ((5, 0, 1 / 2, 0, 2, 0), (5, 1 / 2, 1 / 2, 0, 2, 1)),
    ((6, 0, 1 / 3, 0, 2, 0), (6, 1 / 3, 2 / 3, 0, 2, 1)),
    ((7, 0, 1 / 4, 0, 2, 0), (7, 1 / 4, 1 / 4, 0, 2, 1)),
    ((7, 1 / 2, 1 / 4, 0, 2, 0), (7, 3 / 4, 1 / 4, 0, 2, 1)),
    ((8, 0, 1 / 3, 0, 2, 0), (8, 1 / 3, 1 / 3, 0, 2, 1)),
    ((8, 2 / 3, 1 / 3, 0, 1, 0), (8, 2 / 3, 1 / 3, 1, 1, 1)),
)
UNITS = tuple(u for g in GROUPS for u in g)


class Place:
    def __init__(self, depth):
        dp, fsdp = lax.axis_index("dp"), lax.axis_index("fsdp")
        self.depth = depth
        self.z, self.y = dp // 2, dp % 2
        self.x, self.c = fsdp // 2, fsdp % 2

    def at(self, z=None, y=None, x=None, c=None):
        z = self.z if z is None else z
        y = self.y if y is None else y
        x = self.x if x is None else x
        c = self.c if c is None else c
        return (z * 2 + y, x * 2 + c)

    def flat(self, ncore):
        return (self.z * 2 + self.y) * ncore + self.x * 2 + self.c

    def other_z(self, k):
        return lax.rem(self.z + k, self.depth)

    def barrier(self, every=None):
        bar = pltpu.get_barrier_semaphore()
        if every is not None:
            for d in every:
                pl.semaphore_signal(bar, inc=1, device_id=d, device_id_type=MESH)
            pl.semaphore_wait(bar, len(every))
            return
        ids = [self.at(z=self.other_z(k)) for k in range(1, self.depth)]
        ids += [self.at(y=1 - self.y), self.at(x=1 - self.x), self.at(c=1 - self.c)]
        for d in ids:
            pl.semaphore_signal(bar, inc=1, device_id=d, device_id_type=MESH)
        pl.semaphore_wait(bar, len(ids))


class Counter:
    def __init__(self, send, recv):
        self.send, self.recv, self.n = send, recv, 0

    def remote(self, src, dst, device):
        n, self.n = self.n, self.n + 1
        return pltpu.make_async_remote_copy(src_ref=src, dst_ref=dst, send_sem=self.send.at[n], recv_sem=self.recv.at[n],
                                            device_id=device, device_id_type=MESH)

    def local(self, src, dst):
        n, self.n = self.n, self.n + 1
        return pltpu.make_async_copy(src, dst, self.send.at[n])


def unit_shape(unit, shapes):
    w, r0, nr, l0, nl, route = unit
    c8, share = shapes[w]
    half = c8 // 2
    return w, round(half * r0), round(half * nr), round(l0 * share), round(nl * share), route, half


class GatherUnit:
    def __init__(self, unit, shapes, place, count, block, out):
        w, r0, n, l0, nl, route, half = unit_shape(unit, shapes)
        self.p, p = place, place
        self.route = route
        share = shapes[w][1]
        row = pl.ds(pl.multiple_of(p.c * half + r0, 16), n)
        other = pl.ds(pl.multiple_of((1 - p.c) * half + r0, 16), n)
        lane = lambda x: pl.ds(pl.multiple_of(x * (2 * share) + l0, 128), nl)
        own = block[w].at[pl.ds(r0, n), pl.ds(l0, nl)]
        o = out[w]
        mine, theirs = lane(p.x), lane(1 - p.x)
        D = p.depth
        dst = o.at[p.z, p.y, row, mine]
        self.local = count.local(own, dst)
        self.zs = [count.remote(own, dst, p.at(z=p.other_z(k))) for k in range(1, D)]
        self.second, self.third = [], []
        for k in range(D):
            zz = p.z if k == 0 else p.other_z(D - k)
            if route == 0:
                a = o.at[zz, p.y, row, mine]
                self.second.append(count.remote(own if k == 0 else a, a, p.at(y=1 - p.y)))
            else:
                a = o.at[zz, p.y, row, mine]
                self.second.append(count.remote(own if k == 0 else a, a, p.at(x=1 - p.x)))
        for k in range(D):
            zz = p.z if k == 0 else p.other_z(D - k)
            if route == 0:
                a = o.at[zz, :, row, mine]
                self.third.append(count.remote(a, a, p.at(x=1 - p.x)))
            else:
                lanes = pl.ds(l0, nl)
                a = [o.at[zz, p.y, row, lane(i)] for i in range(2)]
                self.third.append([count.remote(v, v, p.at(y=1 - p.y)) for v in a])
        sib = [o.at[:, :, row, lane(i)] for i in range(2)]
        self.sib = [count.remote(v, v, p.at(c=1 - p.c)) for v in sib]

    def flat(self, v):
        return v if isinstance(v, list) else [v]

    def begin(self):
        self.local.start()
        for cp in self.zs:
            cp.start()
        self.second[0].start()

    def step_z(self):
        for k, cp in enumerate(self.zs, 1):
            cp.wait_recv()
            self.second[k].start()
        self.local.wait()

    def step_second(self):
        for k, cp in enumerate(self.second):
            cp.wait_recv()
            for c in self.flat(self.third[k]):
                c.start()

    def step_third(self):
        for v in self.third:
            for c in self.flat(v):
                c.wait_recv()
        for c in self.sib:
            c.start()

    def settled(self):
        for c in self.sib:
            c.wait_recv()

    def finish(self):
        for c in self.sib + self.zs + self.second + [c for v in self.third for c in self.flat(v)]:
            c.wait_send()


def others(place, ndp, ncore):
    total = ndp * ncore
    me = place.flat(ncore)
    found = []
    for k in range(1, total):
        t = lax.rem(me + k, total)
        found.append((k, t, (t // ncore, t % ncore)))
    return found


def split_columns(values, index, parts, width):
    picked = values[:, :width]
    for i in range(1, parts):
        picked = jnp.where(index == i, values[:, i * width : (i + 1) * width], picked)
    return picked


def three(value):
    one = value.astype(BF16)
    rest = value - one.astype(F32)
    two = rest.astype(BF16)
    return one, two, (rest - two.astype(F32)).astype(BF16)


def fine_nt(left, right):
    a, b, c = three(left)
    return nt(a, right) + (nt(b, right) + nt(c, right))


def fine_nn(left, right):
    a, b, c = three(left)
    return nn(a, right) + (nn(b, right) + nn(c, right))


def silu(v):
    return v / (1.0 + jnp.exp(-v))


AHEAD = 2


class ForwardLinks:
    NAMES = ("tin", "tout", "wsp", "wso", "wcq", "wcm", "wco", "wup", "wdn")

    def __init__(self, mesh, shapes, r):
        self.ndp, self.ncore = mesh.shape["dp"], mesh.shape["fsdp"]
        self.shapes, self.r = shapes, r
        depth = self.ndp // 2
        self.p = p = Place(depth)
        self.count = count = Counter(r["send"], r["recv"])
        self.every = others(p, self.ndp, self.ncore)
        nw = len(shapes)
        turned, landed, block = r["turned"], r["landed"], r["block"]
        for w in range(nw):
            turned[w][...] = r["shards"][w][...].T
        me = p.flat(self.ncore)
        r["eall"][me] = r["emb"][...]
        p.barrier([d for _, _, d in self.every])
        self.spread = []
        swaps = []
        for w, (c8, share) in enumerate(shapes):
            half = c8 // 2
            theirs = turned[w].at[pl.ds(pl.multiple_of((1 - p.c) * half, 16), half), :]
            swaps.append(count.remote(theirs, landed[w], p.at(c=1 - p.c)))
            swaps[-1].start()
        for k, t, d in self.every:
            c = count.remote(r["eall"].at[me], r["eall"].at[me], d)
            c.start()
            self.spread.append(c)
        self.units = []
        for w, (c8, share) in enumerate(shapes):
            half = c8 // 2
            swaps[w].wait_recv()
            own = turned[w][pl.ds(pl.multiple_of(p.c * half, 16), half), :]
            got = landed[w][...]
            first = p.c == 0
            block[w][...] = jnp.concatenate([jnp.where(first, own, got), jnp.where(first, got, own)], axis=1)
        self.units = [[GatherUnit(u, shapes, p, count, block, r["full"]) for u in g] for g in GROUPS]
        self.swaps, self.begun = swaps, 0
        self.start(AHEAD)
        self.now, self.fetched, self.waiting, self.saves = 0, {}, {}, []
        self.pump = self.tick

    def start(self, upto):
        while self.begun < min(upto, len(self.units)):
            for u in self.units[self.begun]:
                u.begin()
            self.begun += 1

    def tick(self, n=1):
        for _ in range(n):
            t, self.now = self.now, self.now + 1
            n = len(self.units)
            self.start(t + AHEAD)
            if t < n:
                for u in self.units[t]:
                    u.step_z()
            if 0 <= t - 1 < n:
                for u in self.units[t - 1]:
                    u.step_second()
            if 0 <= t - 2 < n:
                for u in self.units[t - 2]:
                    u.step_third()

    def fetch(self, *names):
        for name in names:
            if name in self.fetched:
                continue
            w = self.NAMES.index(name)
            mine = [(i, k) for i, g in enumerate(GROUPS) for k, u in enumerate(g) if u[0] == w]
            while self.now - 3 < mine[-1][0]:
                self.tick()
            for i, k in mine:
                self.units[i][k].settled()
            c8 = self.shapes[w][0]
            self.fetched[name] = []
            for z in range(self.p.depth):
                for y in range(2):
                    c = self.count.local(self.r["full"][w].at[z, y], self.r[name].at[pl.ds((2 * z + y) * c8, c8), :])
                    c.start()
                    self.fetched[name].append(c)

    def use(self, *names):
        self.fetch(*names)
        for name in names:
            for c in self.fetched[name]:
                c.wait()

    def modulation(self):
        r, p = self.r, self.p
        self.fetch("tin", "tout")
        for c in self.spread:
            c.wait_recv()
        self.use("tin", "tout")
        total = self.ndp * self.ncore
        rows = total * 8
        one = fine_nt(r["eall"][...].reshape(rows, FREQ), r["tin"][...])
        hidden = silu(one)
        two = fine_nt(hidden, r["tout"][...])
        r["pre1"][...] = one
        r["pre2"][...] = two
        cond = silu(two)
        deep, wide = r["modw"].shape
        part = wide // 2
        mine = split_columns(cond, p.x * 2 + p.c, self.ncore, deep)
        low = mine.astype(BF16)
        high = pltpu.roll(mine, 4, 0).astype(BF16)
        ready = nn(low, r["modw"][:, :part]) + nn(high, r["modw"][:, part:])
        pad = r["psend"].shape[2] - part
        r["psend"][...] = jnp.concatenate([ready, jnp.zeros((rows, pad), F32)], axis=1).reshape(total, 8, part + pad)
        me = p.flat(self.ncore)
        self.parts = []
        for k, t, d in self.every:
            c = self.count.remote(r["psend"].at[t], r["pgot"].at[me], d)
            c.start()
            self.parts.append(c)
        r["pgot"][me] = r["psend"][me]
        self.done("pre1", "pre2", "eall")
        self.tick(1)
        for c in self.parts:
            c.wait_recv()
        found = []
        for i in range(self.ndp):
            s = r["pgot"][i * self.ncore]
            for j in range(1, self.ncore):
                s = s + r["pgot"][i * self.ncore + j]
            found += [s[:4, :part], s[4:, :part]]
        rows = jnp.concatenate(found, axis=1)
        r["mod"][...] = jnp.concatenate([rows, jnp.zeros_like(rows)], axis=0)
        self.done("mod")

    def done(self, *names):
        for name in names:
            c = self.count.local(self.r[name], self.r["out_" + name])
            c.start()
            self.saves.append(c)

    def finish(self):
        while self.now < len(self.units) + 2:
            self.tick()
        for g, units in zip(GROUPS, self.units):
            for u, unit in zip(g, units):
                if self.NAMES[u[0]] not in self.fetched:
                    unit.settled()
                unit.finish()
        for c in self.swaps + self.spread + self.parts:
            c.wait_send()
        for c in self.saves:
            c.wait()


SAVED = ("mod", "pre1", "pre2", "eall", "stream", "xh1", "m1", "packed", "qa1", "att1", "br1", "xh2", "m2", "mem", "qa2",
         "att2", "br2", "rs")


def gather_forward(mesh, lens, tlens, keep, loud, emb, lat, noi, text, modw, shards):
    ndp, ncore = mesh.shape["dp"], mesh.shape["fsdp"]
    depth, total = ndp // 2, ndp * ncore
    shapes = [(w.shape[1], w.shape[0]) for w in shards]
    nw = len(shapes)
    t, d = lat.shape
    x, wide = text.shape[0], HEADS * PAIR
    vm = lambda shape, kind=BF16: pltpu.VMEM(shape, kind)
    part = modw.shape[1] // 2
    padded = -(-part // 128) * 128
    kept = {
        "mod": ((8, 9 * d), F32), "pre1": ((total * 8, d), F32), "pre2": ((total * 8, d), F32),
        "eall": ((total, 8, FREQ), F32), "stream": ((t, d), F32), "xh1": ((t, d), BF16), "m1": ((t, d), BF16),
        "packed": ((t, 3 * d), BF16), "qa1": ((t, wide), BF16), "att1": ((t, d), BF16), "br1": ((t, d), BF16),
        "xh2": ((t, d), BF16), "m2": ((t, d), BF16), "mem": ((x, 2 * d), BF16), "qa2": ((t, wide), BF16),
        "att2": ((t, d), BF16), "br2": ((t, d), BF16), "rs": ((t, 128), F32),
    }
    full = [(c8 * ndp, share * ncore) for c8, share in shapes]
    scratch = {name: vm(*kept[name]) for name in SAVED}
    for w, name in enumerate(ForwardLinks.NAMES[:7]):
        scratch[name] = vm(full[w])
    scratch.update(aq=vm((t, PAIR)), aks=vm((t, PAIR)), akc=vm((x, PAIR)), qb=vm((t, d)), tmp=vm((t, d), F32))
    scratch.update(psend=vm((total, 8, padded), F32), pgot=vm((total, 8, padded), F32))
    for w, (c8, share) in enumerate(shapes):
        scratch[f"turned{w}"] = vm((c8, share))
        scratch[f"landed{w}"] = vm((c8 // 2, share))
        scratch[f"block{w}"] = vm((c8 // 2, 2 * share))
    ns = 9 + 2 * (total - 1) + len(SAVED) + 7 * ndp
    ns += sum(1 + (depth - 1) + depth + depth * (1 if u[5] == 0 else 2) + 2 for u in UNITS)
    scratch.update(send=pltpu.SemaphoreType.DMA((ns,)), recv=pltpu.SemaphoreType.DMA((ns,)))
    names = list(scratch)

    def kernel(*refs):
        lens, tlens, keep, loud, emb, lat, noi, text, modw = refs[:9]
        r = dict(emb=emb, modw=modw, shards=refs[9 : 9 + nw])
        at = 9 + nw
        r["full"] = refs[at : at + nw]
        at += nw
        for name in SAVED:
            r["out_" + name] = refs[at]
            at += 1
        r.update(zip(names, refs[at:]))
        for kind in ("turned", "landed", "block"):
            r[kind] = [r[f"{kind}{w}"] for w in range(nw)]
        links = ForwardLinks(mesh, shapes, r)
        forward_attention(links, lens, tlens, keep, loud, r["mod"], lat, noi, text,
                          *[r[n] for n in ("wsp", "wso", "wcq", "wcm", "wco", "stream", "xh1", "m1", "packed", "qa1",
                                           "att1", "br1", "xh2", "m2", "mem", "qa2", "att2", "br2", "rs", "aq", "aks",
                                           "akc", "qb", "tmp")])
        links.finish()

    got = pl.pallas_call(
        kernel,
        out_shape=[sds((depth, 2, c8, share * ncore)) for c8, share in shapes] + [sds(*kept[n]) for n in SAVED],
        in_specs=[SM] * 4 + [VM] * (5 + nw),
        out_specs=[ANY] * (nw + len(SAVED)),
        scratch_shapes=list(scratch.values()),
        cost_estimate=pl.CostEstimate(flops=int(3e10), bytes_accessed=int(6e7), transcendentals=0),
        compiler_params=pltpu.CompilerParams(collective_id=0, has_side_effects=True, vmem_limit_bytes=60 * MIB),
    )(lens, tlens, keep, loud, emb, lat, noi, text, modw, *shards)
    weights = [f.reshape(-1, f.shape[-1]) for f in got[:nw]]
    return weights, dict(zip(SAVED, got[nw:]))


SUM_GROUPS = (
    ((6, 0, 1, 0, 1 / 2, 0), (6, 0, 1, 1 / 2, 1 / 2, 1)),
    ((6, 0, 1, 1, 1 / 2, 0), (6, 0, 1, 3 / 2, 1 / 2, 1)),
    ((5, 0, 1 / 4, 0, 2, 0), (5, 1 / 4, 1 / 4, 0, 2, 1)),
    ((5, 1 / 2, 1 / 4, 0, 2, 0), (5, 3 / 4, 1 / 4, 0, 2, 1)),
    ((4, 0, 1, 0, 2, 0), (2, 0, 1, 0, 2, 1)),
    ((3, 0, 1 / 2, 0, 2, 0), (3, 1 / 2, 1 / 2, 0, 2, 1)),
    ((1, 0, 1, 0, 2, 0), (0, 0, 1 / 3, 0, 2, 1)),
    ((0, 1 / 3, 1 / 3, 0, 2, 0), (0, 2 / 3, 1 / 3, 0, 2, 1)),
)
EARLY = 4


def each(count, fn):
    def step(i, carry):
        fn(i)
        return carry

    lax.fori_loop(0, count, step, 0)


def plus(a, b):
    return (a.astype(F32) + b.astype(F32)).astype(BF16)


class SumUnit:
    def __init__(self, unit, shapes, place, count, grads, own, bufs, final):
        w, r0, n, l0, nl, route, half = unit_shape(unit, shapes)
        self.p, self.route, self.D = place, route, place.depth
        p, D = place, place.depth
        share = shapes[w][1]
        row = pl.ds(pl.multiple_of(p.c * half + r0, 16), n)
        other = pl.ds(pl.multiple_of((1 - p.c) * half + r0, 16), n)
        self.total, self.first, self.second, self.lasts = bufs
        self.final, self.at = final[w], (pl.ds(r0, n), pl.ds(l0, nl))
        self.loads, self.swaps, self.lanes = [], [], []
        self.row, self.grad, self.own = row, grads[w], own
        for i in range(2):
            lane = pl.ds(i * 2 * share + l0, nl)
            self.lanes.append(lane)
            if own is not None:
                self.loads.append(count.local(grads[w].at[:, :, row, lane], own.at[i]))
            self.swaps.append(count.remote(grads[w].at[:, :, other, lane], self.total.at[i], p.at(c=1 - p.c)))
        x, y, z = p.x, p.y, p.z
        total = self.total
        if route == 0:
            self.one = count.remote(total.at[1 - x], self.first, p.at(x=1 - x))
            self.two = count.remote(total.at[x, :, 1 - y], self.second, p.at(y=1 - y))
        else:
            self.one = count.remote(total.at[:, :, 1 - y], self.first, p.at(y=1 - y))
            self.two = count.remote(total.at[1 - x, :, y], self.second, p.at(x=1 - x))
        self.three = []
        for k in range(1, D):
            zz = p.other_z(k)
            self.three.append(count.remote(total.at[x, zz, y], self.lasts.at[k - 1], p.at(z=zz)))

    def load(self):
        for c in self.loads:
            c.start()

    def swap(self):
        for c in self.swaps:
            c.start()

    def add_own(self, x, z, y):
        if self.own is not None:
            v = self.own[x, z, y]
        else:
            if isinstance(x, int):
                v = self.grad[z, y, self.row, self.lanes[x]]
            else:
                width = self.lanes[1].start - self.lanes[0].start
                lane = pl.ds(pl.multiple_of(x * width + self.lanes[0].start, 128), self.lanes[0].size)
                v = self.grad[z, y, self.row, lane]
        self.total[x, z, y] = plus(self.total[x, z, y], v)

    def step_core(self):
        for c in self.loads:
            c.wait()
        for c in self.swaps:
            c.wait_recv()
        x, y, D = self.p.x, self.p.y, self.D
        if self.route == 0:
            each(2 * D, lambda i: self.add_own(1 - x, i // 2, i % 2))
            self.one.start()
            each(2 * D, lambda i: self.add_own(x, i // 2, i % 2))
        else:
            each(2 * D, lambda i: self.add_own(i // D, i % D, 1 - y))
            self.one.start()
            each(2 * D, lambda i: self.add_own(i // D, i % D, y))

    def step_one(self):
        self.one.wait_recv()
        x, y, D = self.p.x, self.p.y, self.D
        total, got = self.total, self.first
        if self.route == 0:
            def add(yy):
                def fn(i):
                    total[x, i, yy] = plus(total[x, i, yy], got[i, yy])
                each(D, fn)
            add(1 - y)
            self.two.start()
            add(y)
        else:
            def add(xx):
                def fn(i):
                    total[xx, i, y] = plus(total[xx, i, y], got[xx, i])
                each(D, fn)
            add(1 - x)
            self.two.start()
            add(x)

    def step_two(self):
        self.two.wait_recv()
        x, y = self.p.x, self.p.y
        total, got = self.total, self.second
        for k in range(1, self.D):
            zz = self.p.other_z(k)
            total[x, zz, y] = plus(total[x, zz, y], got[zz])
            self.three[k - 1].start()

    def step_three(self):
        for c in self.three:
            c.wait_recv()
        x, y, z = self.p.x, self.p.y, self.p.z
        value = self.total[x, z, y].astype(F32) + self.second[z].astype(F32)
        for k in range(self.D - 1):
            value += self.lasts[k].astype(F32)
        self.final[self.at] = value

    def sent(self):
        for c in self.swaps + [self.one, self.two] + self.three:
            c.wait_send()


class LastSwap:
    def __init__(self, w, shapes, place, count, final, part, out):
        self.c8, self.share = shapes[w]
        self.p, self.final, self.part, self.out = place, final[w], part[w], out[w]
        half = self.c8 // 2
        self.rows = pl.ds(pl.multiple_of(place.c * half, 16), half)
        self.copy = count.remote(self.part, self.out.at[self.rows, :], place.at(c=1 - place.c))

    def begin(self):
        total = self.final[...]
        low, high = total[:, : self.share], total[:, self.share :]
        first = self.p.c == 0
        self.part[...] = jnp.where(first, high, low)
        self.copy.start()
        self.out[self.rows, :] = jnp.where(first, low, high)

    def finish(self):
        self.copy.wait()


class BackwardLinks:
    def __init__(self, mesh, shapes, r):
        self.ndp, self.ncore = mesh.shape["dp"], mesh.shape["fsdp"]
        self.shapes, self.r = shapes, r
        self.p = p = Place(self.ndp // 2)
        self.count = count = Counter(r["send"], r["recv"])
        self.every = others(p, self.ndp, self.ncore)
        p.barrier([d for _, _, d in self.every])
        self.groups, self.now = [], 0
        for gi, g in enumerate(SUM_GROUPS):
            early = gi < EARLY
            units = []
            for k, u in enumerate(g):
                own = r[f"own{gi % 2}_{k}"] if early else None
                units.append(SumUnit(u, shapes, p, count, r["grads"], own, r["slot_of"][(gi, k)], r["final"]))
            self.groups.append(units)
        self.swaps = [LastSwap(w, shapes, p, count, r["final"], r["part"], r["shares"]) for w in range(len(shapes))]
        last = {u[0]: gi for gi, g in enumerate(SUM_GROUPS) for u in g}
        self.closing = {gi: [w for w, l in last.items() if l == gi] for gi in range(len(SUM_GROUPS))}
        for units in self.groups[:EARLY]:
            for u in units:
                u.swap()
        for units in self.groups[:2]:
            for u in units:
                u.load()
        self.moves, self.saves = {}, []

    def load(self, name, src=None, to=None):
        to = self.r[name] if to is None else to
        c = self.count.local(self.r["in_" + (src or name)], to)
        c.start()
        self.moves[src or name] = c

    def ready(self, *names):
        for name in names:
            self.moves.pop(name).wait()

    def step(self, t, first, upto):
        for back, name in ((0, "step_core"), (1, "step_one"), (2, "step_two"), (3, "step_three")):
            g = first + t - back
            if first <= g < upto:
                for u in self.groups[g]:
                    getattr(u, name)()
                if back == 0 and g + 2 < EARLY:
                    for u in self.groups[g + 2]:
                        u.load()
                if back == 3:
                    for w in self.closing[g]:
                        self.swaps[w].begin()

    def tick(self):
        self.step(self.now, 0, EARLY)
        self.now += 1

    def drain_early(self):
        p = self.p
        while self.now < EARLY + 3:
            self.tick()
        for units in self.groups[:EARLY]:
            for u in units:
                u.sent()
        ids = [p.at(z=p.other_z(k)) for k in range(1, p.depth)] + [p.at(y=1 - p.y), p.at(x=1 - p.x), p.at(c=1 - p.c)]
        for d in ids:
            pl.semaphore_signal(self.r["free"], inc=1, device_id=d, device_id_type=MESH)
        self.partners, self.open = len(ids), False

    def swap(self, *groups):
        if not self.open:
            pl.semaphore_wait(self.r["free"], self.partners)
            self.open = True
        for gi in groups:
            for u in self.groups[gi]:
                u.swap()

    def late(self, t):
        self.step(t, EARLY, len(self.groups))

    def save(self, value, name):
        c = self.count.local(value, self.r["out_" + name])
        c.start()
        self.saves.append(c)

    def send_sums(self, sums):
        r, p = self.r, self.p
        total = self.ndp * self.ncore
        wide = sums.shape[1] // self.ndp
        part = wide // 2
        pad = r["gs"].shape[2] - part
        value = sums[...].astype(BF16).astype(F32)
        blank = jnp.zeros((8, pad), F32)
        for i in range(self.ndp):
            low = value[:4, i * wide : i * wide + part]
            high = value[:4, i * wide + part : (i + 1) * wide]
            r["gs"][i] = jnp.concatenate([jnp.concatenate([low, high], axis=0), blank], axis=1)
        me = p.flat(self.ncore)
        self.spread = []
        for k, t, d in self.every:
            c = self.count.remote(r["gs"].at[t // self.ncore], r["ggot"].at[me], d)
            c.start()
            self.spread.append(c)
        r["ggot"][me] = r["gs"][me // self.ncore]

    def condition_back(self, pre2):
        r, p = self.r, self.p
        total = self.ndp * self.ncore
        rows = total * 8
        for c in self.spread:
            c.wait_recv()
        modw = r["modw"]
        deep, wide = modw.shape
        part = wide // 2
        got = r["ggot"][...].reshape(rows, r["ggot"].shape[2])[:, :part].astype(BF16)
        mine = split_columns(silu(pre2[...]), p.x * 2 + p.c, self.ncore, deep)
        high = pltpu.roll(mine, 4, 0).astype(BF16)
        r["mg"][...] = jnp.concatenate([tn(mine.astype(BF16), got), tn(high, got)], axis=1)
        back = nt(got, modw[:, :part]) + pltpu.roll(nt(got, modw[:, part:]), rows - 4, 0)
        live = lax.broadcasted_iota(jnp.int32, (rows, 1), 0) % 8 < 4
        back = jnp.where(live, back, 0.0)
        pad = r["ds"].shape[2] - deep
        block = self.ncore * 8
        r["ds"][...] = jnp.concatenate([back, jnp.zeros((rows, pad), F32)], axis=1).reshape(self.ndp, block, deep + pad)
        dp, fsdp = p.z * 2 + p.y, p.x * 2 + p.c
        self.sums = []
        for k in range(1, self.ndp):
            i = lax.rem(dp + k, self.ndp)
            c = self.count.remote(r["ds"].at[i], r["dgot"].at[dp], (i, fsdp))
            c.start()
            self.sums.append(c)
        r["dgot"][dp] = r["ds"][dp]

    def condition_spread(self):
        r, p = self.r, self.p
        for c in self.sums:
            c.wait_recv()
        value = r["dgot"][0]
        for i in range(1, self.ndp):
            value = value + r["dgot"][i]
        block = self.ncore * 8
        at = lax.broadcasted_iota(jnp.int32, (self.ncore * 4, block), 0)
        of = lax.broadcasted_iota(jnp.int32, (self.ncore * 4, block), 1)
        pick_rows = jnp.where(of == (at // 4) * 8 + at % 4, 1.0, 0.0).astype(BF16)
        me = p.flat(self.ncore)
        r["cgot"][me] = nn(pick_rows, value.astype(BF16)).astype(BF16)
        self.last = []
        for k, t, d in self.every:
            c = self.count.remote(r["cgot"].at[me], r["cgot"].at[me], d)
            c.start()
            self.last.append(c)

    def time_back(self, pre1, pre2, tout):
        r, p = self.r, self.p
        total = self.ndp * self.ncore
        rows = total * 8
        deep = r["modw"].shape[0]
        for c in self.last:
            c.wait_recv()
        small = self.ncore * 4
        cols = []
        for j in range(self.ncore):
            cols.append(jnp.concatenate([r["cgot"][i * self.ncore + j][:, :deep] for i in range(self.ndp)], axis=0))
        dense = jnp.concatenate(cols, axis=1)
        count = self.ndp * small
        at = lax.broadcasted_iota(jnp.int32, (rows, count), 0)
        of = lax.broadcasted_iota(jnp.int32, (rows, count), 1)
        spread = jnp.where((at % 8 < 4) & (of == (at // 8) * 4 + at % 8), 1.0, 0.0).astype(BF16)
        one, two = pre1[...], pre2[...]
        back_two = nn(spread, dense) * silu_back(two)
        back_one = fine_nn(back_two, tout[...]) * silu_back(one)
        hidden = silu(one)
        dp, fsdp = p.z * 2 + p.y, p.x * 2 + p.c
        wide = r["tog"].shape[1]
        left = split_columns(hidden, fsdp, self.ncore, r["tog"].shape[0])
        r["tog"][...] = fine_tn(left, split_columns(back_two, dp, self.ndp, wide))
        emb = r["eall"][...].reshape(rows, FREQ)
        left = split_columns(emb, fsdp, self.ncore, r["tig"].shape[0])
        r["tig"][...] = fine_tn(left, split_columns(back_one, dp, self.ndp, wide))

    def finish(self):
        for units in self.groups[EARLY:]:
            for u in units:
                u.sent()
        for s in self.swaps:
            s.finish()
        for c in self.spread + self.sums + self.last:
            c.wait_send()
        for c in self.saves:
            c.wait()


def silu_back(v):
    s = 1.0 / (1.0 + jnp.exp(-v))
    return s * (1.0 + v * (1.0 - s))


def fine_tn(left, right):
    a, b, c = three(left)
    d, e, f = three(right)
    return tn(a, d) + (tn(a, e) + tn(b, d)) + (tn(b, e) + tn(a, f) + tn(c, d))


def backward_linked(links, r, lens, tlens, keep, mod, text, rs, sums):
    frames, width = r["stage"].shape
    slots = text.shape[0]
    qa, att, m, xh, wo, dq, datt, stage, tmp = [r[n] for n in ("qa", "att", "m", "xh", "wo", "dq", "datt", "stage", "tmp")]
    packed, dpack, acc = r["packed"], r["dpack"], r["acc"]
    mem = packed.at[pl.ds(0, slots), pl.ds(0, 2 * width)]
    dmem = dpack.at[pl.ds(0, slots), pl.ds(0, 2 * width)]
    grads = r["flat"]
    links.load("dq", "b2")
    links.load("att", "att2")
    links.load("wo", "wco")
    links.load("qa", "qa2")
    links.load("mem", to=mem)
    links.load("m", "m2")
    links.load("xh", "xh2")
    links.load("stage", "g")
    links.load("wsp")
    fill_masks(lens, tlens, r["aq"], r["aks"], r["akc"])
    links.ready("b2", "att2", "wco")
    grads(4, dq, att, width)
    datt[...] = nn(dq[...], wo[...]).astype(BF16)
    links.load("wo", "wcq")
    links.ready("qa2", "mem")
    links.tick()
    attention_backward(qa, mem, 0, width, r["akc"], att, datt, dq, dmem, 0, width, acc, links.tick)
    links.load("qa", "qa1")
    links.load("att", "att1")
    links.load("packed")
    links.load("datt", "br1")
    links.ready("m2")
    grads(2, dq, m, width)
    links.load("m", "m1")
    grads(3, dmem, text, width)
    links.ready("wcq")
    tmp[...] = nn(dq[...], wo[...])
    links.load("wo", "wso")
    links.ready("xh2", "g", "br1")

    def middle(at):
        rows = pl.ds(at, TILE)
        own = owners_column(lens, at, TILE)
        s = stage[rows, :] + norm_back_tile(lens, at, own, mod, tmp[rows, :], xh, rs, 1, sums, width)
        stage[rows, :] = s
        gate_tile(lens, at, own, mod, s, datt, 0, sums, dq, width)

    tiles(frames, middle)
    links.load("xh", "xh1")
    links.ready("att1", "wso")
    links.tick()
    grads(1, dq, att, width)
    datt[...] = nn(dq[...], wo[...]).astype(BF16)
    links.load("wo", "tout")
    links.ready("qa1", "packed")
    links.drain_early()
    links.swap(4, 5)
    steps = iter((0, 1))
    attention_backward(qa, packed, width, 2 * width, r["aks"], att, datt, dpack, dpack, width, 2 * width, acc,
                       lambda: links.late(next(steps)))
    links.ready("m1", "wsp")
    grads(0, dpack, m, width)
    links.swap(6, 7)
    tmp[...] = nn(dpack[...], r["wsp"][...])
    links.late(2)
    links.ready("xh1")

    def last(at):
        rows = pl.ds(at, TILE)
        own = owners_column(lens, at, TILE)
        s = stage[rows, :] + norm_back_tile(lens, at, own, mod, tmp[rows, :], xh, rs, 0, sums, width)
        stage[rows, :] = pick(own, keep[0], keep[1], keep[2]) * s

    tiles(frames, last)
    links.send_sums(sums)
    links.save(stage, "latents")
    pre1, pre2 = tmp.at[pl.ds(0, r["in_pre1"].shape[0])], tmp.at[pl.ds(r["in_pre1"].shape[0], r["in_pre1"].shape[0])]
    links.load("pre2", to=pre2)
    links.load("pre1", to=pre1)
    links.late(3)
    links.ready("pre2")
    links.condition_back(pre2)
    links.late(4)
    links.condition_spread()
    links.late(5)
    links.ready("pre1", "tout")
    links.time_back(pre1, pre2, wo)
    for t in range(6, len(SUM_GROUPS) - EARLY + 3):
        links.late(t)


def reduce_backward(mesh, lens, tlens, keep, small, big, grads_ff, tables):
    ndp, ncore = mesh.shape["dp"], mesh.shape["fsdp"]
    depth, total = ndp // 2, ndp * ncore
    d = big["wso"].shape[0]
    t = big["g"].shape[0]
    x = small["text"].shape[0]
    cols = (3 * d, d, d, 2 * d, d, grads_ff[0].shape[0], grads_ff[1].shape[0])
    rows_of = (d, d, d, d, d, grads_ff[0].shape[1], grads_ff[1].shape[1])
    shapes = [(c // ndp, rw // ncore) for c, rw in zip(cols, rows_of)]
    vm = lambda shape, kind=BF16: pltpu.VMEM(shape, kind)
    wide = HEADS * PAIR
    deep, mcols = small["modw"].shape
    padded = -(-(mcols // 2) // 128) * 128
    dpad = -(-deep // 128) * 128
    tin_rows, t_cols = FREQ // ncore, d // ndp
    scratch = dict(
        qa=vm((t, wide)), att=vm((t, d)), m=vm((t, d)), xh=vm((t, d)), wo=vm((d, d)), dq=vm((t, d)), datt=vm((t, d)),
        stage=vm((t, d), F32), tmp=vm((t, d), F32), packed=vm((t, 3 * d)), dpack=vm((t, 3 * d)), wsp=vm((3 * d, d)),
        acc=vm((PAIR, t), F32), aq=vm((t, PAIR)), aks=vm((t, PAIR)), akc=vm((x, PAIR)), sums=vm((16, 9 * d), F32),
        gs=vm((ndp, 8, padded), F32), ggot=vm((total, 8, padded), F32), ds=vm((ndp, ncore * 8, dpad), F32),
        dgot=vm((ndp, ncore * 8, dpad), F32), cgot=vm((total, ncore * 4, dpad)),
    )
    for w in range(5):
        c8, share = shapes[w]
        scratch[f"grad{w}"] = vm((depth, 2, c8, share * ncore))
    for w, (c8, share) in enumerate(shapes):
        scratch[f"final{w}"] = vm((c8 // 2, 2 * share), F32)
        scratch[f"part{w}"] = vm((c8 // 2, share), F32)
    dims = lambda u: unit_shape(u, shapes)
    size = {}
    for gi, g in enumerate(SUM_GROUPS):
        early = gi < EARLY
        for k, u in enumerate(g):
            _, _, n, _, nl, route, _ = dims(u)
            key = (gi - (0 if early else EARLY), k)
            size.setdefault(key, {})[early] = (n, nl, route)
    slot_names = {}
    for (gi, k), kinds in size.items():
        same = len(kinds) == 2 and kinds[True] == kinds[False]
        for early, (n, nl, route) in kinds.items():
            tag = f"slot{gi}_{k}" + ("" if same else ("e" if early else "l"))
            slot_names[(gi + (0 if early else EARLY), k)] = tag
            if tag + "a" not in scratch:
                scratch[tag + "a"] = vm((2, depth, 2, n, nl))
                scratch[tag + "b"] = vm((depth, 2, n, nl) if route == 0 else (2, depth, n, nl))
                scratch[tag + "c"] = vm((depth, n, nl))
                scratch[tag + "d"] = vm((depth - 1, n, nl))
    for gi in range(EARLY):
        for k, u in enumerate(SUM_GROUPS[gi]):
            _, _, n, _, nl, _, _ = dims(u)
            scratch[f"own{gi % 2}_{k}"] = vm((2, depth, 2, n, nl))
    ns = sum(len(g) * (4 + 2 + depth - 1) for g in SUM_GROUPS) + len(shapes) + 2 * (total - 1) + ndp + 40
    scratch.update(send=pltpu.SemaphoreType.DMA((ns,)), recv=pltpu.SemaphoreType.DMA((ns,)), free=pltpu.SemaphoreType.REGULAR)
    names = list(scratch)
    small_names, big_names = list(small), list(big)
    outs = dict(latents=((t, d), F32), mg=((deep, mcols), F32), tig=((tin_rows, t_cols), F32), tog=((d // ncore, t_cols), F32))

    def kernel(*refs):
        lens, tlens, keep = refs[:3]
        at = 3
        r = {}
        for n in small_names:
            r["sums_in" if n == "sums" else n] = refs[at]
            at += 1
        for n in big_names:
            r["in_" + n] = refs[at]
            at += 1
        ff = refs[at : at + 2]
        at += 2
        r["out_latents"] = refs[at]
        r["mg"], r["tig"], r["tog"] = refs[at + 1 : at + 4]
        at += 4
        r["shares"] = refs[at : at + len(shapes)]
        at += len(shapes)
        r.update(zip(names, refs[at:]))
        r["grads"] = [r[f"grad{w}"] for w in range(5)] + list(ff)
        r["final"] = [r[f"final{w}"] for w in range(len(shapes))]
        r["part"] = [r[f"part{w}"] for w in range(len(shapes))]
        r["sums"][...] = r["sums_in"][...]

        def flat(w, left, right, width):
            out = r[f"grad{w}"]
            c8 = shapes[w][0]
            per = ndp
            while per % 2 == 0 and per // 2 * c8 >= width and per // 2 * c8 % 128 == 0:
                per //= 2

            def step(i, carry):
                cols = pl.ds(pl.multiple_of(i * per * c8, per * c8), per * c8)
                value = tn(left[:, cols], right[...]).astype(BF16)
                for k in range(per):
                    b = i * per + k
                    out[b // 2, b % 2] = value[k * c8 : (k + 1) * c8, :]
                return carry

            lax.fori_loop(0, ndp // per, step, 0)

        r["flat"] = flat
        tagged = {}
        for (gi, k), tag in slot_names.items():
            tagged[(gi, k)] = [r[tag + e] for e in "abcd"]
        r["slot_of"] = tagged
        links = BackwardLinks(mesh, shapes, r)
        backward_linked(links, r, lens, tlens, keep, r["mod"], r["text"], r["rs"], r["sums"])
        links.finish()

    got = pl.pallas_call(
        kernel,
        out_shape=[sds(*outs[n]) for n in outs] + [sds(s, F32) for s in shapes],
        in_specs=[SM] * 3 + [VM] * len(small) + [ANY] * (len(big) + 2),
        out_specs=[ANY] + [VM] * (3 + len(shapes)),
        scratch_shapes=list(scratch.values()),
        cost_estimate=pl.CostEstimate(flops=int(6e10), bytes_accessed=int(8e7), transcendentals=0),
        compiler_params=pltpu.CompilerParams(collective_id=1, has_side_effects=True, vmem_limit_bytes=63 * MIB),
    )(lens, tlens, keep, *small.values(), *big.values(),
      *[g.reshape(depth, 2, shapes[5 + k][0], g.shape[1]) for k, g in enumerate(grads_ff)])
    turned = pl.pallas_call(
        partial(turn_body, len(shapes)),
        out_shape=[sds(s[::-1], F32) for s in shapes],
        in_specs=[VM] * len(shapes),
        out_specs=[VM] * len(shapes),
    )(*got[4:])
    return got[:4], turned


def turn_body(nw, *refs):
    for w in range(nw):
        refs[nw + w][...] = refs[w][...].T


HIGHEST = lax.Precision.HIGHEST
BOTH = ("dp", "fsdp")


def high_dot(left, right, lc=1, rc=0):
    return lax.dot_general(left, right, (((lc,), (rc,)), ((), ())), precision=HIGHEST, preferred_element_type=F32)


def plan(step_row):
    levels = step_row.astype(F32)
    cumulative = jnp.cos(0.5 * math.pi * (levels / 1000.0 + 0.008) / 1.008) ** 2
    half_width = FREQ // 2
    frequency = jnp.exp(-math.log(10000.0) * jnp.arange(half_width, dtype=F32) / half_width)
    angles = levels[:, None] * frequency[None, :]
    embedding = jnp.concatenate([jnp.cos(angles), jnp.sin(angles)], axis=1)
    return jnp.sqrt(cumulative), jnp.sqrt(1.0 - cumulative), embedding


def silu_slope(v):
    s = jax.nn.sigmoid(v)
    return s * (1.0 + v * (1.0 - s))


def plain_gather(w):
    part = lax.all_gather(w, "fsdp", axis=0, tiled=True)
    return lax.all_gather(part, "dp", axis=1, tiled=True).T


def plain_reduce(g):
    part = lax.psum_scatter(g.T, "dp", scatter_dimension=1, tiled=True).astype(BF16)
    return lax.psum_scatter(part, "fsdp", scatter_dimension=0, tiled=True).astype(F32)


def fits(mesh, frames, weights):
    if mesh.shape["fsdp"] != 4 or mesh.shape["dp"] % 2:
        return False
    if mesh.shape["dp"] * mesh.shape["fsdp"] * 16 > frames:
        return False
    return all(w.shape[0] * 2 % 128 == 0 and w.shape[1] % 32 == 0 for w in weights)


def columns(values, index, width):
    return lax.dynamic_slice_in_dim(values, index * width, width, axis=1)


def body(mesh, latents, noise_draw, text_states, time_steps, item_lengths, text_lengths, cotangent, time_in, time_out,
         modulation, *others):
    ndp, nfs = mesh.shape["dp"], mesh.shape["fsdp"]
    i, j = lax.axis_index("dp"), lax.axis_index("fsdp")
    width = latents.shape[1]
    items = time_steps.shape[0]
    sent = (time_in, time_out) + others
    direct = fits(mesh, latents.shape[0], sent)
    text = text_states.reshape(-1, width)
    keep, loud, embedding = plan(time_steps)
    deep, wide = modulation.shape
    if direct:
        embedding = jnp.pad(embedding, ((0, 8 - items), (0, 0)))
        full, saved = gather_forward(mesh, item_lengths, text_lengths, keep, loud, embedding, latents, noise_draw, text,
                                     modulation, sent)
        mod = saved["mod"]
        first = [saved[n] for n in SAVED[4:]]
        weights = full[2:]
        second = run_ff(item_lengths, mod, first[0], *weights[5:])
        g, b2, dwd, dwu, sums = run_ff_back(item_lengths, mod, cotangent, saved["br2"], second, *weights[5:])
        small = dict(mod=mod, text=text, rs=saved["rs"], sums=sums, modw=modulation, eall=saved["eall"])
        big = {n: saved[n] for n in ("att2", "qa2", "mem", "m2", "xh2", "qa1", "att1", "packed", "br1", "m1", "xh1", "pre1", "pre2")}
        big.update(b2=b2, g=g, wsp=weights[0], wso=weights[1], wcq=weights[2], wco=weights[4], tout=full[1])
        (lat_grad, modulation_grad, time_in_grad, time_out_grad), shares = reduce_backward(
            mesh, item_lengths, text_lengths, keep, small, big, (dwu, dwd), None)
        return (second[5], lat_grad, time_in_grad, time_out_grad, modulation_grad, *shares)
    full = [plain_gather(w) for w in sent]
    t_in, t_out = full[0].astype(F32), full[1].astype(F32)
    embedding = lax.all_gather(embedding, BOTH, axis=0, tiled=True)
    pre_one = high_dot(embedding, t_in, 1, 1)
    hidden = jax.nn.silu(pre_one)
    pre_two = high_dot(hidden, t_out, 1, 1)
    mine = columns(jax.nn.silu(pre_two).astype(BF16), j, deep)
    part = jnp.dot(mine, modulation, preferred_element_type=F32).reshape(ndp, nfs * items, wide)
    part = lax.psum_scatter(part, "fsdp", scatter_dimension=1, tiled=True)
    rows = lax.all_to_all(part, "dp", 0, 0, tiled=True)
    mod = jnp.pad(rows.transpose(1, 0, 2).reshape(items, -1), ((0, 8 - items), (0, 0)))
    first = run_attention(item_lengths, text_lengths, keep, loud, mod, latents, noise_draw, text, *full[2:7])
    weights = full[2:]
    second = run_ff(item_lengths, mod, first[0], *weights[5:])
    out, lat_grad, *grads, sums = run_backward(item_lengths, text_lengths, keep, mod, text, cotangent, first, second, *weights)
    shares = [plain_reduce(g) for g in grads]

    sent_sums = sums[:items].astype(BF16).reshape(items, ndp, wide).transpose(1, 0, 2)
    got = lax.all_to_all(sent_sums, "dp", 0, 0, tiled=True)
    got = lax.all_gather(got, "fsdp", axis=1, tiled=True).reshape(-1, wide)
    modulation_grad = lax.dot_general(mine, got, (((0,), (0,)), ((), ())), preferred_element_type=F32)
    back = lax.dot_general(got, modulation, (((1,), (1,)), ((), ())), preferred_element_type=F32)
    back = lax.all_gather(lax.psum(back, "dp"), "fsdp", axis=1, tiled=True)
    back_two = back * silu_slope(pre_two)
    back_one = high_dot(back_two, t_out) * silu_slope(pre_one)
    time_in_grad = high_dot(columns(embedding, j, time_in.shape[0]), columns(back_one, i, time_in.shape[1]), 0, 0)
    time_out_grad = high_dot(columns(hidden, j, time_out.shape[0]), columns(back_two, i, time_out.shape[1]), 0, 0)
    return (out, lat_grad, time_in_grad, time_out_grad, modulation_grad, *shares)


def solution(mesh):
    rows, weight = P(BOTH, None), P("fsdp", "dp")
    return jax.shard_map(
        partial(body, mesh),
        mesh=mesh,
        in_specs=(rows, rows, P(BOTH, None, None), P(BOTH), rows, P(BOTH), rows) + (weight,) * 10,
        out_specs=(rows, rows) + (weight,) * 10,
        check_vma=False,
    )
```

```python
from functools import partial
import math

import jax
import jax.numpy as jnp
from jax import lax
from jax.experimental import pallas as pl
from jax.experimental.pallas import tpu as pltpu
from jax.sharding import PartitionSpec as P

F32, BF16 = jnp.float32, jnp.bfloat16
HEADS = 12
FREQ = 256
HD = 64
FACTOR = float(HD) ** -0.5
PAIR = 2 * HD
PAIRS = HEADS // 2
BIG = 1e30
TILE = 256
MIB = 2**20


def dot(left, right, lc, rc):
    return lax.dot_general(left, right, (((lc,), (rc,)), ((), ())), preferred_element_type=F32)


def nt(left, right):
    return dot(left, right, 1, 1)


def nn(left, right):
    return dot(left, right, 1, 0)


def tn(left, right):
    return dot(left, right, 0, 0)


def owners_column(lens, first, rows):
    place = lax.broadcasted_iota(jnp.int32, (rows, 1), 0) + first
    end = lens[0, 0]
    return (place >= end).astype(jnp.int32) + (place >= end + lens[0, 1]).astype(jnp.int32)


def owners_row(lens, cols):
    place = lax.broadcasted_iota(jnp.int32, (1, cols), 1)
    end = lens[0, 0]
    return (place >= end).astype(jnp.int32) + (place >= end + lens[0, 1]).astype(jnp.int32)


def pick(own, a, b, c):
    return jnp.where(own == 0, a, jnp.where(own == 1, b, c))


def expand(own, mod, block, width):
    lo = block * width
    return pick(own, mod[0:1, lo : lo + width], mod[1:2, lo : lo + width], mod[2:3, lo : lo + width])


def item_sums(lens, first, rows, values):
    items = lax.broadcasted_iota(jnp.int32, (16, rows), 0)
    place = lax.broadcasted_iota(jnp.int32, (16, rows), 1) + first
    end = lens[0, 0]
    own = (place >= end).astype(jnp.int32) + (place >= end + lens[0, 1]).astype(jnp.int32)
    member = jnp.where(items == own, 1.0, 0.0).astype(BF16)
    return nn(member, values.astype(BF16))


def fill_masks(lens, tlens, aq, aks, akc):
    rows = aq.shape[0]
    lane = lax.broadcasted_iota(jnp.int32, (rows, PAIR), 1) % HD
    own = owners_column(lens, 0, rows)
    aq[...] = jnp.where(own == lane, 1.0, 0.0).astype(BF16)
    minus = jnp.where((lane >= 3) & (lane < 6), -1.0, 0.0)
    aks[...] = jnp.where((lane < 3) & (own != lane), -BIG, minus).astype(BF16)
    slots = akc.shape[0]
    text = slots // 3
    lane = lax.broadcasted_iota(jnp.int32, (slots, PAIR), 1) % HD
    minus = jnp.where((lane >= 3) & (lane < 6), -1.0, 0.0)
    slot = lax.broadcasted_iota(jnp.int32, (slots, 1), 0)
    item = (slot >= text).astype(jnp.int32) + (slot >= 2 * text).astype(jnp.int32)
    live = slot - item * text < pick(item, tlens[0], tlens[1], tlens[2])
    akc[...] = jnp.where((lane < 3) & ((item != lane) | ~live), -BIG, minus).astype(BF16)


def pieces(column):
    one = column.astype(BF16).astype(F32)
    two = (column - one).astype(BF16).astype(F32)
    return one, two, column - one - two


def in_parts(pair, pump, step=3):
    if pump is None:
        lax.fori_loop(0, PAIRS, pair, 0)
        return
    for first in range(0, PAIRS, step):
        lax.fori_loop(first, first + step, pair, 0)
        pump()


def attention_forward(q, k, k_at, v_at, ak, aq, out, qaug, pump=None):
    frames = q.shape[0]

    def pair(p, carry):
        lanes = pl.ds(pl.multiple_of(p * PAIR, PAIR), PAIR)
        kp = k[:, pl.ds(pl.multiple_of(k_at + p * PAIR, PAIR), PAIR)]
        vp = k[:, pl.ds(pl.multiple_of(v_at + p * PAIR, PAIR), PAIR)]
        klow = lax.broadcasted_iota(jnp.int32, kp.shape, 1) < HD
        keys = (jnp.where(klow, kp, ak[...]), jnp.where(klow, ak[...], kp))
        one = jnp.ones_like(vp)
        values = (jnp.where(klow, vp, one), jnp.where(klow, one, vp))
        lane = lax.broadcasted_iota(jnp.int32, (TILE, PAIR), 1)
        low, inner = lane < HD, lane % HD
        for t in range(frames // TILE):
            rows = pl.ds(t * TILE, TILE)
            qp = q[rows, lanes] * jnp.asarray(FACTOR, BF16)
            mark = aq[rows, :]
            done = []
            for h in range(2):
                own = low if h == 0 else ~low
                qh = jnp.where(own, qp, mark)
                s = nt(qh, keys[h])
                top = jnp.max(s, axis=1, keepdims=True)
                e = jnp.exp(s - top).astype(BF16)
                o = nn(e, values[h])
                total = o[:, HD : HD + 1] if h == 0 else o[:, 0:1]
                done.append(o * (1.0 / total))
                a, b, c = pieces(top + jnp.log(total))
                extra = jnp.where(inner == 3, a, jnp.where(inner == 4, b, c))
                extra = jnp.where((inner >= 3) & (inner < 6), extra, mark.astype(F32)).astype(BF16)
                at = pl.ds(pl.multiple_of((2 * p + h) * PAIR, PAIR), PAIR)
                qaug[rows, at] = jnp.where(own, qp, extra)
            out[rows, lanes] = jnp.where(low, done[0], done[1]).astype(BF16)
        return carry

    in_parts(pair, pump)


def attention_backward(qaug, k, k_at, v_at, ak, att, datt, dq, dk, dk_at, dv_at, acc, pump=None, step_pairs=3):
    frames = att.shape[0]
    tall = k.shape[0]
    step = TILE if tall % TILE == 0 else PAIR

    def pair(p, carry):
        lanes = pl.ds(pl.multiple_of(p * PAIR, PAIR), PAIR)
        lane = lax.broadcasted_iota(jnp.int32, (frames, PAIR), 1)
        low, inner = lane < HD, lane % HD
        do = datt[:, lanes]
        both = do.astype(F32) * att[:, lanes].astype(F32)
        outs, queries = [], []
        for h in range(2):
            own = low if h == 0 else ~low
            a, b, c = pieces(jnp.sum(jnp.where(own, both, 0.0), axis=1, keepdims=True))
            extra = jnp.where(inner == 3, a, jnp.where(inner == 4, b, c))
            extra = jnp.where((inner >= 3) & (inner < 6), extra, 0.0).astype(BF16)
            outs.append(jnp.where(own, do, extra))
            queries.append(qaug[:, pl.ds(pl.multiple_of((2 * p + h) * PAIR, PAIR), PAIR)])
        for t in range(tall // step):
            rows = pl.ds(t * step, step)
            kp = k[rows, pl.ds(pl.multiple_of(k_at + p * PAIR, PAIR), PAIR)]
            vp = k[rows, pl.ds(pl.multiple_of(v_at + p * PAIR, PAIR), PAIR)]
            mark = ak[rows, :]
            klow = lax.broadcasted_iota(jnp.int32, kp.shape, 1) < HD
            kt = kp.T
            dks, dvs = [], []
            for h in range(2):
                own = klow if h == 0 else ~klow
                pt = jnp.exp(nt(jnp.where(own, kp, mark), queries[h]))
                dpt = nt(jnp.where(own, vp, mark), outs[h])
                dst = (pt * dpt).astype(BF16)
                dvs.append(nn(pt.astype(BF16), do))
                dks.append(nn(dst, queries[h]))
                part = nn(kt[h * HD : (h + 1) * HD, :], dst)
                at = pl.ds(h * HD, HD)
                if t == 0:
                    acc[at, :] = part
                else:
                    acc[at, :] += part
            dk[rows, pl.ds(pl.multiple_of(dk_at + p * PAIR, PAIR), PAIR)] = jnp.where(klow, dks[0], dks[1]).astype(BF16)
            dk[rows, pl.ds(pl.multiple_of(dv_at + p * PAIR, PAIR), PAIR)] = jnp.where(klow, dvs[0], dvs[1]).astype(BF16)
        dq[:, lanes] = (acc[...].T * FACTOR).astype(BF16)
        return carry

    in_parts(pair, pump, step_pairs)


def norm_tile(s):
    width = s.shape[1]
    center = s - jnp.sum(s, axis=1, keepdims=True) * (1.0 / width)
    spread = jnp.sum(center * center, axis=1, keepdims=True) * (1.0 / width)
    rs = lax.rsqrt(spread + 1e-06)
    return center * rs, rs


def tiles(count, fn):
    def step(i, carry):
        fn(pl.multiple_of(i * TILE, TILE))
        return carry

    lax.fori_loop(0, count // TILE, step, 0)


def big_nt(left, right, out, width):
    def step(n, carry):
        cols = pl.ds(pl.multiple_of(n * width, width), width)
        out[:, cols] = nt(left[...], right[cols, :]).astype(BF16)
        return carry

    lax.fori_loop(0, right.shape[0] // width, step, 0)


def big_tn(left, right, out, width):
    def step(n, carry):
        cols = pl.ds(pl.multiple_of(n * width, width), width)
        out[cols, :] = tn(left[:, cols], right[...]).astype(BF16)
        return carry

    lax.fori_loop(0, left.shape[1] // width, step, 0)


def norm_into(s, rows, own, lens, mod, sub, xh, m, rs, width):
    hat, r = norm_tile(s)
    xh[rows, :] = hat.astype(BF16)
    base = 3 * sub
    m[rows, :] = (hat * (1.0 + expand(own, mod, base + 1, width)) + expand(own, mod, base, width)).astype(BF16)
    lane = lax.broadcasted_iota(jnp.int32, (TILE, 128), 1)
    rs[rows, :] = jnp.where(lane == sub, r, rs[rows, :])


class NoLinks:
    pump = None

    def use(self, *names):
        pass

    def fetch(self, *names):
        pass

    def tick(self, n=1):
        pass

    def modulation(self):
        pass

    def done(self, *names):
        pass


def forward_attention(links, lens, tlens, keep, loud, mod, lat, noi, text, wsp, wso, wcq, wcm, wco,
                      stream, xh1, m1, packed, qa1, att1, br1, xh2, m2, mem, qa2, att2, br2, rs,
                      aq, aks, akc, qb, tmp):
    frames, width = lat.shape
    fill_masks(lens, tlens, aq, aks, akc)
    rs[...] = jnp.zeros_like(rs)
    links.modulation()

    def start(at):
        rows = pl.ds(at, TILE)
        own = owners_column(lens, at, TILE)
        s = pick(own, keep[0], keep[1], keep[2]) * lat[rows, :].astype(F32)
        s = s + pick(own, loud[0], loud[1], loud[2]) * noi[rows, :].astype(F32)
        stream[rows, :] = s
        norm_into(s, rows, own, lens, mod, 0, xh1, m1, rs, width)

    tiles(frames, start)
    links.done("xh1", "m1")
    links.use("wsp")
    big_nt(m1, wsp, packed, width)
    links.done("packed")
    links.tick()
    attention_forward(packed, packed, width, 2 * width, aks, aq, att1, qa1, links.pump)
    links.done("att1", "qa1")
    links.use("wso")
    tmp[...] = nt(att1[...], wso[...])

    def middle(at):
        rows = pl.ds(at, TILE)
        own = owners_column(lens, at, TILE)
        br = tmp[rows, :]
        br1[rows, :] = br.astype(BF16)
        s = stream[rows, :] + expand(own, mod, 2, width) * br
        stream[rows, :] = s
        norm_into(s, rows, own, lens, mod, 1, xh2, m2, rs, width)

    tiles(frames, middle)
    links.done("br1", "xh2", "m2")
    links.use("wcq", "wcm")
    big_nt(m2, wcq, qb, width)
    big_nt(text, wcm, mem, width)
    links.done("mem")
    attention_forward(qb, mem, 0, width, akc, aq, att2, qa2, links.pump)
    links.done("att2", "qa2")
    links.use("wco")
    tmp[...] = nt(att2[...], wco[...])

    def last(at):
        rows = pl.ds(at, TILE)
        own = owners_column(lens, at, TILE)
        br = tmp[rows, :]
        br2[rows, :] = br.astype(BF16)
        stream[rows, :] = stream[rows, :] + expand(own, mod, 5, width) * br

    tiles(frames, last)
    links.done("br2")


GELU_A, GELU_B = math.sqrt(2.0 / math.pi), 0.044715


def gelu_tile(x, rows, act, slope):
    sq = x * x
    t = jnp.tanh(x * (GELU_A + GELU_A * GELU_B * sq))
    half = 0.5 + 0.5 * t
    act[rows, :] = (x * half).astype(BF16)
    slope[rows, :] = (half + half * (1.0 - t) * x * (GELU_A + 3.0 * GELU_A * GELU_B * sq)).astype(BF16)


def forward_ff(lens, mod, stream, wup, wdn, xh3, m3, act, slope, br3, out, rs, tmp):
    frames, width = stream.shape
    rs[...] = jnp.zeros_like(rs)

    def start(at):
        rows = pl.ds(at, TILE)
        own = owners_column(lens, at, TILE)
        norm_into(stream[rows, :], rows, own, lens, mod, 2, xh3, m3, rs, width)

    tiles(frames, start)

    def chunk(n, carry):
        cols = pl.ds(pl.multiple_of(n * width, width), width)
        tmp[...] = nt(m3[...], wup[cols, :])

        def gelu(at):
            rows = pl.ds(at, TILE)
            gelu_tile(tmp[rows, :], rows, act.at[:, cols], slope.at[:, cols])

        tiles(frames, gelu)
        return carry

    lax.fori_loop(0, wup.shape[0] // width, chunk, 0)
    tmp[...] = nt(act[...], wdn[...])

    def last(at):
        rows = pl.ds(at, TILE)
        own = owners_column(lens, at, TILE)
        br = tmp[rows, :]
        br3[rows, :] = br.astype(BF16)
        out[rows, :] = (stream[rows, :] + expand(own, mod, 8, width) * br).astype(BF16)

    tiles(frames, last)


def norm_back(dm, hat, r, stretch):
    width = dm.shape[1]
    dh = dm * (1.0 + stretch)
    a = jnp.sum(dh, axis=1, keepdims=True) * (1.0 / width)
    b = jnp.sum(dh * hat, axis=1, keepdims=True) * (1.0 / width)
    return r * (dh - a - hat * b)


def add_sums(lens, at, sums, cols, values):
    sums[:, cols] += item_sums(lens, at, TILE, values)


def gate_tile(lens, at, own, mod, g, br, sub, sums, b, width):
    rows = pl.ds(at, TILE)
    add_sums(lens, at, sums, pl.ds((3 * sub + 2) * width, width), g * br[rows, :].astype(F32))
    b[rows, :] = (expand(own, mod, 3 * sub + 2, width) * g).astype(BF16)


def norm_back_tile(lens, at, own, mod, dm, xh, rs, sub, sums, width):
    rows = pl.ds(at, TILE)
    hat = xh[rows, :].astype(F32)
    add_sums(lens, at, sums, pl.ds(3 * sub * width, width), dm)
    add_sums(lens, at, sums, pl.ds((3 * sub + 1) * width, width), dm * hat)
    return norm_back(dm, hat, rs[rows, sub : sub + 1], expand(own, mod, 3 * sub + 1, width))


def backward_ff(lens, mod, cot, br3, act, slope, xh3, m3, rs, wup, wdn, g, b2, br2, dwd, dwu, sums, b3, ig, tmp):
    frames, width = cot.shape
    sums[...] = jnp.zeros_like(sums)

    def start(at):
        rows = pl.ds(at, TILE)
        own = owners_column(lens, at, TILE)
        gate_tile(lens, at, own, mod, cot[rows, :].astype(F32), br3, 2, sums, b3, width)

    tiles(frames, start)

    def chunk(n, carry):
        cols = pl.ds(pl.multiple_of(n * width, width), width)
        dwd[:, cols] = tn(b3[...], act[:, cols]).astype(BF16)
        ig[:, cols] = (nn(b3[...], wdn[:, cols]) * slope[:, cols].astype(F32)).astype(BF16)
        dwu[cols, :] = tn(ig[:, cols], m3[...]).astype(BF16)
        return carry

    lax.fori_loop(0, wup.shape[0] // width, chunk, 0)
    tmp[...] = nn(ig[...], wup[...])

    def last(at):
        rows = pl.ds(at, TILE)
        own = owners_column(lens, at, TILE)
        s = cot[rows, :].astype(F32) + norm_back_tile(lens, at, own, mod, tmp[rows, :], xh3, rs, 2, sums, width)
        g[rows, :] = s
        gate_tile(lens, at, own, mod, s, br2, 1, sums, b2, width)

    tiles(frames, last)


def backward_attention(lens, tlens, keep, mod, text, g, b2, xh1, m1, packed, qa1, att1, br1, xh2, m2, mem, qa2, att2, rs,
                       wsp, wso, wcq, wcm, wco, sums_in,
                       lat_grad, dsp, dso, dcq, dcm, dco, sums,
                       aq, aks, akc, datt, dq, dmem, dpack, acc, tmp, stage):
    frames, width = g.shape
    fill_masks(lens, tlens, aq, aks, akc)
    sums[...] = sums_in[...]
    big_tn(b2, att2, dco, width)
    datt[...] = nn(b2[...], wco[...]).astype(BF16)
    attention_backward(qa2, mem, 0, width, akc, att2, datt, dq, dmem, 0, width, acc)
    big_tn(dq, m2, dcq, width)
    big_tn(dmem, text, dcm, width)
    tmp[...] = nn(dq[...], wcq[...])

    def middle(at):
        rows = pl.ds(at, TILE)
        own = owners_column(lens, at, TILE)
        s = g[rows, :] + norm_back_tile(lens, at, own, mod, tmp[rows, :], xh2, rs, 1, sums, width)
        stage[rows, :] = s
        gate_tile(lens, at, own, mod, s, br1, 0, sums, dq, width)

    tiles(frames, middle)
    big_tn(dq, att1, dso, width)
    datt[...] = nn(dq[...], wso[...]).astype(BF16)
    attention_backward(qa1, packed, width, 2 * width, aks, att1, datt, dpack, dpack, width, 2 * width, acc)
    big_tn(dpack, m1, dsp, width)
    tmp[...] = nn(dpack[...], wsp[...])

    def last(at):
        rows = pl.ds(at, TILE)
        own = owners_column(lens, at, TILE)
        s = stage[rows, :] + norm_back_tile(lens, at, own, mod, tmp[rows, :], xh1, rs, 0, sums, width)
        lat_grad[rows, :] = pick(own, keep[0], keep[1], keep[2]) * s

    tiles(frames, last)


def sds(shape, kind=BF16):
    return jax.ShapeDtypeStruct(shape, kind)


VM = pl.BlockSpec(memory_space=pltpu.VMEM)
SM = pl.BlockSpec(memory_space=pltpu.SMEM)


def call(body, scalars, ins, outs, scratch, flops):
    cost = pl.CostEstimate(flops=int(flops), bytes_accessed=int(3e7), transcendentals=0)
    return pl.pallas_call(
        body,
        out_shape=outs,
        in_specs=[SM] * len(scalars) + [VM] * len(ins),
        out_specs=[VM] * len(outs),
        scratch_shapes=scratch,
        cost_estimate=cost,
        compiler_params=pltpu.CompilerParams(vmem_limit_bytes=62 * MIB),
    )(*scalars, *ins)


def run_attention(lens, tlens, keep, loud, mod, lat, noi, text, wsp, wso, wcq, wcm, wco):
    t, d = lat.shape
    x = text.shape[0]
    wide = HEADS * PAIR
    return call(partial(forward_attention, NoLinks()), (lens, tlens, keep, loud),
                (mod, lat, noi, text, wsp, wso, wcq, wcm, wco),
                [sds((t, d), F32), sds((t, d)), sds((t, d)), sds((t, 3 * d)), sds((t, wide)), sds((t, d)), sds((t, d)),
                 sds((t, d)), sds((t, d)), sds((x, 2 * d)), sds((t, wide)), sds((t, d)), sds((t, d)), sds((t, 128), F32)],
                [pltpu.VMEM((t, PAIR), BF16), pltpu.VMEM((t, PAIR), BF16), pltpu.VMEM((x, PAIR), BF16),
                 pltpu.VMEM((t, d), BF16), pltpu.VMEM((t, d), F32)], 3e10)


def run_ff(lens, mod, stream, wup, wdn):
    t, d = stream.shape
    ff = wup.shape[0]
    return call(forward_ff, (lens,), (mod, stream, wup, wdn),
                [sds((t, d)), sds((t, d)), sds((t, ff)), sds((t, ff)), sds((t, d)), sds((t, d)), sds((t, 128), F32)],
                [pltpu.VMEM((t, d), F32)], 1e10)


def run_ff_back(lens, mod, cot, br2, kept, wup, wdn):
    t, d = cot.shape
    xh3, m3, act, slope, br3, out, rs3 = kept
    ff = wup.shape[0]

    def kernel(lens, mod, cot, br3, act, slope, xh3, m3, rs, wup, wdn, br2, g, b2, dwd, dwu, sums, b3, ig, tmp):
        backward_ff(lens, mod, cot, br3, act, slope, xh3, m3, rs, wup, wdn, g, b2, br2, dwd, dwu, sums, b3, ig, tmp)

    return call(kernel, (lens,), (mod, cot, br3, act, slope, xh3, m3, rs3, wup, wdn, br2),
                [sds((t, d), F32), sds((t, d)), sds((d, ff)), sds((ff, d)), sds((16, 9 * d), F32)],
                [pltpu.VMEM((t, d), BF16), pltpu.VMEM((t, ff), BF16), pltpu.VMEM((t, d), F32)], 3e10)


def run_backward(lens, tlens, keep, mod, text, cot, a, b, wsp, wso, wcq, wcm, wco, wup, wdn):
    t, d = cot.shape
    x = text.shape[0]
    stream, xh1, m1, packed, qa1, att1, br1, xh2, m2, mem, qa2, att2, br2, rs = a
    out = b[5]
    g, b2, dwd, dwu, sums = run_ff_back(lens, mod, cot, br2, b, wup, wdn)
    lat_grad, dsp, dso, dcq, dcm, dco, sums = call(
        backward_attention, (lens, tlens, keep),
        (mod, text, g, b2, xh1, m1, packed, qa1, att1, br1, xh2, m2, mem, qa2, att2, rs, wsp, wso, wcq, wcm, wco, sums),
        [sds((t, d), F32), sds((3 * d, d)), sds((d, d)), sds((d, d)), sds((2 * d, d)), sds((d, d)), sds((16, 9 * d), F32)],
        [pltpu.VMEM((t, PAIR), BF16), pltpu.VMEM((t, PAIR), BF16), pltpu.VMEM((x, PAIR), BF16),
         pltpu.VMEM((t, d), BF16), pltpu.VMEM((t, d), BF16), pltpu.VMEM((x, 2 * d), BF16), pltpu.VMEM((t, 3 * d), BF16),
         pltpu.VMEM((PAIR, t), F32), pltpu.VMEM((t, d), F32), pltpu.VMEM((t, d), F32)], 6e10)
    return out, lat_grad, dsp, dso, dcq, dcm, dco, dwu, dwd, sums

MESH = pl.DeviceIdType.MESH
ANY = pl.BlockSpec(memory_space=pl.ANY)
GROUPS = (
    ((0, 0, 1, 0, 2, 0), (1, 0, 1 / 3, 0, 2, 0), (1, 1 / 3, 2 / 3, 0, 2, 1)),
    ((2, 0, 5 / 9, 0, 2, 0), (2, 5 / 9, 4 / 9, 0, 2, 1)),
    ((3, 0, 1, 0, 2, 1), (4, 0, 1, 0, 2, 0)),
    ((5, 0, 1 / 2, 0, 2, 0), (5, 1 / 2, 1 / 2, 0, 2, 1)),
    ((6, 0, 1 / 3, 0, 2, 0), (6, 1 / 3, 2 / 3, 0, 2, 1)),
    ((7, 0, 1 / 4, 0, 2, 0), (7, 1 / 4, 1 / 4, 0, 2, 1)),
    ((7, 1 / 2, 1 / 4, 0, 2, 0), (7, 3 / 4, 1 / 4, 0, 2, 1)),
    ((8, 0, 1 / 3, 0, 2, 0), (8, 1 / 3, 1 / 3, 0, 2, 1)),
    ((8, 2 / 3, 1 / 3, 0, 1, 0), (8, 2 / 3, 1 / 3, 1, 1, 1)),
)
UNITS = tuple(u for g in GROUPS for u in g)


class Place:
    def __init__(self, depth):
        dp, fsdp = lax.axis_index("dp"), lax.axis_index("fsdp")
        self.depth = depth
        self.z, self.y = dp // 2, dp % 2
        self.x, self.c = fsdp // 2, fsdp % 2

    def at(self, z=None, y=None, x=None, c=None):
        z = self.z if z is None else z
        y = self.y if y is None else y
        x = self.x if x is None else x
        c = self.c if c is None else c
        return (z * 2 + y, x * 2 + c)

    def flat(self, ncore):
        return (self.z * 2 + self.y) * ncore + self.x * 2 + self.c

    def other_z(self, k):
        return lax.rem(self.z + k, self.depth)

    def greet(self, every):
        bar = pltpu.get_barrier_semaphore()
        for d in every:
            pl.semaphore_signal(bar, inc=1, device_id=d, device_id_type=MESH)

    def meet(self, count):
        pl.semaphore_wait(pltpu.get_barrier_semaphore(), count)


class Counter:
    def __init__(self, send, recv):
        self.send, self.recv, self.n = send, recv, 0

    def remote(self, src, dst, device):
        n, self.n = self.n, self.n + 1
        return pltpu.make_async_remote_copy(src_ref=src, dst_ref=dst, send_sem=self.send.at[n], recv_sem=self.recv.at[n],
                                            device_id=device, device_id_type=MESH)

    def local(self, src, dst):
        n, self.n = self.n, self.n + 1
        return pltpu.make_async_copy(src, dst, self.send.at[n])


def unit_shape(unit, shapes):
    w, r0, nr, l0, nl, route = unit
    c8, share = shapes[w]
    half = c8 // 2
    return w, round(half * r0), round(half * nr), round(l0 * share), round(nl * share), route, half


class GatherUnit:
    def __init__(self, unit, shapes, place, count, block, out):
        w, r0, n, l0, nl, route, half = unit_shape(unit, shapes)
        self.p, p = place, place
        self.route = route
        share = shapes[w][1]
        row = pl.ds(pl.multiple_of(p.c * half + r0, 16), n)
        other = pl.ds(pl.multiple_of((1 - p.c) * half + r0, 16), n)
        lane = lambda x: pl.ds(pl.multiple_of(x * (2 * share) + l0, 128), nl)
        own = block[w].at[pl.ds(r0, n), pl.ds(l0, nl)]
        o = out[w]
        mine, theirs = lane(p.x), lane(1 - p.x)
        D = p.depth
        dst = o.at[p.z, p.y, row, mine]
        self.local = count.local(own, dst)
        self.zs = [count.remote(own, dst, p.at(z=p.other_z(k))) for k in range(1, D)]
        self.second, self.third = [], []
        for k in range(D):
            zz = p.z if k == 0 else p.other_z(D - k)
            if route == 0:
                a = o.at[zz, p.y, row, mine]
                self.second.append(count.remote(own if k == 0 else a, a, p.at(y=1 - p.y)))
            else:
                a = o.at[zz, p.y, row, mine]
                self.second.append(count.remote(own if k == 0 else a, a, p.at(x=1 - p.x)))
        for k in range(D):
            zz = p.z if k == 0 else p.other_z(D - k)
            if route == 0:
                a = o.at[zz, :, row, mine]
                self.third.append(count.remote(a, a, p.at(x=1 - p.x)))
            else:
                lanes = pl.ds(l0, nl)
                a = [o.at[zz, p.y, row, lane(i)] for i in range(2)]
                self.third.append([count.remote(v, v, p.at(y=1 - p.y)) for v in a])
        sib = [o.at[:, :, row, lane(i)] for i in range(2)]
        self.sib = [count.remote(v, v, p.at(c=1 - p.c)) for v in sib]

    def flat(self, v):
        return v if isinstance(v, list) else [v]

    def begin(self):
        self.local.start()
        for cp in self.zs:
            cp.start()
        self.second[0].start()

    def step_z(self):
        for k, cp in enumerate(self.zs, 1):
            cp.wait_recv()
            self.second[k].start()
        self.local.wait()

    def step_second(self):
        for k, cp in enumerate(self.second):
            cp.wait_recv()
            for c in self.flat(self.third[k]):
                c.start()

    def step_third(self):
        for v in self.third:
            for c in self.flat(v):
                c.wait_recv()
        for c in self.sib:
            c.start()

    def settled(self):
        for c in self.sib:
            c.wait_recv()

    def finish(self):
        for c in self.sib + self.zs + self.second + [c for v in self.third for c in self.flat(v)]:
            c.wait_send()


def others(place, ndp, ncore):
    total = ndp * ncore
    me = place.flat(ncore)
    found = []
    for k in range(1, total):
        t = lax.rem(me + k, total)
        found.append((k, t, (t // ncore, t % ncore)))
    return found


def split_columns(values, index, parts, width):
    picked = values[:, :width]
    for i in range(1, parts):
        picked = jnp.where(index == i, values[:, i * width : (i + 1) * width], picked)
    return picked


def three(value):
    one = value.astype(BF16)
    rest = value - one.astype(F32)
    two = rest.astype(BF16)
    return one, two, (rest - two.astype(F32)).astype(BF16)


def fine_nt(left, right):
    a, b, c = three(left)
    return nt(a, right) + (nt(b, right) + nt(c, right))


def fine_nn(left, right):
    a, b, c = three(left)
    return nn(a, right) + (nn(b, right) + nn(c, right))


def silu(v):
    return v / (1.0 + jnp.exp(-v))


AHEAD = 2


class ForwardLinks:
    NAMES = ("tin", "tout", "wsp", "wso", "wcq", "wcm", "wco", "wup", "wdn")

    def __init__(self, mesh, shapes, r):
        self.ndp, self.ncore = mesh.shape["dp"], mesh.shape["fsdp"]
        self.shapes, self.r = shapes, r
        depth = self.ndp // 2
        self.p = p = Place(depth)
        self.count = count = Counter(r["send"], r["recv"])
        self.every = others(p, self.ndp, self.ncore)
        nw = len(shapes)
        turned, landed, block = r["turned"], r["landed"], r["block"]
        p.greet([d for _, _, d in self.every])
        for w in range(nw):
            turned[w][...] = r["shards"][w][...].T
        me = p.flat(self.ncore)
        r["eall"][me] = r["emb"][...]
        p.meet(len(self.every))
        self.spread = []
        swaps = []
        for w, (c8, share) in enumerate(shapes):
            half = c8 // 2
            theirs = turned[w].at[pl.ds(pl.multiple_of((1 - p.c) * half, 16), half), :]
            swaps.append(count.remote(theirs, landed[w], p.at(c=1 - p.c)))
            swaps[-1].start()
        for k, t, d in self.every:
            c = count.remote(r["eall"].at[me], r["eall"].at[me], d)
            c.start()
            self.spread.append(c)
        self.units = []
        for w, (c8, share) in enumerate(shapes):
            half = c8 // 2
            swaps[w].wait_recv()
            own = turned[w][pl.ds(pl.multiple_of(p.c * half, 16), half), :]
            got = landed[w][...]
            first = p.c == 0
            block[w][...] = jnp.concatenate([jnp.where(first, own, got), jnp.where(first, got, own)], axis=1)
        self.units = [[GatherUnit(u, shapes, p, count, block, r["full"]) for u in g] for g in GROUPS]
        self.swaps, self.begun = swaps, 0
        self.start(AHEAD)
        self.now, self.fetched, self.saves = 0, {}, {}
        self.pump = self.tick

    def start(self, upto):
        while self.begun < min(upto, len(self.units)):
            for u in self.units[self.begun]:
                u.begin()
            self.begun += 1

    def tick(self, n=1):
        for _ in range(n):
            t, self.now = self.now, self.now + 1
            n = len(self.units)
            self.start(t + AHEAD)
            if t < n:
                for u in self.units[t]:
                    u.step_z()
            if 0 <= t - 1 < n:
                for u in self.units[t - 1]:
                    u.step_second()
            if 0 <= t - 2 < n:
                for u in self.units[t - 2]:
                    u.step_third()

    def fetch(self, *names):
        for name in names:
            if name in self.fetched:
                continue
            w = self.NAMES.index(name)
            mine = [(i, k) for i, g in enumerate(GROUPS) for k, u in enumerate(g) if u[0] == w]
            while self.now - 3 < mine[-1][0]:
                self.tick()
            for i, k in mine:
                self.units[i][k].settled()
            self.fetched[name] = []
            for src, dst in self.places(name, w):
                c = self.count.local(src, dst)
                c.start()
                self.fetched[name].append(c)

    def places(self, name, w):
        r, c8 = self.r, self.shapes[w][0]
        found = []
        for z in range(self.p.depth):
            for y in range(2):
                b, src = 2 * z + y, r["full"][w].at[z, y]
                if name == "wup":
                    width = src.shape[1]
                    n, at = b * c8 // width, b * c8 % width
                    found.append((src, self.ups[n].at[pl.ds(at, c8), :]))
                elif name == "wdn":
                    for n, down in enumerate(self.downs):
                        width = down.shape[1]
                        found.append((src.at[:, pl.ds(n * width, width)], down.at[pl.ds(b * c8, c8), :]))
                else:
                    found.append((src, r[name].at[pl.ds(b * c8, c8), :]))
        return found

    def use(self, *names):
        self.fetch(*names)
        for name in names:
            for c in self.fetched[name]:
                c.wait()

    def modulation(self):
        r, p = self.r, self.p
        self.fetch("tin", "tout")
        for c in self.spread:
            c.wait_recv()
        self.use("tin", "tout")
        total = self.ndp * self.ncore
        rows = total * 8
        one = fine_nt(r["eall"][...].reshape(rows, FREQ), r["tin"][...])
        hidden = silu(one)
        two = fine_nt(hidden, r["tout"][...])
        r["pre1"][...] = one
        r["pre2"][...] = two
        cond = silu(two)
        deep, wide = r["modw"].shape
        part = wide // 2
        mine = split_columns(cond, p.x * 2 + p.c, self.ncore, deep)
        low = mine.astype(BF16)
        high = pltpu.roll(mine, 4, 0).astype(BF16)
        ready = nn(low, r["modw"][:, :part]) + nn(high, r["modw"][:, part:])
        pad = r["psend"].shape[2] - part
        r["psend"][...] = jnp.concatenate([ready, jnp.zeros((rows, pad), F32)], axis=1).reshape(total, 8, part + pad)
        me = p.flat(self.ncore)
        self.parts = []
        for k, t, d in self.every:
            c = self.count.remote(r["psend"].at[t], r["pgot"].at[me], d)
            c.start()
            self.parts.append(c)
        r["pgot"][me] = r["psend"][me]
        self.done("pre1", "pre2", "eall")
        self.tick(1)
        for c in self.parts:
            c.wait_recv()
        found = []
        for i in range(self.ndp):
            s = r["pgot"][i * self.ncore]
            for j in range(1, self.ncore):
                s = s + r["pgot"][i * self.ncore + j]
            found += [s[:4, :part], s[4:, :part]]
        rows = jnp.concatenate(found, axis=1)
        r["mod"][...] = jnp.concatenate([rows, jnp.zeros_like(rows)], axis=0)
        self.done("mod")

    def done(self, *names):
        for name in names:
            self.save(name, self.r[name], self.r["out_" + name])

    def save(self, name, value, to):
        c = self.count.local(value, to)
        c.start()
        self.saves[name] = c

    def saved(self, *names):
        for name in names:
            self.saves.pop(name).wait()

    def finish(self):
        while self.now < len(self.units) + 2:
            self.tick()
        for g, units in zip(GROUPS, self.units):
            for u, unit in zip(g, units):
                if self.NAMES[u[0]] not in self.fetched:
                    unit.settled()
                unit.finish()
        for c in self.swaps + self.spread + self.parts:
            c.wait_send()
        for c in self.saves.values():
            c.wait()


def forward_ff_linked(links, r, lens, mod):
    stream, tmp = r["stream"], r["tmp"]
    frames, width = stream.shape
    block = lambda ref, k: ref.at[:, pl.ds(k * width, width)]
    links.ups = [r["wsp"].at[pl.ds(k * width, width)] for k in range(3)] + [r["wso"]]
    links.downs = [r["wcq"], r["wcm"].at[pl.ds(0, width)], r["wcm"].at[pl.ds(width, width)], r["wco"]]
    acts = [block(r["packed"], k) for k in range(3)] + [r["qb"]]
    slopes = [block(r[q], k) for q in ("qa1", "qa2") for k in range(2)]
    links.fetch("wup")
    links.saved("xh1", "m1", "packed", "qa1", "qa2", "att1", "br1")

    def start(at):
        rows = pl.ds(at, TILE)
        own = owners_column(lens, at, TILE)
        norm_into(stream[rows, :], rows, own, lens, mod, 2, r["xh1"], r["m1"], r["rs"], width)

    tiles(frames, start)
    links.save("xh3", r["xh1"], r["out_xh3"])
    links.save("m3", r["m1"], r["out_m3"])
    links.done("rs")
    links.use("wup")
    for n in range(len(acts)):
        act, slope = acts[n], slopes[n]
        tmp[...] = nt(r["m1"][...], links.ups[n][...])

        def gelu(at):
            rows = pl.ds(at, TILE)
            gelu_tile(tmp[rows, :], rows, act, slope)

        tiles(frames, gelu)
        cols = pl.ds(n * width, width)
        links.save(f"act{n}", act, r["out_act"].at[:, cols])
        links.save(f"slope{n}", slope, r["out_slope"].at[:, cols])
        if n % 2 == 1:
            links.tick()
    links.use("wdn")
    tmp[...] = nt(acts[0][...], links.downs[0][...])
    for n in range(1, len(acts)):
        tmp[...] += nt(acts[n][...], links.downs[n][...])

    def last(at):
        rows = pl.ds(at, TILE)
        own = owners_column(lens, at, TILE)
        br = tmp[rows, :]
        r["br1"][rows, :] = br.astype(BF16)
        r["att1"][rows, :] = (stream[rows, :] + expand(own, mod, 8, width) * br).astype(BF16)

    tiles(frames, last)
    links.save("br3", r["br1"], r["out_br3"])
    links.save("out", r["att1"], r["out_out"])


SAVED = ("mod", "pre1", "pre2", "eall", "xh1", "m1", "packed", "qa1", "att1", "br1", "xh2", "m2", "mem", "qa2",
         "att2", "br2", "rs", "xh3", "m3", "act", "slope", "br3", "out")


def gather_forward(mesh, lens, tlens, keep, loud, emb, lat, noi, text, modw, shards):
    ndp, ncore = mesh.shape["dp"], mesh.shape["fsdp"]
    depth, total = ndp // 2, ndp * ncore
    shapes = [(w.shape[1], w.shape[0]) for w in shards]
    nw = len(shapes)
    t, d = lat.shape
    ff = shards[7].shape[1] * ndp
    x, wide = text.shape[0], HEADS * PAIR
    vm = lambda shape, kind=BF16: pltpu.VMEM(shape, kind)
    part = modw.shape[1] // 2
    padded = -(-part // 128) * 128
    kept = {
        "mod": ((8, 9 * d), F32), "pre1": ((total * 8, d), F32), "pre2": ((total * 8, d), F32),
        "eall": ((total, 8, FREQ), F32), "xh1": ((t, d), BF16), "m1": ((t, d), BF16),
        "packed": ((t, 3 * d), BF16), "qa1": ((t, wide), BF16), "att1": ((t, d), BF16), "br1": ((t, d), BF16),
        "xh2": ((t, d), BF16), "m2": ((t, d), BF16), "mem": ((x, 2 * d), BF16), "qa2": ((t, wide), BF16),
        "att2": ((t, d), BF16), "br2": ((t, d), BF16), "rs": ((t, 128), F32), "xh3": ((t, d), BF16), "m3": ((t, d), BF16),
        "act": ((t, ff), BF16), "slope": ((t, ff), BF16), "br3": ((t, d), BF16), "out": ((t, d), BF16),
    }
    full = [(c8 * ndp, share * ncore) for c8, share in shapes]
    scratch = {name: vm(*kept[name]) for name in SAVED[: SAVED.index("xh3")] if name != "stream"}
    scratch["stream"] = vm((t, d), F32)
    for w, name in enumerate(ForwardLinks.NAMES[:7]):
        scratch[name] = vm(full[w])
    scratch.update(aq=vm((t, PAIR)), aks=vm((t, PAIR)), akc=vm((x, PAIR)), qb=vm((t, d)), tmp=vm((t, d), F32))
    scratch.update(psend=vm((total, 8, padded), F32), pgot=vm((total, 8, padded), F32))
    for w, (c8, share) in enumerate(shapes):
        scratch[f"turned{w}"] = vm((c8, share))
        scratch[f"landed{w}"] = vm((c8 // 2, share))
        scratch[f"block{w}"] = vm((c8 // 2, 2 * share))
    ns = 9 + 2 * (total - 1) + 2 * len(SAVED) + 12 * ndp
    ns += sum(1 + (depth - 1) + depth + depth * (1 if u[5] == 0 else 2) + 2 for u in UNITS)
    scratch.update(send=pltpu.SemaphoreType.DMA((ns,)), recv=pltpu.SemaphoreType.DMA((ns,)))
    names = list(scratch)

    def kernel(*refs):
        lens, tlens, keep, loud, emb, lat, noi, text, modw = refs[:9]
        r = dict(emb=emb, modw=modw, shards=refs[9 : 9 + nw])
        at = 9 + nw
        r["full"] = refs[at : at + nw]
        at += nw
        for name in SAVED:
            r["out_" + name] = refs[at]
            at += 1
        r.update(zip(names, refs[at:]))
        for kind in ("turned", "landed", "block"):
            r[kind] = [r[f"{kind}{w}"] for w in range(nw)]
        links = ForwardLinks(mesh, shapes, r)
        forward_attention(links, lens, tlens, keep, loud, r["mod"], lat, noi, text,
                          *[r[n] for n in ("wsp", "wso", "wcq", "wcm", "wco", "stream", "xh1", "m1", "packed", "qa1",
                                           "att1", "br1", "xh2", "m2", "mem", "qa2", "att2", "br2", "rs", "aq", "aks",
                                           "akc", "qb", "tmp")])
        forward_ff_linked(links, r, lens, r["mod"])
        links.finish()

    got = pl.pallas_call(
        kernel,
        out_shape=[sds((depth, 2, c8, share * ncore)) for c8, share in shapes] + [sds(*kept[n]) for n in SAVED],
        in_specs=[SM] * 4 + [VM] * (5 + nw),
        out_specs=[ANY] * (nw + len(SAVED)),
        scratch_shapes=list(scratch.values()),
        cost_estimate=pl.CostEstimate(flops=int(3e10), bytes_accessed=int(6e7), transcendentals=0),
        compiler_params=pltpu.CompilerParams(collective_id=0, has_side_effects=True, vmem_limit_bytes=60 * MIB),
    )(lens, tlens, keep, loud, emb, lat, noi, text, modw, *shards)
    weights = [f.reshape(-1, f.shape[-1]) for f in got[:nw]]
    return weights, dict(zip(SAVED, got[nw:]))


SUM_GROUPS = (
    ((6, 0, 1, 0, 1 / 2, 0), (6, 0, 1, 1 / 2, 1 / 2, 1)),
    ((6, 0, 1, 1, 1 / 2, 0), (6, 0, 1, 3 / 2, 1 / 2, 1)),
    ((5, 0, 1 / 4, 0, 2, 0), (5, 1 / 4, 1 / 4, 0, 2, 1)),
    ((5, 1 / 2, 1 / 4, 0, 2, 0), (5, 3 / 4, 1 / 4, 0, 2, 1)),
    ((4, 0, 1, 0, 2, 0), (2, 0, 1, 0, 2, 1)),
    ((3, 0, 1 / 2, 0, 2, 0), (3, 1 / 2, 1 / 2, 0, 2, 1)),
    ((1, 0, 1, 0, 2, 0),),
    ((0, 0, 1 / 3, 0, 2, 0), (0, 1 / 3, 1 / 3, 0, 2, 1)),
    ((0, 2 / 3, 1 / 3, 0, 2, 1),),
)
EARLY = 4
SLOTS = (((0, 0), (0, 1)), ((1, 0), (1, 1)), ((2, 0),), ((3, 0), (3, 1)), ((2, 1),))
ORDER = (0, 1, 2, 3, 4, 5, 6, None, 7, 8, None, None, None)


def each(count, fn):
    def step(i, carry):
        fn(i)
        return carry

    lax.fori_loop(0, count, step, 0)


def plus(a, b):
    return a + b


class SumUnit:
    def __init__(self, unit, shapes, place, count, grads, own, bufs, final):
        w, r0, n, l0, nl, route, half = unit_shape(unit, shapes)
        self.p, self.route, self.D = place, route, place.depth
        p, D = place, place.depth
        share = shapes[w][1]
        row = pl.ds(pl.multiple_of(p.c * half + r0, 16), n)
        other = pl.ds(pl.multiple_of((1 - p.c) * half + r0, 16), n)
        self.total, self.first, self.second, self.lasts = bufs
        self.final, self.at = final[w], (pl.ds(r0, n), pl.ds(l0, nl))
        self.loads, self.swaps, self.lanes = [], [], []
        self.row, self.grad, self.own = row, grads[w], own
        for i in range(2):
            lane = pl.ds(i * 2 * share + l0, nl)
            self.lanes.append(lane)
            if own is not None:
                self.loads.append(count.local(grads[w].at[:, :, row, lane], own.at[i]))
            self.swaps.append(count.remote(grads[w].at[:, :, other, lane], self.total.at[i], p.at(c=1 - p.c)))
        x, y, z = p.x, p.y, p.z
        total = self.total
        if route == 0:
            self.one = count.remote(total.at[1 - x], self.first, p.at(x=1 - x))
            self.two = count.remote(total.at[x, :, 1 - y], self.second, p.at(y=1 - y))
        else:
            self.one = count.remote(total.at[:, :, 1 - y], self.first, p.at(y=1 - y))
            self.two = count.remote(total.at[1 - x, :, y], self.second, p.at(x=1 - x))
        self.three = []
        for k in range(1, D):
            zz = p.other_z(k)
            self.three.append(count.remote(total.at[x, zz, y], self.lasts.at[k - 1], p.at(z=zz)))

    def load(self):
        for c in self.loads:
            c.start()

    def swap(self):
        for c in self.swaps:
            c.start()

    def add_own(self, x, z, y):
        if self.own is not None:
            v = self.own[x, z, y]
        else:
            if isinstance(x, int):
                v = self.grad[z, y, self.row, self.lanes[x]]
            else:
                width = self.lanes[1].start - self.lanes[0].start
                lane = pl.ds(pl.multiple_of(x * width + self.lanes[0].start, 128), self.lanes[0].size)
                v = self.grad[z, y, self.row, lane]
        self.total[x, z, y] = plus(self.total[x, z, y], v)

    def step_core(self):
        for c in self.loads:
            c.wait()
        for c in self.swaps:
            c.wait_recv()
        x, y, D = self.p.x, self.p.y, self.D
        if self.route == 0:
            each(2 * D, lambda i: self.add_own(1 - x, i // 2, i % 2))
            self.one.start()
            each(2 * D, lambda i: self.add_own(x, i // 2, i % 2))
        else:
            each(2 * D, lambda i: self.add_own(i // D, i % D, 1 - y))
            self.one.start()
            each(2 * D, lambda i: self.add_own(i // D, i % D, y))

    def step_one(self):
        self.one.wait_recv()
        x, y, D = self.p.x, self.p.y, self.D
        total, got = self.total, self.first
        if self.route == 0:
            def add(yy):
                def fn(i):
                    total[x, i, yy] = plus(total[x, i, yy], got[i, yy])
                each(D, fn)
            add(1 - y)
            self.two.start()
            add(y)
        else:
            def add(xx):
                def fn(i):
                    total[xx, i, y] = plus(total[xx, i, y], got[xx, i])
                each(D, fn)
            add(1 - x)
            self.two.start()
            add(x)

    def step_two(self):
        self.two.wait_recv()
        x, y = self.p.x, self.p.y
        total, got = self.total, self.second
        for k in range(1, self.D):
            zz = self.p.other_z(k)
            total[x, zz, y] = plus(total[x, zz, y], got[zz])
            self.three[k - 1].start()

    def step_three(self):
        for c in self.three:
            c.wait_recv()
        x, y, z = self.p.x, self.p.y, self.p.z
        value = self.total[x, z, y].astype(F32) + self.second[z].astype(F32)
        for k in range(self.D - 1):
            value += self.lasts[k].astype(F32)
        self.final[self.at] = value

    def sent(self):
        for c in self.swaps + [self.one, self.two] + self.three:
            c.wait_send()


class LastSwap:
    def __init__(self, w, shapes, place, count, final, part, out):
        self.c8, self.share = shapes[w]
        self.p, self.final, self.part, self.out = place, final[w], part[w], out[w]
        half = self.c8 // 2
        self.rows = pl.ds(pl.multiple_of(place.c * half, 16), half)
        self.copy = count.remote(self.part, self.out.at[self.rows, :], place.at(c=1 - place.c))

    def begin(self):
        total = self.final[...]
        low, high = total[:, : self.share], total[:, self.share :]
        first = self.p.c == 0
        self.part[...] = jnp.where(first, high, low)
        self.copy.start()
        self.out[self.rows, :] = jnp.where(first, low, high)

    def finish(self):
        self.copy.wait()


class BackwardLinks:
    def __init__(self, mesh, shapes, r):
        self.ndp, self.ncore = mesh.shape["dp"], mesh.shape["fsdp"]
        self.shapes, self.r = shapes, r
        self.p = p = Place(self.ndp // 2)
        self.count = count = Counter(r["send"], r["recv"])
        self.every = others(p, self.ndp, self.ncore)
        p.greet([d for _, _, d in self.every])
        self.groups, self.now, self.opened, self.given, self.through = [], 0, set(), set(), set()
        for gi, g in enumerate(SUM_GROUPS):
            early = gi < EARLY
            units = []
            for k, u in enumerate(g):
                own = r[f"own{gi % 2}_{k}"] if early else None
                units.append(SumUnit(u, shapes, p, count, r["grads"], own, r["slot_of"][(gi, k) if early else SLOTS[gi - EARLY][k]], r["final"]))
            self.groups.append(units)
        self.swaps = [LastSwap(w, shapes, p, count, r["final"], r["part"], r["shares"]) for w in range(len(shapes))]
        last = {u[0]: gi for gi, g in enumerate(SUM_GROUPS) for u in g}
        self.closing = {gi: [w for w, l in last.items() if l == gi] for gi in range(len(SUM_GROUPS))}
        self.moves, self.saves, self.writes = {}, [], []

    def met(self):
        self.p.meet(len(self.every))

    def write(self, value, to):
        c = self.count.local(value, to)
        c.start()
        self.writes.append(c)

    def written(self):
        for c in self.writes:
            c.wait()
        self.writes = []

    def early(self, *groups):
        for gi in groups:
            for u in self.groups[gi]:
                u.swap()
            self.given.add(gi)
        self.load_own()

    def load_own(self):
        for gi in sorted(self.given):
            if gi < 2 or gi - 2 in self.through:
                for u in self.groups[gi]:
                    u.load()
                self.given.remove(gi)

    def load(self, name, src=None, to=None):
        to = self.r[name] if to is None else to
        c = self.count.local(self.r["in_" + (src or name)], to)
        c.start()
        self.moves[src or name] = c

    def load_part(self, name, src, to):
        c = self.count.local(src, to)
        c.start()
        self.moves[name] = c

    def ready(self, *names):
        for name in names:
            self.moves.pop(name).wait()

    def tick(self):
        t, self.now = self.now, self.now + 1
        for back, name in ((0, "step_core"), (1, "step_one"), (2, "step_two"), (3, "step_three")):
            g = ORDER[t - back] if 0 <= t - back < len(ORDER) else None
            if g is None:
                continue
            for u in self.groups[g]:
                getattr(u, name)()
            if back == 0:
                self.through.add(g)
                self.load_own()
            if back == 3:
                for w in self.closing[g]:
                    self.swaps[w].begin()
                if g < EARLY:
                    self.release(g)

    def release(self, g):
        p = self.p
        for u in self.groups[g]:
            u.sent()
        ids = [p.at(z=p.other_z(k)) for k in range(1, p.depth)] + [p.at(y=1 - p.y), p.at(x=1 - p.x), p.at(c=1 - p.c)]
        for d in ids:
            pl.semaphore_signal(self.r["free"].at[g], inc=1, device_id=d, device_id_type=MESH)
        self.partners = len(ids)

    def swap(self, g):
        for slot in sorted({s for s, _ in SLOTS[g - EARLY]} - self.opened):
            pl.semaphore_wait(self.r["free"].at[slot], self.partners)
            self.opened.add(slot)
        for u in self.groups[g]:
            u.swap()

    def save(self, value, name):
        c = self.count.local(value, self.r["out_" + name])
        c.start()
        self.saves.append(c)

    def send_sums(self, sums):
        r, p = self.r, self.p
        total = self.ndp * self.ncore
        wide = sums.shape[1] // self.ndp
        part = wide // 2
        pad = r["gs"].shape[2] - part
        value = sums[...].astype(BF16).astype(F32)
        blank = jnp.zeros((8, pad), F32)
        for i in range(self.ndp):
            low = value[:4, i * wide : i * wide + part]
            high = value[:4, i * wide + part : (i + 1) * wide]
            r["gs"][i] = jnp.concatenate([jnp.concatenate([low, high], axis=0), blank], axis=1)
        me = p.flat(self.ncore)
        self.spread = []
        for k, t, d in self.every:
            c = self.count.remote(r["gs"].at[t // self.ncore], r["ggot"].at[me], d)
            c.start()
            self.spread.append(c)
        r["ggot"][me] = r["gs"][me // self.ncore]

    def condition_back(self, pre2):
        r, p = self.r, self.p
        total = self.ndp * self.ncore
        rows = total * 8
        for c in self.spread:
            c.wait_recv()
        modw = r["modw"]
        deep, wide = modw.shape
        part = wide // 2
        got = r["ggot"][...].reshape(rows, r["ggot"].shape[2])[:, :part].astype(BF16)
        mine = split_columns(silu(pre2[...]), p.x * 2 + p.c, self.ncore, deep)
        high = pltpu.roll(mine, 4, 0).astype(BF16)
        r["mg"][...] = jnp.concatenate([tn(mine.astype(BF16), got), tn(high, got)], axis=1)
        back = nt(got, modw[:, :part]) + pltpu.roll(nt(got, modw[:, part:]), rows - 4, 0)
        live = lax.broadcasted_iota(jnp.int32, (rows, 1), 0) % 8 < 4
        back = jnp.where(live, back, 0.0)
        pad = r["ds"].shape[2] - deep
        block = self.ncore * 8
        r["ds"][...] = jnp.concatenate([back, jnp.zeros((rows, pad), F32)], axis=1).reshape(self.ndp, block, deep + pad)
        dp, fsdp = p.z * 2 + p.y, p.x * 2 + p.c
        self.sums = []
        for k in range(1, self.ndp):
            i = lax.rem(dp + k, self.ndp)
            c = self.count.remote(r["ds"].at[i], r["dgot"].at[dp], (i, fsdp))
            c.start()
            self.sums.append(c)
        r["dgot"][dp] = r["ds"][dp]

    def condition_spread(self):
        r, p = self.r, self.p
        for c in self.sums:
            c.wait_recv()
        value = r["dgot"][0]
        for i in range(1, self.ndp):
            value = value + r["dgot"][i]
        block = self.ncore * 8
        at = lax.broadcasted_iota(jnp.int32, (self.ncore * 4, block), 0)
        of = lax.broadcasted_iota(jnp.int32, (self.ncore * 4, block), 1)
        pick_rows = jnp.where(of == (at // 4) * 8 + at % 4, 1.0, 0.0).astype(BF16)
        me = p.flat(self.ncore)
        r["cgot"][me] = nn(pick_rows, value.astype(BF16)).astype(BF16)
        self.last = []
        for k, t, d in self.every:
            c = self.count.remote(r["cgot"].at[me], r["cgot"].at[me], d)
            c.start()
            self.last.append(c)

    def time_back(self, pre1, pre2, tout):
        r, p = self.r, self.p
        total = self.ndp * self.ncore
        rows = total * 8
        deep = r["modw"].shape[0]
        for c in self.last:
            c.wait_recv()
        small = self.ncore * 4
        cols = []
        for j in range(self.ncore):
            cols.append(jnp.concatenate([r["cgot"][i * self.ncore + j][:, :deep] for i in range(self.ndp)], axis=0))
        dense = jnp.concatenate(cols, axis=1)
        count = self.ndp * small
        at = lax.broadcasted_iota(jnp.int32, (rows, count), 0)
        of = lax.broadcasted_iota(jnp.int32, (rows, count), 1)
        spread = jnp.where((at % 8 < 4) & (of == (at // 8) * 4 + at % 8), 1.0, 0.0).astype(BF16)
        one, two = pre1[...], pre2[...]
        back_two = nn(spread, dense) * silu_back(two)
        back_one = fine_nn(back_two, tout[...]) * silu_back(one)
        hidden = silu(one)
        dp, fsdp = p.z * 2 + p.y, p.x * 2 + p.c
        wide = r["tog"].shape[1]
        left = split_columns(hidden, fsdp, self.ncore, r["tog"].shape[0])
        r["tog"][...] = fine_tn(left, split_columns(back_two, dp, self.ndp, wide))
        emb = r["eall"][...].reshape(rows, FREQ)
        left = split_columns(emb, fsdp, self.ncore, r["tig"].shape[0])
        r["tig"][...] = fine_tn(left, split_columns(back_one, dp, self.ndp, wide))

    def finish(self):
        for units in self.groups[EARLY:]:
            for u in units:
                u.sent()
        for s in self.swaps:
            s.finish()
        for c in self.spread + self.sums + self.last:
            c.wait_send()
        for c in self.saves:
            c.wait()


def silu_back(v):
    s = 1.0 / (1.0 + jnp.exp(-v))
    return s * (1.0 + v * (1.0 - s))


def fine_tn(left, right):
    a, b, c = three(left)
    d, e, f = three(right)
    return tn(a, d) + (tn(a, e) + tn(b, d)) + (tn(b, e) + tn(a, f) + tn(c, d))


def backward_ff_linked(links, r, lens, mod, rs, sums):
    frames, width = r["stage"].shape
    quarters = r["in_wup"].shape[0] // width
    packed, dpack, qa, wsp, dq, tmp, stage = [r[n] for n in ("packed", "dpack", "qa", "wsp", "dq", "tmp", "stage")]
    block = lambda ref, k: ref.at[:, pl.ds(k * width, width)]
    acts, slopes = (block(packed, 0), block(packed, 1)), (block(packed, 2), block(qa, 0))
    downs, ups = (wsp.at[pl.ds(0, width)], wsp.at[pl.ds(width, width)]), (wsp.at[pl.ds(2 * width, width)], block(qa, 1))
    ig, outs = block(dpack, 0), (block(dpack, 1), block(dpack, 2))
    order = [n for n in range(0, quarters, 2)] + [n for n in range(1, quarters, 2)]
    half = r["ffu"].shape[2]

    def fetch(i):
        n, k = order[i], i % 2
        cols = pl.ds(n * width, width)
        links.load_part(f"act{n}", r["in_act"].at[:, cols], acts[k])
        links.load_part(f"down{n}", r["in_wdn"].at[:, cols], downs[k])
        links.load_part(f"slope{n}", r["in_slope"].at[:, cols], slopes[k])
        links.load_part(f"up{n}", r["in_wup"].at[cols, :], ups[k])

    links.load("datt", "cot")
    links.load("att", "br3")
    fetch(0)
    links.load("m", "m3")
    links.load("xh", "xh3")
    links.load("wo", "wco")
    sums[...] = jnp.zeros_like(sums)
    links.ready("cot", "br3")

    def start(at):
        rows = pl.ds(at, TILE)
        own = owners_column(lens, at, TILE)
        gate_tile(lens, at, own, mod, r["datt"][rows, :].astype(F32), r["att"], 2, sums, dq, width)

    tiles(frames, start)
    links.load("att", "br2")
    for i, n in enumerate(order):
        k = i % 2
        if i + 1 < quarters:
            fetch(i + 1)
        links.ready(f"act{n}", f"down{n}", f"slope{n}", f"up{n}")
        cols = pl.ds(n * width, width)
        grad = r["grad1"] if k == 0 else r["grad2"]
        value = tn(dq[...], acts[k][...]).astype(BF16)
        if i >= 2:
            links.written()
        c8 = grad.shape[2]
        for b in range(width // c8):
            grad[b // 2, b % 2] = value[b * c8 : (b + 1) * c8, :]
        links.write(grad, r["ffd"].at[:, :, :, cols])
        ig[...] = (nn(dq[...], downs[k][...]) * slopes[k][...].astype(F32)).astype(BF16)
        if i == 0:
            links.ready("m3")
        outs[k][...] = tn(ig[...], r["m"][...]).astype(BF16)
        for y in range(2):
            links.write(outs[k].at[pl.ds(y * half, half)], r["ffu"].at[n, y])
        part = nn(ig[...], ups[k][...])
        if i == 0:
            tmp[...] = part
        else:
            tmp[...] += part
        if i == 1:
            links.written()
            links.met()
            links.early(0)
        if i == quarters - 2:
            links.tick()
        if i == quarters - 1:
            links.written()
            links.early(1, 2, 3)
    links.ready("xh3", "br2")

    def last(at):
        rows = pl.ds(at, TILE)
        own = owners_column(lens, at, TILE)
        s = r["datt"][rows, :].astype(F32) + norm_back_tile(lens, at, own, mod, tmp[rows, :], r["xh"], rs, 2, sums, width)
        stage[rows, :] = s
        gate_tile(lens, at, own, mod, s, r["att"], 1, sums, dq, width)

    tiles(frames, last)
    links.tick()


def backward_linked(links, r, lens, tlens, keep, mod, text, rs, sums):
    frames, width = r["stage"].shape
    slots = text.shape[0]
    qa, att, m, xh, wo, dq, datt, stage, tmp = [r[n] for n in ("qa", "att", "m", "xh", "wo", "dq", "datt", "stage", "tmp")]
    packed, dpack, acc = r["packed"], r["dpack"], r["acc"]
    mem = packed.at[pl.ds(0, slots), pl.ds(0, 2 * width)]
    dmem = dpack.at[pl.ds(0, slots), pl.ds(0, 2 * width)]
    grads = r["flat"]
    links.load("att", "att2")
    links.load("qa", "qa2")
    links.load("mem", to=mem)
    links.load("m", "m2")
    links.load("xh", "xh2")
    links.load("wsp")
    fill_masks(lens, tlens, r["aq"], r["aks"], r["akc"])
    links.ready("wco")
    datt[...] = nn(dq[...], wo[...]).astype(BF16)
    links.load("wo", "wcq")
    links.ready("att2")
    grads(4, dq, att, width)
    links.ready("qa2", "mem")
    links.tick()
    steps = iter((links.tick, lambda: None))
    attention_backward(qa, mem, 0, width, r["akc"], att, datt, dq, dmem, 0, width, acc, lambda: next(steps)())
    links.load("qa", "qa1")
    links.load("att", "att1")
    links.load("packed")
    links.load("datt", "br1")
    links.ready("m2")
    grads(2, dq, m, width)
    links.swap(4)
    links.load("m", "m1")
    grads(3, dmem, text, width)
    links.ready("wcq")
    tmp[...] = nn(dq[...], wo[...])
    links.load("wo", "wso")
    links.tick()
    links.swap(5)
    links.ready("xh2", "br1")

    def middle(at):
        rows = pl.ds(at, TILE)
        own = owners_column(lens, at, TILE)
        s = stage[rows, :] + norm_back_tile(lens, at, own, mod, tmp[rows, :], xh, rs, 1, sums, width)
        stage[rows, :] = s
        gate_tile(lens, at, own, mod, s, datt, 0, sums, dq, width)

    tiles(frames, middle)
    links.load("xh", "xh1")
    links.ready("att1", "wso")
    grads(1, dq, att, width)
    datt[...] = nn(dq[...], wo[...]).astype(BF16)
    links.load("wo", "tout")
    links.tick()
    links.swap(6)
    links.ready("qa1", "packed")
    steps = iter((links.tick, links.tick, lambda: None))
    attention_backward(qa, packed, width, 2 * width, r["aks"], att, datt, dpack, dpack, width, 2 * width, acc,
                       lambda: next(steps)(), 2)
    links.ready("m1", "wsp")
    grads(0, dpack, m, width)
    links.swap(7)
    links.swap(8)
    tmp[...] = nn(dpack[...], r["wsp"][...])
    links.tick()
    links.ready("xh1")

    def last(at):
        rows = pl.ds(at, TILE)
        own = owners_column(lens, at, TILE)
        s = stage[rows, :] + norm_back_tile(lens, at, own, mod, tmp[rows, :], xh, rs, 0, sums, width)
        stage[rows, :] = pick(own, keep[0], keep[1], keep[2]) * s

    tiles(frames, last)
    links.send_sums(sums)
    links.save(stage, "latents")
    pre1, pre2 = tmp.at[pl.ds(0, r["in_pre1"].shape[0])], tmp.at[pl.ds(r["in_pre1"].shape[0], r["in_pre1"].shape[0])]
    links.load("pre2", to=pre2)
    links.load("pre1", to=pre1)
    links.tick()
    links.ready("pre2")
    links.condition_back(pre2)
    links.tick()
    links.condition_spread()
    links.tick()
    links.ready("pre1", "tout")
    links.time_back(pre1, pre2, wo)
    while links.now < len(ORDER):
        links.tick()


def reduce_backward(mesh, lens, tlens, keep, small, big):
    ndp, ncore = mesh.shape["dp"], mesh.shape["fsdp"]
    depth, total = ndp // 2, ndp * ncore
    d = big["wso"].shape[0]
    t = big["cot"].shape[0]
    ff = big["wup"].shape[0]
    x = small["text"].shape[0]
    cols = (3 * d, d, d, 2 * d, d, ff, d)
    rows_of = (d, d, d, d, d, d, ff)
    shapes = [(c // ndp, rw // ncore) for c, rw in zip(cols, rows_of)]
    vm = lambda shape, kind=BF16: pltpu.VMEM(shape, kind)
    wide = HEADS * PAIR
    deep, mcols = small["modw"].shape
    padded = -(-(mcols // 2) // 128) * 128
    dpad = -(-deep // 128) * 128
    tin_rows, t_cols = FREQ // ncore, d // ndp
    scratch = dict(
        qa=vm((t, wide)), att=vm((t, d)), m=vm((t, d)), xh=vm((t, d)), wo=vm((d, d)), dq=vm((t, d)), datt=vm((t, d)),
        stage=vm((t, d), F32), tmp=vm((t, d), F32), packed=vm((t, 3 * d)), dpack=vm((t, 3 * d)), wsp=vm((3 * d, d)),
        acc=vm((PAIR, t), F32), aq=vm((t, PAIR)), aks=vm((t, PAIR)), akc=vm((x, PAIR)), sums=vm((16, 9 * d), F32),
        gs=vm((ndp, 8, padded), F32), ggot=vm((total, 8, padded), F32), ds=vm((ndp, ncore * 8, dpad), F32),
        dgot=vm((ndp, ncore * 8, dpad), F32), cgot=vm((total, ncore * 4, dpad)),
    )
    for w in range(5):
        c8, share = shapes[w]
        scratch[f"grad{w}"] = vm((depth, 2, c8, share * ncore))
    for w, (c8, share) in enumerate(shapes):
        scratch[f"final{w}"] = vm((c8 // 2, 2 * share), F32)
        scratch[f"part{w}"] = vm((c8 // 2, share), F32)
    dims = lambda u: unit_shape(u, shapes)
    slot_names = {}
    for gi in range(EARLY):
        for k, u in enumerate(SUM_GROUPS[gi]):
            _, _, n, _, nl, route, _ = dims(u)
            tag = slot_names[(gi, k)] = f"slot{gi}_{k}"
            scratch[tag + "a"] = vm((2, depth, 2, n, nl))
            scratch[tag + "b"] = vm((depth, 2, n, nl) if route == 0 else (2, depth, n, nl))
            scratch[tag + "c"] = vm((depth, n, nl))
            scratch[tag + "d"] = vm((depth - 1, n, nl))
    for gi in range(EARLY):
        for k, u in enumerate(SUM_GROUPS[gi]):
            _, _, n, _, nl, _, _ = dims(u)
            scratch[f"own{gi % 2}_{k}"] = vm((2, depth, 2, n, nl))
    ns = sum(len(g) * (4 + 2 + depth - 1) for g in SUM_GROUPS) + len(shapes) + 2 * (total - 1) + ndp + 80
    scratch.update(send=pltpu.SemaphoreType.DMA((ns,)), recv=pltpu.SemaphoreType.DMA((ns,)), free=pltpu.SemaphoreType.REGULAR((EARLY,)))
    names = list(scratch)
    small_names, big_names = list(small), list(big)
    outs = dict(latents=((t, d), F32), mg=((deep, mcols), F32), tig=((tin_rows, t_cols), F32), tog=((d // ncore, t_cols), F32))

    def kernel(*refs):
        lens, tlens, keep = refs[:3]
        at = 3
        r = {}
        for n in small_names:
            r[n] = refs[at]
            at += 1
        for n in big_names:
            r["in_" + n] = refs[at]
            at += 1
        r["out_latents"] = refs[at]
        r["mg"], r["tig"], r["tog"] = refs[at + 1 : at + 4]
        at += 4
        r["shares"] = refs[at : at + len(shapes)]
        at += len(shapes)
        r["ffu"], r["ffd"] = refs[at : at + 2]
        at += 2
        r.update(zip(names, refs[at:]))
        r["grads"] = [r[f"grad{w}"] for w in range(5)] + [r["ffu"], r["ffd"]]
        r["final"] = [r[f"final{w}"] for w in range(len(shapes))]
        r["part"] = [r[f"part{w}"] for w in range(len(shapes))]
        def flat(w, left, right, width):
            out = r[f"grad{w}"]
            c8 = shapes[w][0]
            per = ndp
            while per % 2 == 0 and per // 2 * c8 >= width and per // 2 * c8 % 128 == 0:
                per //= 2

            def step(i, carry):
                cols = pl.ds(pl.multiple_of(i * per * c8, per * c8), per * c8)
                value = tn(left[:, cols], right[...]).astype(BF16)
                for k in range(per):
                    b = i * per + k
                    out[b // 2, b % 2] = value[k * c8 : (k + 1) * c8, :]
                return carry

            lax.fori_loop(0, ndp // per, step, 0)

        r["flat"] = flat
        tagged = {}
        for (gi, k), tag in slot_names.items():
            tagged[(gi, k)] = [r[tag + e] for e in "abcd"]
        r["slot_of"] = tagged
        links = BackwardLinks(mesh, shapes, r)
        backward_ff_linked(links, r, lens, r["mod"], r["rs"], r["sums"])
        backward_linked(links, r, lens, tlens, keep, r["mod"], r["text"], r["rs"], r["sums"])
        links.finish()

    got = pl.pallas_call(
        kernel,
        out_shape=[sds(*outs[n]) for n in outs] + [sds(s, F32) for s in shapes]
        + [sds((depth, 2) + (shapes[w][0], shapes[w][1] * ncore)) for w in (5, 6)],
        in_specs=[SM] * 3 + [VM] * len(small) + [ANY] * len(big),
        out_specs=[ANY] + [VM] * (3 + len(shapes)) + [ANY] * 2,
        scratch_shapes=list(scratch.values()),
        cost_estimate=pl.CostEstimate(flops=int(6e10), bytes_accessed=int(8e7), transcendentals=0),
        compiler_params=pltpu.CompilerParams(collective_id=1, has_side_effects=True, vmem_limit_bytes=63 * MIB),
    )(lens, tlens, keep, *small.values(), *big.values())
    turned = pl.pallas_call(
        partial(turn_body, len(shapes)),
        out_shape=[sds(s[::-1], F32) for s in shapes],
        in_specs=[VM] * len(shapes),
        out_specs=[VM] * len(shapes),
    )(*got[4 : 4 + len(shapes)])
    return got[:4], turned


def turn_body(nw, *refs):
    for w in range(nw):
        refs[nw + w][...] = refs[w][...].T


HIGHEST = lax.Precision.HIGHEST
BOTH = ("dp", "fsdp")


def high_dot(left, right, lc=1, rc=0):
    return lax.dot_general(left, right, (((lc,), (rc,)), ((), ())), precision=HIGHEST, preferred_element_type=F32)


def plan(step_row):
    levels = step_row.astype(F32)
    cumulative = jnp.cos(0.5 * math.pi * (levels / 1000.0 + 0.008) / 1.008) ** 2
    half_width = FREQ // 2
    frequency = jnp.exp(-math.log(10000.0) * jnp.arange(half_width, dtype=F32) / half_width)
    angles = levels[:, None] * frequency[None, :]
    embedding = jnp.concatenate([jnp.cos(angles), jnp.sin(angles)], axis=1)
    return jnp.sqrt(cumulative), jnp.sqrt(1.0 - cumulative), embedding


def silu_slope(v):
    s = jax.nn.sigmoid(v)
    return s * (1.0 + v * (1.0 - s))


def plain_gather(w):
    part = lax.all_gather(w, "fsdp", axis=0, tiled=True)
    return lax.all_gather(part, "dp", axis=1, tiled=True).T


def plain_reduce(g):
    part = lax.psum_scatter(g.T, "dp", scatter_dimension=1, tiled=True).astype(BF16)
    return lax.psum_scatter(part, "fsdp", scatter_dimension=0, tiled=True).astype(F32)


def fits(mesh, frames, weights):
    if mesh.shape["fsdp"] != 4 or mesh.shape["dp"] % 2:
        return False
    if mesh.shape["dp"] * mesh.shape["fsdp"] * 16 > frames or frames != weights[1].shape[0] * mesh.shape["fsdp"]:
        return False
    return all(w.shape[0] * 2 % 128 == 0 and w.shape[1] % 32 == 0 for w in weights)


def columns(values, index, width):
    return lax.dynamic_slice_in_dim(values, index * width, width, axis=1)


def body(mesh, latents, noise_draw, text_states, time_steps, item_lengths, text_lengths, cotangent, time_in, time_out,
         modulation, *others):
    ndp, nfs = mesh.shape["dp"], mesh.shape["fsdp"]
    i, j = lax.axis_index("dp"), lax.axis_index("fsdp")
    width = latents.shape[1]
    items = time_steps.shape[0]
    sent = (time_in, time_out) + others
    direct = fits(mesh, latents.shape[0], sent)
    text = text_states.reshape(-1, width)
    keep, loud, embedding = plan(time_steps)
    deep, wide = modulation.shape
    if direct:
        embedding = jnp.pad(embedding, ((0, 8 - items), (0, 0)))
        full, saved = gather_forward(mesh, item_lengths, text_lengths, keep, loud, embedding, latents, noise_draw, text,
                                     modulation, sent)
        mod = saved["mod"]
        weights = full[2:]
        small = dict(mod=mod, text=text, rs=saved["rs"], modw=modulation, eall=saved["eall"])
        names = ("att2", "qa2", "mem", "m2", "xh2", "qa1", "att1", "packed", "br1", "m1", "xh1", "br2", "pre1", "pre2",
                 "xh3", "m3", "act", "slope", "br3")
        big = {n: saved[n] for n in names}
        big.update(cot=cotangent, wsp=weights[0], wso=weights[1], wcq=weights[2], wco=weights[4], wup=weights[5],
                   wdn=weights[6], tout=full[1])
        (lat_grad, modulation_grad, time_in_grad, time_out_grad), shares = reduce_backward(
            mesh, item_lengths, text_lengths, keep, small, big)
        return (saved["out"], lat_grad, time_in_grad, time_out_grad, modulation_grad, *shares)
    full = [plain_gather(w) for w in sent]
    t_in, t_out = full[0].astype(F32), full[1].astype(F32)
    embedding = lax.all_gather(embedding, BOTH, axis=0, tiled=True)
    pre_one = high_dot(embedding, t_in, 1, 1)
    hidden = jax.nn.silu(pre_one)
    pre_two = high_dot(hidden, t_out, 1, 1)
    mine = columns(jax.nn.silu(pre_two).astype(BF16), j, deep)
    part = jnp.dot(mine, modulation, preferred_element_type=F32).reshape(ndp, nfs * items, wide)
    part = lax.psum_scatter(part, "fsdp", scatter_dimension=1, tiled=True)
    rows = lax.all_to_all(part, "dp", 0, 0, tiled=True)
    mod = jnp.pad(rows.transpose(1, 0, 2).reshape(items, -1), ((0, 8 - items), (0, 0)))
    first = run_attention(item_lengths, text_lengths, keep, loud, mod, latents, noise_draw, text, *full[2:7])
    weights = full[2:]
    second = run_ff(item_lengths, mod, first[0], *weights[5:])
    out, lat_grad, *grads, sums = run_backward(item_lengths, text_lengths, keep, mod, text, cotangent, first, second, *weights)
    shares = [plain_reduce(g) for g in grads]

    sent_sums = sums[:items].astype(BF16).reshape(items, ndp, wide).transpose(1, 0, 2)
    got = lax.all_to_all(sent_sums, "dp", 0, 0, tiled=True)
    got = lax.all_gather(got, "fsdp", axis=1, tiled=True).reshape(-1, wide)
    modulation_grad = lax.dot_general(mine, got, (((0,), (0,)), ((), ())), preferred_element_type=F32)
    back = lax.dot_general(got, modulation, (((1,), (1,)), ((), ())), preferred_element_type=F32)
    back = lax.all_gather(lax.psum(back, "dp"), "fsdp", axis=1, tiled=True)
    back_two = back * silu_slope(pre_two)
    back_one = high_dot(back_two, t_out) * silu_slope(pre_one)
    time_in_grad = high_dot(columns(embedding, j, time_in.shape[0]), columns(back_one, i, time_in.shape[1]), 0, 0)
    time_out_grad = high_dot(columns(hidden, j, time_out.shape[0]), columns(back_two, i, time_out.shape[1]), 0, 0)
    return (out, lat_grad, time_in_grad, time_out_grad, modulation_grad, *shares)


def solution(mesh):
    rows, weight = P(BOTH, None), P("fsdp", "dp")
    return jax.shard_map(
        partial(body, mesh),
        mesh=mesh,
        in_specs=(rows, rows, P(BOTH, None, None), P(BOTH), rows, P(BOTH), rows) + (weight,) * 10,
        out_specs=(rows, rows) + (weight,) * 10,
        check_vma=False,
    )
```
